32 devices in a mesh: dp: 8 (over z, x), mp: 4 (over y, core).
Axes of the slice: x: 2, y: 2, z: 4, core: 2. Of those that a mesh axis runs over, the one named last changes fastest.
Arguments:
- input_ids: int32 [16, 512], P('dp'), may hold values from 0 to 6303
- seq_lengths: int32 [16, 4], P('dp'), may hold values from 0 to 512, as said below
- loss_positions: int32 [16, 80], P('dp'), may hold values from 0 to 511, as said below
- targets: int32 [16, 80], P('dp'), may hold values from 0 to 6303
- block_owner: int32 [192], replicated, may hold values from 0 to 191, as said below
- layer_master: float32 [4, 192, 128, 128], P('mp', 'dp')
- stats_left: float32 [4, 192, 128, 128], P('mp', 'dp'), as said below
- stats_right: float32 [4, 192, 128, 128], P('mp', 'dp'), as said below
- root_left: float32 [4, 192, 128, 128], P('mp', 'dp'), as said below
- root_right: float32 [4, 192, 128, 128], P('mp', 'dp'), as said below
- table_master: float32 [6304, 1024], P(('dp', 'mp')), may hold values from -0.36 to 0.36
- table_first: float32 [6304, 1024], P(('dp', 'mp')), may hold values from -1.2 to 1.2
- table_second: float32 [6304, 1024], P(('dp', 'mp')), may hold values from 0.01 to 0.1
- vector_master: float32 [526, 1024], replicated
- vector_first: float32 [526, 1024], replicated, may hold values from -1.2 to 1.2
- vector_second: float32 [526, 1024], replicated, may hold values from 0.01 to 0.1
Outputs:
- loss: float32 [], replicated
- grad_norm: float32 [], replicated
- layer_new: float32 [4, 192, 128, 128], P('mp', 'dp')
- left_new: float32 [4, 192, 128, 128], P('mp', 'dp')
- right_new: float32 [4, 192, 128, 128], P('mp', 'dp')
- table_new: float32 [6304, 1024], P(('dp', 'mp'))
- table_first_new: float32 [6304, 1024], P(('dp', 'mp'))
- table_second_new: float32 [6304, 1024], P(('dp', 'mp'))
- vector_new: float32 [526, 1024], replicated
- vector_first_new: float32 [526, 1024], replicated
- vector_second_new: float32 [526, 1024], replicated
The draws below stay inside these ranges and needn't reach their ends.
Inputs may be any that keep to these rules, and one draw needn't show every extreme that they name: `seq_lengths`: each row packs its sequences from slot 0 on, each 128 to 512 long, unused slots 0 after the used ones, and the lengths sum to at most 512; the rest of the row is padding. `loss_positions`: distinct positions of one row, each below the sum of that row's lengths. `block_owner`: a permutation; device index i of dp owns the blocks at slots i * 24 to (i + 1) * 24 - 1. `stats_left`: symmetric. `stats_right`: symmetric. `root_left`: symmetric. `root_right`: symmetric.
All inputs are finite; a program needn't handle non-finite values.
Results may differ from the reference program's by a relative error of at most 0.00205.
The reference program's roundings to bfloat16 on the way count: a program that leaves them out, or rounds other values in their place, can miss the bound.
Values may be sent and summed in bfloat16 or wider, within the bound.
No kernel may reach another device: no remote copies, remote signals or barrier semaphores. Data moves between devices by JAX's collectives and lax.ppermute only.
A program may use at most 256 MiB of HBM per device.

```python
import math
import jax
import jax.numpy as jnp
import numpy as np
from jax import lax

D = 1024
HEADS = 16
HD = 64
FF = 4096
V = 6304
LEN = 512
LMIN = 128
SLOTS = 4
POS = 80
KB = 128
DM = 256
FM = 1024
NBLK = 192
TOTAL_ROWS = 16
COUNT = 1280
VROWS = 526
N_MP = 4


def owner_order(base_key):
    return jax.random.permutation(jax.random.fold_in(base_key, 7), NBLK).astype(jnp.int32)


def draw_block_owner(key, part):
    return owner_order(key)


def draw_layer_master(key, part):
    count_joined = D // KB * (3 * DM // KB)
    count_output = DM // KB * (D // KB)
    count_upward = D // KB * (FM // KB)
    block_index = jnp.arange(NBLK)
    spread = jnp.where(block_index < count_joined, D ** (-0.5), jnp.where(block_index < count_joined + count_output, 8.0 * D ** (-0.5), jnp.where(block_index < count_joined + count_output + count_upward, D ** (-0.5), FF ** (-0.5))))
    natural = jax.random.normal(jax.random.fold_in(key, 3), (N_MP, NBLK, KB, KB), jnp.float32) * spread[None, :, None, None]
    return jnp.take(natural, owner_order(key), axis=1)


def symmetric_tiles(base_key, diag_low, diag_high, off_scale):
    tile_shape = (N_MP, NBLK, KB, KB)
    off_part = jax.random.normal(jax.random.fold_in(base_key, 1), tile_shape, jnp.float32) * off_scale
    off_part = (off_part + jnp.swapaxes(off_part, 2, 3)) * 0.7071
    diagonal = jax.random.uniform(jax.random.fold_in(base_key, 2), (N_MP, NBLK, KB), jnp.float32, diag_low, diag_high)
    return off_part + diagonal[..., None] * jnp.eye(KB, dtype=jnp.float32)


def draw_stats_left(key, part):
    return symmetric_tiles(jax.random.fold_in(key, 21), 2.0, 10.0, 5.0 / KB ** 0.5)


def draw_stats_right(key, part):
    return symmetric_tiles(jax.random.fold_in(key, 22), 2.0, 10.0, 5.0 / KB ** 0.5)


def draw_root_left(key, part):
    return symmetric_tiles(jax.random.fold_in(key, 23), 0.5, 1.5, 0.45 / KB ** 0.5)


def draw_root_right(key, part):
    return symmetric_tiles(jax.random.fold_in(key, 24), 0.5, 1.5, 0.45 / KB ** 0.5)


def draw_vector_master(key, part):
    ff_rows = FF // D
    row_count = LEN + 10 + ff_rows
    random_part = jax.random.normal(jax.random.fold_in(key, 5), (row_count, D), jnp.float32) * 0.2
    row_index = jnp.arange(row_count)
    gain_rows = (row_index == LEN) | (row_index == LEN + 5) | (row_index == LEN + 8 + ff_rows)
    return random_part + gain_rows.astype(jnp.float32)[:, None]


def length_table(base_key):
    drawn = jax.random.randint(jax.random.fold_in(base_key, 11), (TOTAL_ROWS, SLOTS), LMIN, LEN + 1, jnp.int32)
    drawn = drawn.at[0, 0].set(LEN)
    seq_ends = jnp.cumsum(drawn, axis=1)
    return jnp.where(seq_ends <= LEN, drawn, 0).astype(jnp.int32)


def draw_seq_lengths(key, part):
    return length_table(key)


def draw_loss_positions(key, part):
    lengths = length_table(key)
    valid_count = jnp.sum(lengths, axis=1)
    places = jnp.arange(LEN, dtype=jnp.int32)
    row_keys = jax.random.split(jax.random.fold_in(key, 13), TOTAL_ROWS)
    shuffled = jax.vmap(lambda row_key: jax.random.permutation(row_key, LEN))(row_keys).astype(jnp.int32)
    priority = jnp.where(places[None, :] < valid_count[:, None], shuffled, LEN + places[None, :])
    priority = priority.at[0, 0].set(-2).at[0, LEN - 1].set(-1)
    return jnp.argsort(priority, axis=1)[:, :POS].astype(jnp.int32)


def place_ends(values, own_key, smallest, high):
    longest = values.shape.index(max(values.shape))
    spots = []
    for shift in (0, 1):
        where = [jax.random.randint(jax.random.fold_in(own_key, axis), (), 0, length) for axis, length in enumerate(values.shape)]
        where[longest] = (where[longest] + shift) % values.shape[longest]
        spots.append(tuple(where))
    return values.at[spots[0]].set(smallest).at[spots[1]].set(high)


def block_levels(key, dims, cuts, low, largest):
    level, own = 1.0, jax.random.fold_in(key, 6)
    for position, parts in cuts:
        heights = jnp.exp(jax.random.uniform(jax.random.fold_in(own, position), (parts,), jnp.float32, low / len(cuts), largest / len(cuts)))
        level = level * jnp.repeat(heights, dims[position] // parts).reshape([-1 if axis == position else 1 for axis in range(len(dims))])
    return level


def cumulative_ranks(count, slope):
    weights = [(1 << 20) // math.isqrt(grade ** slope) + 1 for grade in range(1, count + 1)]
    width = 1 + sum(weights) // (1 << 30)
    return np.cumsum(np.array([max(1, weight // width) for weight in weights]))


def ranked_ids(rng, extent, count, skew):
    grid = cumulative_ranks(count, skew)
    ticket = jax.random.randint(jax.random.fold_in(rng, 1), extent, 0, int(grid[count - 1]))
    rank = jnp.searchsorted(jnp.asarray(grid, jnp.int32), ticket, side="right")
    return jax.random.permutation(jax.random.fold_in(rng, 2), count)[rank].astype(jnp.int32)


def normal_values(own_key, shape, deviation, most, cuts=(), kind=jnp.bfloat16):
    level = block_levels(own_key, shape, cuts, -0.22, 0.18) if cuts else 1.0
    array = jax.random.normal(own_key, shape, jnp.float32) * deviation * level
    return jnp.minimum(jnp.maximum(array, -most), most).astype(kind)


def setup_inputs(seed: int = 0) -> dict:
    seeds = jax.random.split(jax.random.key(seed), 17)
    input_ids = place_ends(ranked_ids(seeds[0], (TOTAL_ROWS, LEN), V, 2), jax.random.fold_in(seeds[0], 3), 0, V - 1).astype(jnp.int32)
    seq_lengths = draw_seq_lengths(jax.random.fold_in(seeds[16], 71), 0)
    loss_positions = draw_loss_positions(jax.random.fold_in(seeds[16], 71), 0)
    targets = place_ends(ranked_ids(seeds[3], (TOTAL_ROWS, POS), V, 2), jax.random.fold_in(seeds[3], 3), 0, V - 1).astype(jnp.int32)
    block_owner = draw_block_owner(jax.random.fold_in(seeds[16], 71), 0)
    layer_master = draw_layer_master(jax.random.fold_in(seeds[16], 71), 0)
    stats_left = draw_stats_left(jax.random.fold_in(seeds[16], 71), 0)
    stats_right = draw_stats_right(jax.random.fold_in(seeds[16], 71), 0)
    root_left = draw_root_left(jax.random.fold_in(seeds[16], 71), 0)
    root_right = draw_root_right(jax.random.fold_in(seeds[16], 71), 0)
    table_master = normal_values(seeds[10], (V, D), 0.06, 0.36, ((0, 32),), jnp.float32)
    table_first = normal_values(seeds[11], (V, D), 0.2, 1.2, ((0, 32),), jnp.float32)
    table_second = jnp.clip(jnp.exp(math.log(0.1) - 2.3025851 * jax.random.uniform(seeds[12], (V, D), jnp.float32) ** block_levels(seeds[12], (V, D), ((0, 32),), -0.2, 0.2)), 0.01, 0.1)
    vector_master = draw_vector_master(jax.random.fold_in(seeds[16], 71), 0)
    vector_first = normal_values(seeds[14], (VROWS, D), 0.2, 1.2, (), jnp.float32)
    vector_second = jnp.clip(jnp.exp(jax.random.uniform(seeds[15], (VROWS, D), jnp.float32, math.log(0.01), math.log(0.1))), 0.01, 0.1)
    return dict(input_ids=input_ids, seq_lengths=seq_lengths, loss_positions=loss_positions, targets=targets, block_owner=block_owner, layer_master=layer_master, stats_left=stats_left, stats_right=stats_right, root_left=root_left, root_right=root_right, table_master=table_master, table_first=table_first, table_second=table_second, vector_master=vector_master, vector_first=vector_first, vector_second=vector_second)


HIGH = lax.Precision.HIGHEST
EPS_NORM = 1e-05
EPS_ADAM = 1e-08
BETA_FIRST = 0.5
BETA_SECOND = 0.5
RATE_ADAM = 0.01
RATE_SHAMPOO = 0.03
DECAY_TABLE = 0.01
DECAY_LAYER = 0.01
STAT_DECAY = 0.5
CLIP_FACTOR = 16.0
MASK_FILL = -1000000000.0

@jax.custom_vjp
def low(v):
    return lax.optimization_barrier(v.astype(jnp.bfloat16)).astype(jnp.float32)

@jax.custom_vjp
def low_back(v):
    return v

def low_keep(v):
    return (low(v), None)

def low_pass(kept, grad):
    return (grad,)

def back_keep(v):
    return (v, None)

def back_low(kept, grad):
    return (low(grad),)
low.defvjp(low_keep, low_pass)
low_back.defvjp(back_keep, back_low)

def layer_norm(values, norm_gain, norm_shift):
    row_mean = lax.optimization_barrier(jnp.mean(values, axis=-1, keepdims=True))
    centered = values - row_mean
    variance = lax.optimization_barrier(jnp.mean(centered * centered, axis=-1, keepdims=True))
    return centered * lax.rsqrt(variance + EPS_NORM) * norm_gain + norm_shift

def gelu_exact(values):
    return 0.5 * values * (1.0 + jax.scipy.special.erf(values * 0.7071067811865476))

def positions_of(lengths, length):
    seq_ends = jnp.cumsum(lengths).astype(jnp.int32)
    places = jnp.arange(length, dtype=jnp.int32)
    passed = places[:, None] >= seq_ends[None, :]
    segment = lax.optimization_barrier(jnp.sum(passed.astype(jnp.int32), axis=1)).astype(jnp.int32)
    seq_start = lax.optimization_barrier(jnp.max(jnp.where(passed, seq_ends[None, :], 0), axis=1)).astype(jnp.int32)
    return (segment, places - seq_start)

def from_tiles(stacked, height, breadth, tile_size):
    arranged = stacked.reshape(height // tile_size, breadth // tile_size, tile_size, tile_size)
    return arranged.transpose(0, 2, 1, 3).reshape(height, breadth)

def split_pieces(stacked, model_width, inner_width, hidden, tile_size):
    first_end = model_width // tile_size * (3 * inner_width // tile_size)
    second_end = first_end + inner_width // tile_size * (model_width // tile_size)
    third_end = second_end + model_width // tile_size * (hidden // tile_size)
    joined = from_tiles(stacked[:first_end], model_width, 3 * inner_width, tile_size)
    output = from_tiles(stacked[first_end:second_end], inner_width, model_width, tile_size)
    upward = from_tiles(stacked[second_end:third_end], model_width, hidden, tile_size)
    downward = from_tiles(stacked[third_end:], hidden, model_width, tile_size)
    return (joined, output, upward, downward)

def adam_step(master, moment_one, moment_two, gradient, weight_decay):
    new_one = BETA_FIRST * moment_one + (1.0 - BETA_FIRST) * gradient
    new_two = BETA_SECOND * moment_two + (1.0 - BETA_SECOND) * gradient * gradient
    new_master = master - RATE_ADAM * (new_one / (jnp.sqrt(new_two) + EPS_ADAM) + weight_decay * master)
    return (new_master, new_one, new_two)

def shampoo_step(master, stat_left, stat_right, left_root, right_root, gradient):
    gram_left = jnp.einsum('...ij,...kj->...ik', gradient, gradient, precision=HIGH)
    gram_right = jnp.einsum('...ji,...jk->...ik', gradient, gradient, precision=HIGH)
    new_left = STAT_DECAY * stat_left + (1.0 - STAT_DECAY) * gram_left
    new_right = STAT_DECAY * stat_right + (1.0 - STAT_DECAY) * gram_right
    shaped = jnp.einsum('...ij,...jk->...ik', left_root, gradient, precision=HIGH)
    shaped = jnp.einsum('...ij,...jk->...ik', shaped, right_root, precision=HIGH)
    new_master = master - RATE_SHAMPOO * (shaped + DECAY_LAYER * master)
    return (new_master, new_left, new_right)

def full_weights(layer_low, block_owner):
    block_count = block_owner.shape[0]
    inverse = jnp.zeros((block_count,), jnp.int32).at[block_owner].set(jnp.arange(block_count, dtype=jnp.int32))
    natural = jnp.take(layer_low, inverse, axis=1)
    pieces = [split_pieces(natural[model_rank], D, DM, FM, KB) for model_rank in range(N_MP)]
    query_w = jnp.concatenate([rank_piece[0][:, :DM] for rank_piece in pieces], axis=1)
    key_w = jnp.concatenate([rank_piece[0][:, DM:2 * DM] for rank_piece in pieces], axis=1)
    value_w = jnp.concatenate([rank_piece[0][:, 2 * DM:] for rank_piece in pieces], axis=1)
    output_w = jnp.concatenate([rank_piece[1] for rank_piece in pieces], axis=0)
    upward_w = jnp.concatenate([rank_piece[2] for rank_piece in pieces], axis=1)
    downward_w = jnp.concatenate([rank_piece[3] for rank_piece in pieces], axis=0)
    return (query_w, key_w, value_w, output_w, upward_w, downward_w)

def row_loss(weights, row_data):
    query_w, key_w, value_w, output_w, upward_w, downward_w, table_low, vectors = weights
    token_ids, lengths, places, target_ids = row_data
    segment, offset = positions_of(lengths, LEN)
    ff_rows = FF // D
    tail_rows = vectors[LEN:]
    embedded = jnp.take(table_low, token_ids, axis=0) + jnp.take(vectors, offset, axis=0)
    normed_x = layer_norm(embedded, tail_rows[0], tail_rows[1])
    x_low = low(normed_x)
    queries = low(low_back(jnp.dot(x_low, query_w, precision=HIGH) + tail_rows[2]))
    key_vecs = low(low_back(jnp.dot(x_low, key_w, precision=HIGH)))
    value_vecs = low(low_back(jnp.dot(x_low, value_w, precision=HIGH) + tail_rows[3]))
    scale_factor = HD ** (-0.5)
    raw_scores = jnp.einsum('qhd,khd->hqk', queries.reshape(LEN, HEADS, HD), key_vecs.reshape(LEN, HEADS, HD), precision=HIGH) * scale_factor
    same_seq = segment[:, None] == segment[None, :]
    scores = low_back(jnp.where(same_seq[None], raw_scores, MASK_FILL))
    attn_probs = jax.nn.softmax(scores, axis=-1)
    mixed = jnp.einsum('hqk,khd->qhd', low(attn_probs), value_vecs.reshape(LEN, HEADS, HD), precision=HIGH).reshape(LEN, D)
    mixed_low = low(low_back(mixed))
    attended = low_back(jnp.dot(mixed_low, output_w, precision=HIGH) + tail_rows[4])
    first_out = layer_norm(normed_x + attended, tail_rows[5], tail_rows[6])
    first_low = low(first_out)
    upper_pre = low_back(jnp.dot(first_low, upward_w, precision=HIGH) + tail_rows[7:7 + ff_rows].reshape(FF))
    acted_low = low(gelu_exact(upper_pre))
    branch = low_back(jnp.dot(acted_low, downward_w, precision=HIGH) + tail_rows[7 + ff_rows])
    second_out = layer_norm(first_out + branch, tail_rows[8 + ff_rows], tail_rows[9 + ff_rows])
    picked = low(jnp.take(second_out, places, axis=0))
    logits = low_back(jnp.dot(picked, table_low.T, precision=HIGH))
    log_total = jax.nn.logsumexp(logits, axis=-1)
    chosen = jnp.take_along_axis(logits, target_ids[:, None], axis=1)[:, 0]
    return jnp.sum(log_total - chosen)

def reference(input_ids, seq_lengths, loss_positions, targets, block_owner, layer_master, stats_left, stats_right, root_left, root_right, table_master, table_first, table_second, vector_master, vector_first, vector_second):

    def total_loss(layer_w, table_w, vector_w):
        matrices = full_weights(low(layer_w), block_owner)
        weights = matrices + (low(table_w), vector_w)
        checked = jax.checkpoint(row_loss)

        def add_row(running, row_data):
            return (running + checked(weights, row_data), None)
        total_sum, unused = lax.scan(add_row, jnp.zeros((), jnp.float32), (input_ids, seq_lengths, loss_positions, targets))
        return total_sum
    total_sum, pullback = jax.vjp(total_loss, layer_master, table_master, vector_master)
    grad_layer, grad_table, grad_vector = pullback(jnp.ones((), jnp.float32))
    squares = jnp.sum(grad_layer * grad_layer) + jnp.sum(grad_table * grad_table) + jnp.sum(grad_vector * grad_vector)
    grad_norm = jnp.sqrt(squares)
    limit = CLIP_FACTOR * jnp.sqrt(jnp.float32(COUNT))
    factor = jnp.minimum(1.0, limit / grad_norm)
    layer_new, left_new, right_new = shampoo_step(layer_master, stats_left, stats_right, root_left, root_right, grad_layer * factor)
    table_new, table_one, table_two = adam_step(table_master, table_first, table_second, grad_table * factor, DECAY_TABLE)
    vector_new, vector_one, vector_two = adam_step(vector_master, vector_first, vector_second, grad_vector * factor, 0.0)
    loss = total_sum / jnp.float32(COUNT)
    return (loss, grad_norm, layer_new, left_new, right_new, table_new, table_one, table_two, vector_new, vector_one, vector_two)
```

```python
import math

import jax
import jax.numpy as jnp
from jax import lax
from jax.experimental import pallas as pl
from jax.experimental.pallas import tpu as pltpu
from jax.sharding import PartitionSpec as P

D = 1024
HEADS = 16
HD = 64
FF = 4096
VOC_DEV = 197
VOC_PAD = 208
LEN = 512
POS = 80
KB = 128

HIGH = lax.Precision.HIGHEST
EPS_NORM = 1e-05
EPS_ADAM = 1e-08
BETA_FIRST = 0.5
BETA_SECOND = 0.5
RATE_ADAM = 0.01
RATE_SHAMPOO = 0.03
DECAY_TABLE = 0.01
DECAY_LAYER = 0.01
STAT_DECAY = 0.5
CLIP_FACTOR = 16.0
MASK_FILL = -1000000000.0
RING = 4
VMEM_LIMIT = 56 * 1024 * 1024

f32 = jnp.float32
bf16 = jnp.bfloat16
f16 = jnp.float16


def swap(value, axis, ways, bit):
    pairs = [(i, i ^ bit) for i in range(ways)]
    return jax.tree.map(lambda part: lax.ppermute(part, axis, pairs), value)


def ring_step(value):
    pairs = [(i, (i + 2) % (2 * RING)) for i in range(2 * RING)]
    return lax.ppermute(value, "dp", pairs)


def after(values, *others):
    flat, tree = jax.tree.flatten(values)
    tied = lax.optimization_barrier(tuple(flat) + tuple(others))
    return jax.tree.unflatten(tree, tied[: len(flat)])


def gather_stream(parts):
    held = [[part] for part in parts]
    crossed = [[] for _ in parts]
    jobs_z = [(p, k) for p in range(len(parts)) for k in range(RING - 1)]
    jobs_x = [(p, k) for p in range(len(parts)) for k in range(RING)]
    done_z = 0
    waits = ()
    for slot, (p, k) in enumerate(jobs_x):
        fresh = []
        x_source = held[p][k]
        x_source = after(x_source, *waits) if waits else x_source
        got_x = swap(x_source, "dp", 2 * RING, 1)
        fresh.append(got_x)
        if done_z < len(jobs_z):
            q, j = jobs_z[done_z]
            if len(held[q]) == j + 1:
                z_source = held[q][j]
                z_source = after(z_source, *waits) if waits else z_source
                got_z = ring_step(z_source)
                fresh.append(got_z)
                done_z += 1
                fresh = list(lax.optimization_barrier(tuple(fresh)))
                held[q].append(fresh[1])
        crossed[p].append(fresh[0])
        waits = tuple(fresh)
    return [
        [piece for k in range(RING) for piece in (held[p][k], crossed[p][k])]
        for p in range(len(parts))
    ]


def reduce_stream(stacked, kind):
    def narrow(value):
        return value.astype(kind)

    moving = None
    for slot in range(RING):
        k = (slot + 1) % RING
        outgoing = narrow(stacked[2 * k + 1])
        if moving is not None:
            outgoing, moving = lax.optimization_barrier((outgoing, moving))
        got = swap(outgoing, "dp", 2 * RING, 1)
        total = stacked[2 * k].astype(f32)
        if moving is not None:
            came = ring_step(moving)
            got, came = lax.optimization_barrier((got, came))
            total = total + came.astype(f32)
        total = total + got.astype(f32)
        moving = narrow(total)
    return total


def reduce_mp(value, ways):
    if ways != 4:
        return lax.psum(value, "mp")
    half = value.shape[0] // 2
    low_bit = lax.axis_index("mp") & 1
    mine = lax.dynamic_slice_in_dim(value, low_bit * half, half, 0)
    other = lax.dynamic_slice_in_dim(value, (1 - low_bit) * half, half, 0)
    mine = mine + swap(other, "mp", ways, 1)
    mine = mine + swap(mine, "mp", ways, 2)
    other = swap(mine, "mp", ways, 1)
    return jnp.where(
        low_bit == 0,
        jnp.concatenate([mine, other], axis=0),
        jnp.concatenate([other, mine], axis=0),
    )


def butterfly(value, combine, dp, mp, both=True):
    axes = [("mp", mp)] + ([("dp", dp)] if both else [])
    for axis, ways in axes:
        bit = 1
        while bit < ways:
            value = combine(value, swap(value, axis, ways, bit))
            bit *= 2
    return value


def gelu_exact(values):
    return 0.5 * values * (1.0 + lax.erf(values * 0.7071067811865476))


def gelu_slope(values):
    cumulative = 0.5 * (1.0 + lax.erf(values * 0.7071067811865476))
    density = jnp.exp(-0.5 * values * values) * 0.3989422804014327
    return cumulative + values * density


def norm_forward(values, norm_gain, norm_shift):
    row_mean = jnp.mean(values, axis=-1, keepdims=True)
    centered = values - row_mean
    variance = jnp.mean(centered * centered, axis=-1, keepdims=True)
    inv_dev = lax.rsqrt(variance + EPS_NORM)
    normed = centered * inv_dev
    return (normed * norm_gain + norm_shift, normed, inv_dev)


def norm_backward(grad_out, normed, inv_dev, norm_gain):
    scaled = grad_out * norm_gain
    grad_in = inv_dev * (
        scaled
        - jnp.mean(scaled, axis=-1, keepdims=True)
        - normed * jnp.mean(scaled * normed, axis=-1, keepdims=True)
    )
    return (grad_in, jnp.sum(grad_out * normed, axis=0), jnp.sum(grad_out, axis=0))


def positions_of(lengths):
    ends = jnp.stack([jnp.sum(lengths[:, : s + 1], axis=1) for s in range(lengths.shape[1])], axis=1)
    places = jnp.arange(LEN, dtype=jnp.int32)
    passed = places[None, :, None] >= ends[:, None, :]
    segment = jnp.sum(passed.astype(jnp.int32), axis=2)
    start = jnp.max(jnp.where(passed, ends[:, None, :], 0), axis=2)
    return (segment, places[None, :] - start)


def adam_step(master, moment_one, moment_two, gradient, weight_decay):
    new_one = BETA_FIRST * moment_one + (1.0 - BETA_FIRST) * gradient
    new_two = BETA_SECOND * moment_two + (1.0 - BETA_SECOND) * gradient * gradient
    new_master = master - RATE_ADAM * (
        new_one / (jnp.sqrt(new_two) + EPS_ADAM) + weight_decay * master
    )
    return (new_master, new_one, new_two)


def product(left_side, right_side):
    return jnp.dot(left_side, right_side, preferred_element_type=f32)


def against_rows(left_side, right_side):
    return lax.dot_general(
        left_side, right_side, (((1,), (1,)), ((), ())), preferred_element_type=f32
    )


def over_rows(left_side, right_side):
    return lax.dot_general(
        left_side, right_side, (((0,), (0,)), ((), ())), preferred_element_type=f32
    )


def hit_matrix(codes, count, kind=bf16):
    return (codes[:, None] == jnp.arange(count, dtype=jnp.int32)[None, :]).astype(kind)


def over_rows_exact(hits, values):
    upper = values.astype(bf16)
    rest = values - upper.astype(f32)
    lower = rest.astype(bf16)
    return over_rows(hits, upper) + over_rows(hits, lower)


def power_scale(bound):
    safe = jnp.clip(bound, 1e-30, 1e38)
    return jnp.exp2(jnp.ceil(jnp.log2(safe)) - 14.0)


def whole(count):
    return [pl.BlockSpec(memory_space=pltpu.VMEM) for _ in range(count)]


TILES = ((8, 6), (2, 8), (8, 8), (8, 8))


def unpack_kernel(slots, stacked, *outs):
    block = 0
    for (high, wide), out in zip(TILES, outs):
        for i in range(high):
            for j in range(wide):
                out[i * KB : (i + 1) * KB, j * KB : (j + 1) * KB] = stacked[slots[block]]
                block += 1


def pack_kernel(slots, *refs):
    out = refs[-1]
    block = 0
    for (high, wide), grad in zip(TILES, refs[:-1]):
        for i in range(high):
            for j in range(wide):
                tile = grad[i * KB : (i + 1) * KB, j * KB : (j + 1) * KB]
                out[slots[block]] = tile.astype(out.dtype)
                block += 1


def unpack(slots, stacked):
    return pl.pallas_call(
        unpack_kernel,
        out_shape=[jax.ShapeDtypeStruct((h * KB, w * KB), bf16) for h, w in TILES],
        in_specs=[pl.BlockSpec(memory_space=pltpu.SMEM)] + whole(1),
        out_specs=whole(4),
        compiler_params=pltpu.CompilerParams(vmem_limit_bytes=VMEM_LIMIT),
        name="unpack_weights",
    )(slots, stacked)


def pack(slots, grads, kind):
    return pl.pallas_call(
        pack_kernel,
        out_shape=jax.ShapeDtypeStruct((slots.shape[0], KB, KB), kind),
        in_specs=[pl.BlockSpec(memory_space=pltpu.SMEM)] + whole(4),
        out_specs=pl.BlockSpec(memory_space=pltpu.VMEM),
        compiler_params=pltpu.CompilerParams(vmem_limit_bytes=VMEM_LIMIT),
        name="pack_gradients",
    )(slots, *grads)


def local(
    input_ids,
    seq_lengths,
    loss_positions,
    targets,
    block_owner,
    layer_master,
    stats_left,
    stats_right,
    root_left,
    root_right,
    table_master,
    table_first,
    table_second,
    vector_master,
    vector_first,
    vector_second,
):
    mp = lax.axis_size("mp")
    dp = lax.axis_size("dp")
    fast = dp == 2 * RING
    model_rank = lax.axis_index("mp")
    data_rank = lax.axis_index("dp")
    inner = D // mp
    heads_here = HEADS // mp
    ff_rows = FF // D
    hidden = FF // mp
    rows = input_ids.shape[0]
    tokens = rows * LEN
    share = tokens // mp
    own_blocks = layer_master.shape[1]
    blocks = own_blocks * dp
    scale_factor = HD ** (-0.5)

    if fast:
        z_here, x_here = data_rank // 2, data_rank % 2

        def place_of(owner):
            return 2 * ((z_here - owner // 2) % RING) + (owner % 2 + x_here) % 2
    else:

        def place_of(owner):
            return owner

    share_start = ((model_rank % 2) * (mp // 2) + model_rank // 2) * share

    table_low = jnp.pad(table_master.astype(bf16), ((0, VOC_PAD - VOC_DEV), (0, 0)))
    layer_low = layer_master[0].astype(bf16)
    if fast:
        cut_t, cut_b = 112, own_blocks // 2
        streams = [
            gather_stream([table_low[:cut_t], layer_low[:cut_b]]),
            gather_stream([table_low[cut_t:], layer_low[cut_b:]]),
        ]
        table_all = jnp.stack(
            [jnp.concatenate([a, b], axis=0) for a, b in zip(streams[0][0], streams[1][0])]
        ).reshape(dp * VOC_PAD, D)
        layer_all = jnp.stack(
            [jnp.concatenate([a, b], axis=0) for a, b in zip(streams[0][1], streams[1][1])]
        ).reshape(blocks, KB, KB)
    else:
        table_all = lax.all_gather(table_low, "dp", axis=0, tiled=True)
        layer_all = lax.all_gather(layer_low, "dp", axis=0, tiled=True)
    vocab = dp * VOC_PAD

    natural = jnp.arange(blocks, dtype=jnp.int32)
    slot_of = jnp.sum(
        jnp.where(block_owner[None, :] == natural[:, None], natural[None, :], 0), axis=1
    )
    slots = place_of(slot_of // own_blocks) * own_blocks + slot_of % own_blocks

    def codes_of(ids):
        part = ids // VOC_DEV
        code = place_of(part // mp) * VOC_PAD + ids % VOC_DEV
        return jnp.where(part % mp == model_rank, code, -1)

    tail = vector_master[LEN:]
    rank_first = (model_rank == 0).astype(f32)
    bias_query = lax.dynamic_slice_in_dim(tail[2], model_rank * inner, inner)
    bias_value = lax.dynamic_slice_in_dim(tail[3], model_rank * inner, inner)
    bias_up = lax.dynamic_slice_in_dim(tail[7 : 7 + ff_rows].reshape(FF), model_rank * hidden, hidden)

    segment, offset = positions_of(seq_lengths)
    codes = codes_of(input_ids.reshape(-1))
    word_hits = hit_matrix(codes, vocab)
    words = reduce_mp(product(word_hits, table_all).astype(bf16), mp).astype(f32)
    places = jnp.take(vector_master[:LEN], offset.reshape(-1), axis=0)
    x_out, x_normed, x_inv = norm_forward(words + places, tail[0], tail[1])
    x_low = x_out.astype(bf16)
    flat = (jnp.arange(rows, dtype=jnp.int32)[:, None] * LEN + loss_positions).reshape(-1)
    pick_hits = hit_matrix(loss_positions.reshape(-1), LEN).reshape(rows, POS, LEN)
    picked_x = jnp.take(x_out, flat, axis=0)
    picked_x_low = picked_x.astype(bf16)
    pick_segment = jnp.take_along_axis(segment, loss_positions, axis=1)

    joined_w, output_w, upward_w, downward_w = unpack(slots, layer_all)
    query_w = joined_w[:, :inner]
    keyval_w = joined_w[:, inner:]

    keyval = product(x_low, keyval_w)
    keys_low = keyval[:, :inner].astype(bf16).reshape(rows, LEN, heads_here, HD)
    values_low = (keyval[:, inner:] + bias_value).astype(bf16).reshape(rows, LEN, heads_here, HD)
    queries_low = (product(picked_x_low, query_w) + bias_query).astype(bf16)
    queries_low = queries_low.reshape(rows, POS, heads_here, HD)
    scores = jnp.einsum("rqhd,rkhd->rhqk", queries_low, keys_low, preferred_element_type=f32)
    same = pick_segment[:, :, None] == segment[:, None, :]
    scores = jnp.where(same[:, None], scores * scale_factor, MASK_FILL)
    top = jnp.max(scores, axis=-1, keepdims=True)
    raised = jnp.exp(scores - top)
    probs = raised / jnp.sum(raised, axis=-1, keepdims=True)
    probs_low = probs.astype(bf16)
    mixed_low = (
        jnp.einsum("rhqk,rkhd->rqhd", probs_low, values_low, preferred_element_type=f32)
        .reshape(rows * POS, inner)
        .astype(bf16)
    )
    attended = reduce_mp(product(mixed_low, output_w), mp) + tail[4]
    first_out, first_normed, first_inv = norm_forward(picked_x + attended, tail[5], tail[6])
    first_low = first_out.astype(bf16)
    upper_pre = product(first_low, upward_w) + bias_up
    acted_low = gelu_exact(upper_pre).astype(bf16)
    branch = reduce_mp(product(acted_low, downward_w), mp) + tail[7 + ff_rows]
    second_out, second_normed, second_inv = norm_forward(
        first_out + branch, tail[8 + ff_rows], tail[9 + ff_rows]
    )
    picked_low = second_out.astype(bf16)

    logits = against_rows(picked_low, table_all)
    column = jnp.arange(vocab, dtype=jnp.int32)
    logits = jnp.where(column[None, :] % VOC_PAD < VOC_DEV, logits, -jnp.inf)
    target_hit = codes_of(targets.reshape(-1))[:, None] == column[None, :]
    local_top = jnp.max(logits, axis=-1)
    local_total = jnp.sum(jnp.exp(logits - local_top[:, None]), axis=-1)
    local_target = jnp.sum(jnp.where(target_hit, logits, 0.0), axis=-1)

    def join(one, two):
        high = jnp.maximum(one[0], two[0])
        total = one[1] * jnp.exp(one[0] - high) + two[1] * jnp.exp(two[0] - high)
        return jnp.stack([high, total, one[2] + two[2]])

    stats = butterfly(
        jnp.stack([local_top, local_total, local_target]), join, dp, mp, both=False
    )
    global_top, exp_total, target_logit = stats[0], stats[1], stats[2]
    loss_part = jnp.sum(jnp.log(exp_total) + global_top - target_logit) * rank_first
    grad_logits = (
        jnp.exp(logits - global_top[:, None]) / exp_total[:, None] - target_hit.astype(f32)
    ).astype(bf16)
    grad_second = reduce_mp(product(grad_logits, table_all), mp)

    grad_pre2, gain_two, shift_two = norm_backward(
        grad_second, second_normed, second_inv, tail[8 + ff_rows]
    )
    branch_grad = grad_pre2.astype(bf16)
    upper_grad = (against_rows(branch_grad, downward_w) * gelu_slope(upper_pre)).astype(bf16)
    grad_first = reduce_mp(against_rows(upper_grad, upward_w), mp) + grad_pre2
    downward_grad = over_rows(acted_low, branch_grad)
    upward_grad = over_rows(first_low, upper_grad)
    grad_pre1, gain_one, shift_one = norm_backward(grad_first, first_normed, first_inv, tail[5])
    attended_grad = grad_pre1.astype(bf16)
    output_grad = over_rows(mixed_low, attended_grad)
    mixed_grad = against_rows(attended_grad, output_w).astype(bf16)
    mixed_grad = mixed_grad.reshape(rows, POS, heads_here, HD)
    value_grad = jnp.einsum("rhqk,rqhd->rkhd", probs_low, mixed_grad, preferred_element_type=f32)
    probs_grad = jnp.einsum("rqhd,rkhd->rhqk", mixed_grad, values_low, preferred_element_type=f32)
    inner_sum = jnp.sum(probs_grad * probs, axis=-1, keepdims=True)
    scores_grad = (probs * (probs_grad - inner_sum)).astype(bf16)
    query_grad = scale_factor * jnp.einsum(
        "rhqk,rkhd->rqhd", scores_grad, keys_low, preferred_element_type=f32
    )
    key_grad = scale_factor * jnp.einsum(
        "rhqk,rqhd->rkhd", scores_grad, queries_low, preferred_element_type=f32
    )
    query_grad = query_grad.reshape(rows * POS, inner).astype(bf16)
    keyval_grad = jnp.concatenate(
        [key_grad.reshape(tokens, inner), value_grad.reshape(tokens, inner)], axis=1
    ).astype(bf16)
    joined_grad = jnp.concatenate(
        [over_rows(picked_x_low, query_grad), over_rows(x_low, keyval_grad)], axis=1
    )

    kind = bf16
    layer_grad = pack(slots, (joined_grad, output_grad, upward_grad, downward_grad), f32)
    if fast:
        layer_grad = layer_grad.reshape(dp, own_blocks, KB, KB)
        layer_total = jnp.concatenate(
            [
                reduce_stream([layer_grad[r, :cut_b] for r in range(dp)], kind),
                reduce_stream([layer_grad[r, cut_b:] for r in range(dp)], kind),
            ],
            axis=0,
        )
    else:
        layer_total = lax.psum_scatter(layer_grad, "dp", scatter_dimension=0, tiled=True)

    grad_x = against_rows(keyval_grad, keyval_w)
    pick_grad = against_rows(query_grad, query_w) + grad_pre1 * rank_first
    grad_x = grad_x + over_rows_exact(hit_matrix(flat, tokens), pick_grad)
    if mp == 4:
        half, low_bit, high_bit = tokens // 2, model_rank % 2, model_rank // 2
        mine = lax.dynamic_slice_in_dim(grad_x, low_bit * half, half, 0)
        other = lax.dynamic_slice_in_dim(grad_x, (1 - low_bit) * half, half, 0)
        mine = mine + swap(other, "mp", mp, 1)
        keep = lax.dynamic_slice_in_dim(mine, high_bit * share, share, 0)
        other = lax.dynamic_slice_in_dim(mine, (1 - high_bit) * share, share, 0)
        grad_x = keep + swap(other, "mp", mp, 2)
    else:
        grad_x = lax.dynamic_slice_in_dim(lax.psum(grad_x, "mp"), share_start, share, 0)
    grad_embed, gain_zero, shift_zero = norm_backward(
        grad_x,
        lax.dynamic_slice_in_dim(x_normed, share_start, share, 0),
        lax.dynamic_slice_in_dim(x_inv, share_start, share, 0),
        tail[0],
    )
    scale_here = power_scale(jnp.max(jnp.abs(grad_embed)))
    sent = (grad_embed / scale_here).astype(f16)
    if mp == 4:
        pair = (sent, jnp.broadcast_to(scale_here, (1, 128)))
        far = swap(pair, "mp", mp, 2)

        def wide(one):
            return one[0].astype(f32) * one[1][0, 0]

        def ordered(one, two, bit):
            return jnp.where(
                bit == 0, jnp.concatenate([one, two], 0), jnp.concatenate([two, one], 0)
            )

        halves = ordered(sent, far[0], high_bit)
        scales = ordered(pair[1], far[1], high_bit)
        near = swap((halves, scales), "mp", mp, 1)
        all_sent = ordered(halves, near[0], low_bit)
        all_scales = ordered(scales, near[1], low_bit)
        embed_all = (
            all_sent.astype(f32).reshape(mp, share, D) * all_scales[:, :1, None]
        ).reshape(tokens, D)
    else:
        embed_all = jnp.zeros((tokens, D), f32)
        embed_all = lax.psum(
            lax.dynamic_update_slice_in_dim(embed_all, grad_embed, share_start, 0), "mp"
        )

    place_rows = LEN // mp
    per_owner = place_rows // dp
    place_codes = offset.reshape(-1) - model_rank * place_rows
    place_codes = jnp.where(
        (place_codes >= 0) & (place_codes < place_rows),
        place_of(place_codes // per_owner) * per_owner + place_codes % per_owner,
        -1,
    )
    place_grad = over_rows_exact(hit_matrix(place_codes, place_rows), embed_all)
    table_grad = over_rows_exact(word_hits, embed_all) + over_rows(grad_logits, picked_low)
    if fast:
        place_parts = place_grad.reshape(dp, per_owner, D)
        both = jnp.concatenate([table_grad.reshape(dp, VOC_PAD, D), place_parts], axis=1)
        bound = jnp.max(jnp.abs(both))
        bound = butterfly(jnp.broadcast_to(bound, (1, 128)), jnp.maximum, dp, mp)[0, 0]
        scale_all = power_scale(bound * dp)
        both = both / scale_all
        cut = (VOC_PAD + per_owner) // 2
        total = scale_all * jnp.concatenate(
            [
                reduce_stream([both[r, :cut] for r in range(dp)], f16),
                reduce_stream([both[r, cut:] for r in range(dp)], f16),
            ],
            axis=0,
        )
        table_total, place_total = total[:VOC_DEV], total[VOC_PAD:]
    else:
        table_total = lax.psum_scatter(table_grad, "dp", scatter_dimension=0, tiled=True)[:VOC_DEV]
        place_total = lax.psum_scatter(place_grad, "dp", scatter_dimension=0, tiled=True)
    place_sum = lax.all_gather(
        lax.all_gather(place_total, "dp", axis=0, tiled=True), "mp", axis=0, tiled=True
    )

    def spread(part, width, start):
        return lax.dynamic_update_slice_in_dim(jnp.zeros((width,), f32), part, start, 0)

    keyval_sums = jnp.sum(keyval_grad[:, inner:].astype(f32), axis=0)
    query_sums = jnp.sum(query_grad.astype(f32), axis=0)
    up_rows = spread(jnp.sum(upper_grad.astype(f32), axis=0), FF, model_rank * hidden)
    vector_part = jnp.concatenate(
        [
            jnp.stack(
                [
                    gain_zero,
                    shift_zero,
                    spread(query_sums, D, model_rank * inner),
                    spread(keyval_sums, D, model_rank * inner),
                    jnp.sum(attended_grad.astype(f32), axis=0) * rank_first,
                    gain_one * rank_first,
                    shift_one * rank_first,
                ]
            ),
            up_rows.reshape(ff_rows, D),
            jnp.stack(
                [
                    jnp.sum(branch_grad.astype(f32), axis=0) * rank_first,
                    gain_two * rank_first,
                    shift_two * rank_first,
                    jnp.broadcast_to(loss_part, (D,)),
                ]
            ),
        ],
        axis=0,
    )
    vector_part = butterfly(vector_part, jnp.add, dp, mp)
    tail_sum, loss_sum = vector_part[:-1], vector_part[-1, 0]

    squares = (
        jnp.sum(layer_total * layer_total)
        + jnp.sum(table_total * table_total)
        + jnp.sum(place_total * place_total)
    )
    squares = butterfly(jnp.broadcast_to(squares, (1, 128)), jnp.add, dp, mp)[0, 0]
    squares = squares + jnp.sum(tail_sum * tail_sum)
    grad_norm = jnp.sqrt(squares)
    count_all = rows * dp * POS
    limit = CLIP_FACTOR * math.sqrt(count_all)
    factor = jnp.minimum(1.0, limit / grad_norm)

    gradient = layer_total[None] * factor
    gram_left = jnp.einsum("...ij,...kj->...ik", gradient, gradient, precision=HIGH)
    gram_right = jnp.einsum("...ji,...jk->...ik", gradient, gradient, precision=HIGH)
    left_new = STAT_DECAY * stats_left + (1.0 - STAT_DECAY) * gram_left
    right_new = STAT_DECAY * stats_right + (1.0 - STAT_DECAY) * gram_right
    shaped = jnp.einsum("...ij,...jk->...ik", root_left, gradient, precision=HIGH)
    shaped = jnp.einsum("...ij,...jk->...ik", shaped, root_right, precision=HIGH)
    layer_new = layer_master - RATE_SHAMPOO * (shaped + DECAY_LAYER * layer_master)

    table_new, table_one, table_two = adam_step(
        table_master, table_first, table_second, table_total * factor, DECAY_TABLE
    )
    vector_sum = jnp.concatenate([place_sum, tail_sum], axis=0)
    vector_new, vector_one, vector_two = adam_step(
        vector_master, vector_first, vector_second, vector_sum * factor, 0.0
    )
    loss = loss_sum / f32(count_all)
    return (
        loss,
        grad_norm,
        layer_new,
        left_new,
        right_new,
        table_new,
        table_one,
        table_two,
        vector_new,
        vector_one,
        vector_two,
    )


def solution(mesh):
    blocks = P("mp", "dp", None, None)
    vocab = P(("dp", "mp"), None)
    rows = P("dp", None)
    return jax.shard_map(
        local,
        mesh=mesh,
        in_specs=(rows,) * 4 + (P(),) + (blocks,) * 5 + (vocab,) * 3 + (P(),) * 3,
        out_specs=(P(), P()) + (blocks,) * 3 + (vocab,) * 3 + (P(),) * 3,
        check_vma=False,
    )
```

```python
import functools
import math

import jax
import jax.numpy as jnp
from jax import lax
from jax.experimental import pallas as pl
from jax.experimental.pallas import tpu as pltpu
from jax.sharding import PartitionSpec as P

D = 1024
HEADS = 16
HD = 64
FF = 4096
VOC_DEV = 197
VOC_PAD = 208
LEN = 512
POS = 80
KB = 128
STRIP = 1664

HIGH = lax.Precision.HIGHEST
EPS_NORM = 1e-05
EPS_ADAM = 1e-08
BETA_FIRST = 0.5
BETA_SECOND = 0.5
RATE_ADAM = 0.01
RATE_SHAMPOO = 0.03
DECAY_TABLE = 0.01
DECAY_LAYER = 0.01
STAT_DECAY = 0.5
CLIP_FACTOR = 16.0
MASK_FILL = -1000000000.0
RING = 4
VMEM_SPARE = 60 << 20
VMEM_MOST = 60 << 20

f32 = jnp.float32
bf16 = jnp.bfloat16
f16 = jnp.float16


def swap(value, axis, ways, bit):
    pairs = [(i, i ^ bit) for i in range(ways)]
    return jax.tree.map(lambda part: lax.ppermute(part, axis, pairs), value)


def ring_step(value):
    pairs = [(i, (i + 2) % (2 * RING)) for i in range(2 * RING)]
    return lax.ppermute(value, "dp", pairs)


def after(values, *others):
    if not others:
        return values
    flat, tree = jax.tree.flatten(values)
    tied = lax.optimization_barrier(tuple(flat) + tuple(others))
    return jax.tree.unflatten(tree, tied[: len(flat)])


def along_x(value):
    return swap(value, "dp", 2 * RING, 1)


def fence(*values):
    return lax.optimization_barrier(values)


def half_float(value, bound=None):
    scale = power_scale(jnp.max(jnp.abs(value)) if bound is None else bound)
    return (value / scale).astype(f16), jnp.broadcast_to(scale, (1, 128))


def float_half(pair):
    return pair[0].astype(f32) * pair[1][0, 0]


def sum_halves(keep, send, ways):
    keep = keep + swap(send, "mp", ways, 1)
    keep = keep + swap(keep, "mp", ways, 2)
    return keep, swap(keep, "mp", ways, 1)


def near_sum(value, dp, mp):
    near = [swap(value, "mp", mp, bit) for bit in range(1, mp)]
    value = (value + near[0]) + (near[1] + near[2])
    return value + swap(value, "dp", dp, 1)


def far_sum(value, dp):
    far = [swap(value, "dp", dp, 2 * bit) for bit in range(1, RING)]
    return (value + far[0]) + (far[1] + far[2])


def butterfly(value, combine, dp, mp, both=True):
    axes = [("mp", mp)] + ([("dp", dp)] if both else [])
    for axis, ways in axes:
        bit = 1
        while bit < ways:
            value = combine(value, swap(value, axis, ways, bit))
            bit *= 2
    return value


def gelu_exact(values):
    return 0.5 * values * (1.0 + lax.erf(values * 0.7071067811865476))


def gelu_slope(values):
    cumulative = 0.5 * (1.0 + lax.erf(values * 0.7071067811865476))
    density = jnp.exp(-0.5 * values * values) * 0.3989422804014327
    return cumulative + values * density


def norm_forward(values, norm_gain, norm_shift):
    row_mean = jnp.mean(values, axis=-1, keepdims=True)
    centered = values - row_mean
    variance = jnp.mean(centered * centered, axis=-1, keepdims=True)
    inv_dev = lax.rsqrt(variance + EPS_NORM)
    normed = centered * inv_dev
    return (normed * norm_gain + norm_shift, normed, inv_dev)


def norm_backward(grad_out, normed, inv_dev, norm_gain):
    scaled = grad_out * norm_gain
    grad_in = inv_dev * (
        scaled
        - jnp.mean(scaled, axis=-1, keepdims=True)
        - normed * jnp.mean(scaled * normed, axis=-1, keepdims=True)
    )
    return (grad_in, jnp.sum(grad_out * normed, axis=0), jnp.sum(grad_out, axis=0))


def seq_ends_of(lengths):
    return jnp.stack(
        [jnp.sum(lengths[:, : s + 1], axis=1) for s in range(lengths.shape[1])], axis=1
    )


def positions_of(lengths):
    ends = seq_ends_of(lengths)
    places = jnp.arange(LEN, dtype=jnp.int32)
    passed = places[None, :, None] >= ends[:, None, :]
    segment = jnp.sum(passed.astype(jnp.int32), axis=2)
    start = jnp.max(jnp.where(passed, ends[:, None, :], 0), axis=2)
    return (segment, places[None, :] - start)


def adam_step(master, moment_one, moment_two, gradient, weight_decay):
    new_one = BETA_FIRST * moment_one + (1.0 - BETA_FIRST) * gradient
    new_two = BETA_SECOND * moment_two + (1.0 - BETA_SECOND) * gradient * gradient
    new_master = master - RATE_ADAM * (
        new_one / (jnp.sqrt(new_two) + EPS_ADAM) + weight_decay * master
    )
    return (new_master, new_one, new_two)


def product(left_side, right_side):
    return jnp.dot(left_side, right_side, preferred_element_type=f32)


def against_rows(left_side, right_side):
    return lax.dot_general(
        left_side, right_side, (((1,), (1,)), ((), ())), preferred_element_type=f32
    )


def over_rows(left_side, right_side):
    return lax.dot_general(
        left_side, right_side, (((0,), (0,)), ((), ())), preferred_element_type=f32
    )


def hit_matrix(codes, count, kind=bf16):
    return (codes[:, None] == jnp.arange(count, dtype=jnp.int32)[None, :]).astype(kind)


def split(values, parts):
    made = []
    for _ in range(parts):
        part = lax.reduce_precision(values, 8, 7)
        made.append(part.astype(bf16))
        values = values - part
    return made


def rows_exact(hits, values):
    upper, middle, lower = split(values, 3)
    return product(hits, upper) + product(hits, middle) + product(hits, lower)


def power_scale(bound):
    safe = jnp.clip(bound, 1e-30, 1e38)
    return jnp.exp2(jnp.ceil(jnp.log2(safe)) - 14.0)


SMEM = pl.BlockSpec(memory_space=pltpu.SMEM)
VMEM = pl.BlockSpec(memory_space=pltpu.VMEM)
ANY = pl.BlockSpec(memory_space=pl.ANY)


def params(*arrays, spare=VMEM_SPARE):
    total = spare
    for one in arrays:
        *lead, rows, columns = one.shape
        size = jnp.dtype(one.dtype).itemsize
        tile = 32 // size
        total += math.prod(lead) * -(-rows // tile) * tile * -(-columns // 128) * 128 * size
    return pltpu.CompilerParams(vmem_limit_bytes=min(total, VMEM_MOST))


COST = pl.CostEstimate(flops=1, bytes_accessed=1, transcendentals=0)


def shape(dims, kind=f32):
    return jax.ShapeDtypeStruct(dims, kind)


def call(kernel, outs, scalars, arrays, name, scratch=(), spare=VMEM_SPARE):
    return pl.pallas_call(
        kernel,
        out_shape=outs,
        in_specs=[SMEM] * len(scalars) + [VMEM] * len(arrays),
        out_specs=jax.tree.map(lambda _: VMEM, outs),
        scratch_shapes=list(scratch),
        compiler_params=params(*jax.tree.leaves(outs), *arrays, *scratch, spare=spare),
        cost_estimate=COST,
        name=name,
    )(*scalars, *arrays)


def both_halves(mine, other):
    return jnp.concatenate([mine, other], axis=0)


def part_halves(value, keep, send):
    half = value.shape[0] // 2
    keep[...] = value[:half]
    send[...] = value[half:]


def strips(pieces):
    base = 0
    for piece in pieces:
        for start in range(0, piece.shape[0], STRIP):
            size = min(STRIP, piece.shape[0] - start)
            yield base + start, piece, slice(start, start + size)
        base += piece.shape[0]


def embed_kernel(codes, *refs):
    pieces, words, table = refs[:-2], refs[-2], refs[-1]
    for base, piece, rows in strips(pieces):
        table[base : base + rows.stop - rows.start, :] = piece[rows, :]
    step = 256
    for begin in range(0, words.shape[0], step):
        part = slice(begin, begin + step)
        column = lax.broadcasted_iota(jnp.int32, (step, table.shape[0]), 1)
        hits = jnp.where(codes[part, :] == column, 1.0, 0.0).astype(bf16)
        words[part, :] = product(hits, table[...]).astype(bf16)


def embed_strips_kernel(codes, piece, words, total):
    step = pl.program_id(0)

    @pl.when(step == 0)
    def _():
        total[...] = jnp.zeros_like(total)

    size = piece.shape[0]
    column = lax.broadcasted_iota(jnp.int32, (codes.shape[0], size), 1) + step * size
    hits = jnp.where(codes[...] == column, 1.0, 0.0).astype(bf16)
    total[...] += product(hits, piece[...])

    @pl.when(step == pl.num_programs(0) - 1)
    def _():
        words[...] = total[...].astype(bf16)


def embed(codes, pieces):
    tokens = codes.shape[0]
    out = shape((tokens, D), bf16)
    if len(pieces) > 1:
        vocab = sum(piece.shape[0] for piece in pieces)
        scratch = [pltpu.VMEM((vocab, D), bf16)]
        return call(embed_kernel, out, [], [codes, *pieces], "embed", scratch, VMEM_MOST)
    return pl.pallas_call(
        embed_strips_kernel,
        grid=(pieces[0].shape[0] // STRIP,),
        out_shape=out,
        in_specs=[
            pl.BlockSpec((tokens, 1), lambda r: (0, 0)),
            pl.BlockSpec((STRIP, D), lambda r: (r, 0)),
        ],
        out_specs=pl.BlockSpec((tokens, D), lambda r: (0, 0)),
        scratch_shapes=[pltpu.VMEM((tokens, D), f32)],
        compiler_params=pltpu.CompilerParams(vmem_limit_bytes=32 << 20),
        cost_estimate=COST,
        name="embed",
    )(codes, *pieces)


def normalize_kernel(flat, words, places, affine, x_low, picked, picked_low, *rest):
    x_out = rest[-1]
    step = 128
    for begin in range(0, words.shape[0], step):
        part = slice(begin, begin + step)
        out, _, _ = norm_forward(
            words[part, :].astype(f32) + places[part, :], affine[0:1, :], affine[1:2, :]
        )
        x_out[part, :] = out
        x_low[part, :] = out.astype(bf16)

    def pick_row(p, carry):
        picked[pl.ds(p, 1), :] = x_out[pl.ds(flat[p], 1), :]
        return carry

    lax.fori_loop(0, picked.shape[0], pick_row, 0, unroll=8)
    picked_low[...] = picked[...].astype(bf16)


def head_pair(values, lanes):
    zero = jnp.zeros_like(values)
    return jnp.concatenate([jnp.where(lanes, values, zero), jnp.where(lanes, zero, values)], axis=0)


def attend_kernel(groups, downs, acrosses, *refs):
    pieces, refs = refs[:groups], refs[groups:]
    (
        x_mine,
        x_other,
        picked_mine,
        picked_other,
        bias_query,
        bias_keyval,
        segment,
        pick_segment,
        joined_w,
        output_w,
        upward_w,
        downward_w,
        keyval,
        query,
        probs,
        mixed,
        keep,
        send,
        stacked,
        dense,
        x_low,
        sems,
        out_sems,
    ) = refs
    rows = segment.shape[0]
    inner = query.shape[1]
    hidden = upward_w.shape[1]
    each = pieces[0].shape[0]
    loads = [
        pltpu.make_async_copy(piece, stacked.at[pl.ds(g * each, each)], sems.at[g])
        for g, piece in enumerate(pieces)
    ]
    half = x_low.shape[0] // 2
    loads_x = [
        pltpu.make_async_copy(x_mine, x_low.at[pl.ds(0, half)], sems.at[groups]),
        pltpu.make_async_copy(x_other, x_low.at[pl.ds(half, half)], sems.at[groups + 1]),
    ]
    for load in loads + loads_x:
        load.start()
    for g, load in enumerate(loads):
        load.wait()
        for t in range(g * each, (g + 1) * each):
            down = pl.multiple_of(downs[t], KB)
            across = pl.multiple_of(acrosses[t], KB)
            dense[pl.ds(down, KB), pl.ds(across, KB)] = stacked[t]
    start_up, start_down = 3 * inner, 3 * inner + hidden
    stores = [
        pltpu.make_async_copy(dense.at[down, across], out, out_sems.at[n])
        for n, (out, down, across) in enumerate(
            (
                (joined_w, pl.ds(0, D), pl.ds(0, start_up)),
                (output_w, pl.ds(D, inner), pl.ds(0, D)),
                (upward_w, pl.ds(0, D), pl.ds(start_up, hidden)),
                (downward_w, pl.ds(0, hidden), pl.ds(start_down, D)),
            )
        )
    ]
    for store in stores:
        store.start()
    for load in loads_x:
        load.wait()
    pairs = inner // KB
    picked_low = both_halves(picked_mine[...], picked_other[...])
    query[...] = (product(picked_low, dense[:D, :inner]) + bias_query[...]).astype(bf16)
    lanes = lax.broadcasted_iota(jnp.int32, (POS, KB), 1) < HD
    for r in range(rows):
        part = slice(r * LEN, (r + 1) * LEN)
        picks = slice(r * POS, (r + 1) * POS)
        keyval[part, :] = (
            product(x_low[part, :], dense[:D, inner:start_up]) + bias_keyval[...]
        ).astype(bf16)
        same = pick_segment[picks, :] == segment[r : r + 1, :]
        same = jnp.concatenate([same, same], axis=0)
        for pair in range(pairs):
            cut = slice(pair * KB, (pair + 1) * KB)
            cut_v = slice(inner + pair * KB, inner + (pair + 1) * KB)
            both = head_pair(query[picks, cut], lanes)
            scores = against_rows(both, keyval[part, cut]) * HD ** (-0.5)
            scores = jnp.where(same, scores, MASK_FILL)
            raised = jnp.exp(scores - jnp.max(scores, axis=-1, keepdims=True))
            part_probs = raised / jnp.sum(raised, axis=-1, keepdims=True)
            probs[r * pairs + pair] = part_probs
            out = product(part_probs.astype(bf16), keyval[part, cut_v])
            mixed[picks, cut] = jnp.where(lanes, out[:POS], out[POS:]).astype(bf16)
    part_halves(product(mixed[...], dense[D:, :D]), keep, send)
    for store in stores:
        store.wait()


def attend(corners, pieces, x_halves, picked_halves, bias_query, bias_keyval, segment, pick_segment, hidden):
    rows = segment.shape[0]
    inner = bias_query.shape[1]
    tokens, picks = 2 * x_halves[0].shape[0], 2 * picked_halves[0].shape[0]
    groups = len(pieces)
    total = groups * pieces[0].shape[0]
    scratch = [
        pltpu.VMEM((total, KB, KB), bf16),
        pltpu.VMEM((D + inner, 3 * inner + 2 * hidden), bf16),
        pltpu.VMEM((tokens, D), bf16),
    ]
    outs = [
            shape((D, 3 * inner), bf16),
            shape((inner, D), bf16),
            shape((D, hidden), bf16),
            shape((hidden, D), bf16),
            shape((tokens, 2 * inner), bf16),
            shape((picks, inner), bf16),
            shape((rows * inner // KB, 2 * POS, LEN)),
            shape((picks, inner), bf16),
            shape((picks // 2, D)),
            shape((picks // 2, D)),
    ]
    return pl.pallas_call(
        functools.partial(attend_kernel, groups),
        out_shape=outs,
        in_specs=[SMEM] * 2 + [ANY] * (groups + 2) + [VMEM] * 6,
        out_specs=[ANY] * 4 + [VMEM] * 6,
        scratch_shapes=scratch
        + [pltpu.SemaphoreType.DMA((groups + 2,)), pltpu.SemaphoreType.DMA((4,))],
        compiler_params=params(spare=VMEM_MOST),
        cost_estimate=COST,
        name="attend",
    )(*corners, *pieces, *x_halves, *picked_halves, bias_query, bias_keyval, segment, pick_segment)


def forward_kernel(
    mine,
    other,
    picked_mine,
    picked_other,
    affine,
    bias_up,
    upward_w,
    downward_w,
    normed_out,
    inv_out,
    first,
    first_low,
    upper_pre,
    acted,
    keep,
    send,
):
    attended = both_halves(mine[...], other[...]) + affine[0:1, :]
    out, normed, inv = norm_forward(
        both_halves(picked_mine[...], picked_other[...]) + attended,
        affine[1:2, :],
        affine[2:3, :],
    )
    normed_out[...] = normed
    inv_out[...] = inv
    first[...] = out
    first_low[...] = out.astype(bf16)
    upper = product(first_low[...], upward_w[...]) + bias_up[...]
    upper_pre[...] = upper
    acted[...] = gelu_exact(upper).astype(bf16)
    part_halves(product(acted[...], downward_w[...]), keep, send)


def logits_kernel(mine, other, first, affine, target, *refs):
    pieces, refs = refs[:-6], refs[-6:]
    normed_out, inv_out, picked_low, top_feature, logits, stats = refs
    branch = both_halves(mine[...], other[...]) + affine[0:1, :]
    out, normed, inv = norm_forward(first[...] + branch, affine[1:2, :], affine[2:3, :])
    normed_out[...] = normed
    inv_out[...] = inv
    picked_low[...] = out.astype(bf16)
    top_feature[...] = jnp.broadcast_to(jnp.max(jnp.abs(out)), top_feature.shape)
    count = out.shape[0]
    top = jnp.full((1, count), -jnp.inf, f32)
    chosen = jnp.zeros((1, count), f32)
    for base, piece, rows in strips(pieces):
        size = rows.stop - rows.start
        part = against_rows(piece[rows, :], picked_low[...])
        row = lax.broadcasted_iota(jnp.int32, (size, count), 0) + base
        part = jnp.where(row % VOC_PAD < VOC_DEV, part, -jnp.inf)
        logits[base : base + size, :] = part
        top = jnp.maximum(top, jnp.max(part, axis=0, keepdims=True))
        hit = jnp.where(row == target[...], part, 0.0)
        chosen = chosen + jnp.sum(hit, axis=0, keepdims=True)
    total = jnp.zeros((1, count), f32)
    for base, piece, rows in strips(pieces):
        part = logits[base : base + rows.stop - rows.start, :]
        total = total + jnp.sum(jnp.exp(part - top), axis=0, keepdims=True)
    stats[0:1, :] = top
    stats[1:2, :] = total
    stats[2:3, :] = chosen
    stats[3:8, :] = jnp.zeros((5, count), f32)


def head_kernel(own, near, far, across, target, logits, *refs):
    pieces, refs = refs[:-4], refs[-4:]
    grad_logits, loss, keep, send = refs
    count = target.shape[1]
    middle = count // 2

    def turned(one):
        return jnp.concatenate([one[:, middle:], one[:, :middle]], axis=1)

    everyone = (own[...], turned(near[...]), far[...], turned(across[...]))
    top = functools.reduce(jnp.maximum, [one[0:1, :] for one in everyone])
    parts = [one[1:2, :] * jnp.exp(one[0:1, :] - top) for one in everyone]
    total = (parts[0] + parts[1]) + (parts[2] + parts[3])
    chosen = [one[2:3, :] for one in everyone]
    chosen = (chosen[0] + chosen[1]) + (chosen[2] + chosen[3])
    losses = jnp.sum(jnp.log(total) + top - chosen, axis=1, keepdims=True)
    loss[...] = jnp.broadcast_to(losses, loss.shape)
    back = jnp.zeros((count, D), f32)
    for base, piece, rows in strips(pieces):
        size = rows.stop - rows.start
        row = lax.broadcasted_iota(jnp.int32, (size, count), 0) + base
        hit = jnp.where(row == target[...], 1.0, 0.0)
        part = logits[base : base + size, :]
        part = (jnp.exp(part - top) / total - hit).astype(bf16)
        grad_logits[base : base + size, :] = part
        back = back + over_rows(part, piece[rows, :])
    part_halves(back, keep, send)


def backward_kernel(
    mine,
    other,
    normed,
    inv,
    gain,
    upper_pre,
    upward_w,
    downward_w,
    grad_pre2,
    branch_grad,
    upper_grad,
    row_sums,
    upper_sums,
    keep,
    send,
):
    grad_out = both_halves(mine[...], other[...])
    grad_in, gain_sum, shift_sum = norm_backward(grad_out, normed[...], inv[...], gain[...])
    grad_pre2[...] = grad_in
    branch_grad[...] = grad_in.astype(bf16)
    row_sums[0:1, :] = gain_sum[None]
    row_sums[1:2, :] = shift_sum[None]
    row_sums[2:3, :] = jnp.sum(branch_grad[...].astype(f32), axis=0, keepdims=True)
    upper = against_rows(branch_grad[...], downward_w[...]) * gelu_slope(upper_pre[...])
    upper_grad[...] = upper.astype(bf16)
    upper_sums[...] = jnp.sum(upper_grad[...].astype(f32), axis=0, keepdims=True)
    part_halves(against_rows(upper_grad[...], upward_w[...]), keep, send)


def back_attention_kernel(
    positions,
    rank_first,
    mine,
    other,
    grad_pre2,
    first_normed,
    first_inv,
    gain,
    joined_w,
    output_w,
    keyval,
    query,
    probs,
    keep,
    send,
    row_sums,
    query_sums,
    keyval_sums,
    attended_grad,
    query_grad,
    keyval_grad,
    pick_grad,
):
    picks, inner = query.shape
    rows = picks // POS
    pairs = inner // KB
    scale = HD ** (-0.5)
    grad_out = both_halves(mine[...], other[...]) + grad_pre2[...]
    grad_pre1, gain_sum, shift_sum = norm_backward(
        grad_out, first_normed[...], first_inv[...], gain[...]
    )
    attended_grad[...] = grad_pre1.astype(bf16)
    row_sums[0:1, :] = gain_sum[None]
    row_sums[1:2, :] = shift_sum[None]
    row_sums[2:3, :] = jnp.sum(attended_grad[...].astype(f32), axis=0, keepdims=True)
    mixed_grad = against_rows(attended_grad[...], output_w[...]).astype(bf16)
    lanes = lax.broadcasted_iota(jnp.int32, (POS, KB), 1) < HD
    for r in range(rows):
        part = slice(r * LEN, (r + 1) * LEN)
        here = slice(r * POS, (r + 1) * POS)
        for pair in range(pairs):
            cut = slice(pair * KB, (pair + 1) * KB)
            cut_v = slice(inner + pair * KB, inner + (pair + 1) * KB)
            part_probs = probs[r * pairs + pair]
            out_grad = head_pair(mixed_grad[here, cut], lanes)
            both = head_pair(query[here, cut], lanes)
            probs_grad = against_rows(out_grad, keyval[part, cut_v])
            inner_sum = jnp.sum(probs_grad * part_probs, axis=-1, keepdims=True)
            scores_grad = (part_probs * (probs_grad - inner_sum)).astype(bf16)
            back = product(scores_grad, keyval[part, cut])
            query_grad[here, cut] = (jnp.where(lanes, back[:POS], back[POS:]) * scale).astype(bf16)
            keyval_grad[part, cut] = (over_rows(scores_grad, both) * scale).astype(bf16)
            keyval_grad[part, cut_v] = over_rows(part_probs.astype(bf16), out_grad).astype(bf16)
    query_sums[...] = jnp.sum(query_grad[...].astype(f32), axis=0, keepdims=True)
    keyval_sums[...] = jnp.sum(keyval_grad[...].astype(f32), axis=0, keepdims=True)
    pick_grad[...] = (
        against_rows(query_grad[...], joined_w[:, :inner]) + grad_pre1 * rank_first[0]
    )
    for row, out in ((1, send), (0, keep)):
        out[...] = against_rows(keyval_grad[row * LEN : (row + 1) * LEN, :], joined_w[:, inner:])

        def add_row(p, carry):
            spot = positions[row * POS + p]
            out[pl.ds(spot, 1), :] += pick_grad[pl.ds(row * POS + p, 1), :]
            return carry

        lax.fori_loop(0, POS, add_row, 0, unroll=8)


def back_weights_kernel(
    downs,
    acrosses,
    x_mine,
    x_other,
    keyval_grad,
    picked_mine,
    picked_other,
    query_grad,
    mixed,
    attended_grad,
    acted,
    branch_grad,
    first_low,
    upper_grad,
    *rest,
):
    packed, dense = rest[:-1], rest[-1]
    inner = query_grad.shape[1]
    low = dense.dtype
    picked_low = both_halves(picked_mine[...], picked_other[...])
    dense[:D, :inner] = over_rows(picked_low, query_grad[...]).astype(low)
    half = x_mine.shape[0]
    joined = over_rows(x_mine[...], keyval_grad[:half, :])
    joined = joined + over_rows(x_other[...], keyval_grad[half:, :])
    dense[:D, inner : 3 * inner] = joined.astype(low)
    start_up, start_down = 3 * inner, 3 * inner + upper_grad.shape[1]
    dense[:D, start_up:start_down] = over_rows(first_low[...], upper_grad[...]).astype(low)
    dense[:D, start_down:] = over_rows(acted[...], branch_grad[...]).astype(low)
    dense[D:, :D] = over_rows(mixed[...], attended_grad[...]).astype(low)
    spot = 0
    for out in packed:
        for t in range(out.shape[0]):
            down = pl.multiple_of(downs[spot], KB)
            across = pl.multiple_of(acrosses[spot], KB)
            out[t] = dense[pl.ds(down, KB), pl.ds(across, KB)]
            spot += 1


def tile_corners(natural, inner, hidden):
    count_joined, count_output = D // KB * 3 * inner // KB, inner // KB * D // KB
    count_up = D // KB * hidden // KB
    n_joined = natural
    n_output = natural - count_joined
    n_up = n_output - count_output
    n_down = n_up - count_up
    wide_joined, wide, wide_up = 3 * inner // KB, D // KB, hidden // KB
    down = jnp.where(
        n_output < 0,
        n_joined // wide_joined * KB,
        jnp.where(
            n_up < 0,
            D + n_output // wide * KB,
            jnp.where(n_down < 0, n_up // wide_up * KB, n_down // wide * KB),
        ),
    )
    across = jnp.where(
        n_output < 0,
        n_joined % wide_joined * KB,
        jnp.where(
            n_up < 0,
            n_output % wide * KB,
            jnp.where(
                n_down < 0,
                3 * inner + n_up % wide_up * KB,
                3 * inner + hidden + n_down % wide * KB,
            ),
        ),
    )
    return down, across


def embedding_kernel(keep, came, words, places, gain, grad, sums, top):
    _, normed, inv = norm_forward(words[...].astype(f32) + places[...], gain[...], gain[...])
    grad_in, gain_sum, shift_sum = norm_backward(
        keep[...] + came[...], normed, inv, gain[...]
    )
    grad[...] = grad_in
    sums[0:1, :] = gain_sum[None]
    sums[1:2, :] = shift_sum[None]
    top[...] = jnp.broadcast_to(jnp.max(jnp.abs(grad_in)), top.shape)


def place_kernel(codes, upper, lower, grad):
    rows = grad.shape[0]
    hits = lax.broadcasted_iota(jnp.int32, (rows, codes.shape[1]), 0) == codes[...]
    hits = jnp.where(hits, 1.0, 0.0).astype(bf16)
    grad[...] = product(hits, upper[...]) + product(hits, lower[...])


def table_kernel(codes, upper, lower, grad_logits, picked_low, grad, hits):
    @pl.when(pl.program_id(1) == 0)
    def _():
        rows = grad.shape[0]
        row = lax.broadcasted_iota(jnp.int32, hits.shape, 0) + pl.program_id(0) * rows
        hits[...] = jnp.where(row == codes[...], 1.0, 0.0).astype(bf16)

    total = product(hits[...], upper[...]) + product(hits[...], lower[...])
    grad[...] = total + product(grad_logits[...], picked_low[...])


def table_gradient(codes, upper, lower, grad_logits, picked_low):
    vocab, picks = grad_logits.shape
    tokens = upper.shape[0]
    wide = 256

    def columns(high):
        return pl.BlockSpec((high, wide), lambda r, c: (0, c))

    return pl.pallas_call(
        table_kernel,
        grid=(vocab // STRIP, D // wide),
        out_shape=shape((vocab, D)),
        in_specs=[
            pl.BlockSpec((1, tokens), lambda r, c: (0, 0)),
            columns(tokens),
            columns(tokens),
            pl.BlockSpec((STRIP, picks), lambda r, c: (r, 0)),
            columns(picks),
        ],
        out_specs=pl.BlockSpec((STRIP, wide), lambda r, c: (r, c)),
        scratch_shapes=[pltpu.VMEM((STRIP, tokens), bf16)],
        compiler_params=params(),
        cost_estimate=COST,
        name="table_gradient",
    )(codes, upper, lower, grad_logits, picked_low)


def local(
    input_ids,
    seq_lengths,
    loss_positions,
    targets,
    block_owner,
    layer_master,
    stats_left,
    stats_right,
    root_left,
    root_right,
    table_master,
    table_first,
    table_second,
    vector_master,
    vector_first,
    vector_second,
):
    mp = lax.axis_size("mp")
    dp = lax.axis_size("dp")
    fast = dp == 2 * RING
    model_rank = lax.axis_index("mp")
    data_rank = lax.axis_index("dp")
    inner = D // mp
    ff_rows = FF // D
    hidden = FF // mp
    rows = input_ids.shape[0]
    tokens = rows * LEN
    share = tokens // mp
    own_blocks = layer_master.shape[1]
    blocks = own_blocks * dp

    if fast:
        z_here, x_here = data_rank // 2, data_rank % 2

        def place_of(owner):
            return 2 * ((z_here - owner // 2) % RING) + (owner % 2 + x_here) % 2
    else:

        def place_of(owner):
            return owner

    low_bit, high_bit = model_rank % 2, model_rank // 2

    def turned(array):
        return jnp.where(low_bit == 0, array, array[::-1])

    input_ids, seq_lengths = turned(input_ids), turned(seq_lengths)
    loss_positions, targets = turned(loss_positions), turned(targets)
    rank_first = (model_rank == 0).astype(f32)
    tail = vector_master[LEN:]
    bias_query = lax.dynamic_slice_in_dim(tail[2], model_rank * inner, inner)[None]
    bias_value = lax.dynamic_slice_in_dim(tail[3], model_rank * inner, inner)
    bias_keyval = jnp.concatenate([jnp.zeros((inner,), f32), bias_value])[None]
    bias_up = lax.dynamic_slice_in_dim(tail[7 : 7 + ff_rows].reshape(FF), model_rank * hidden, hidden)[None]
    affine_one = tail[4:7]
    affine_two = tail[7 + ff_rows : 10 + ff_rows]

    segment, offset = positions_of(seq_lengths)
    pick_segment = jnp.sum(
        (seq_ends_of(seq_lengths)[:, None, :] <= loss_positions[:, :, None]).astype(jnp.int32), axis=2
    ).reshape(-1, 1)

    def codes_of(ids):
        part = ids // VOC_DEV
        code = place_of(part // mp) * VOC_PAD + ids % VOC_DEV
        return jnp.where(part % mp == model_rank, code, -1)

    codes = codes_of(input_ids.reshape(-1))
    target_codes = codes_of(targets.reshape(1, -1))

    def corners_of():
        number = jnp.arange(blocks, dtype=jnp.int32)
        if fast:
            part = number // own_blocks
            owner = 2 * ((z_here - part // 2) % RING) + (part % 2 + x_here) % 2
            taken = owner * own_blocks + number % own_blocks
            order = jnp.sum(
                jnp.where(taken[:, None] == number[None, :], block_owner[None, :], 0), axis=1
            )
        else:
            order = block_owner
        return tile_corners(order, inner, hidden)

    table_low = jnp.pad(table_master.astype(bf16), ((0, VOC_PAD - VOC_DEV), (0, 0)))
    layer_low = layer_master[0].astype(bf16)
    vocab = dp * VOC_PAD
    words_half = tokens // 2
    def places_of(row):
        return rows_exact(hit_matrix(offset[row], LEN), vector_master[:LEN])

    def normalize(row, words):
        return call(
            normalize_kernel,
            [
                shape((words_half, D), bf16),
                shape((POS, D)),
                shape((POS, D), bf16),
            ],
            [loss_positions[row]],
            [words, places[row], tail[0:2]],
            "normalize",
            [pltpu.VMEM((words_half, D), f32)],
        )

    send_codes, keep_codes = codes[words_half:, None], codes[:words_half, None]
    if fast:
        held, crossed = [table_low], []
        places = []
        for k in range(RING - 1):
            made = [places_of(k)] if k < rows else []
            moved, met, made = fence(ring_step(held[k]), along_x(held[k]), made)
            held.append(moved)
            crossed.append(met)
            places += made
            held[-1], layer_low = fence(held[-1], layer_low)
        moved, met, last = fence(
            ring_step(layer_low), along_x(layer_low), along_x(held[RING - 1])
        )
        crossed.append(last)
        table_parts = [piece for pair in zip(held, crossed) for piece in pair]
        held, crossed = [layer_low, moved], [met]
        send = embed(send_codes, table_parts)
        near = swap(send, "mp", mp, 1)
        keep = embed(keep_codes, table_parts) + near
        moved, met, keep = fence(ring_step(held[1]), along_x(held[1]), keep)
        held.append(moved)
        crossed.append(met)
        far = swap(keep, "mp", mp, 2)
        moved, met, keep, far = fence(ring_step(held[2]), along_x(held[2]), keep, far)
        held.append(moved)
        crossed.append(met)
        words = keep + far
        near = swap(words, "mp", mp, 1)
        x_mine, x_other = normalize(0, words), normalize(1, near)
        met, x_mine, x_other = fence(along_x(held[3]), x_mine, x_other)
        crossed.append(met)
        layer_parts = [piece for pair in zip(held, crossed) for piece in pair]
    else:
        places = [places_of(row) for row in range(rows)]
        table_parts = [lax.all_gather(table_low, "dp", axis=0, tiled=True)]
        layer_parts = [lax.all_gather(layer_low, "dp", axis=0, tiled=True)]
        keep, send = embed(keep_codes, table_parts), embed(send_codes, table_parts)
        words, near = sum_halves(keep, send, mp)
        x_mine, x_other = normalize(0, words), normalize(1, near)

    (
        joined_w,
        output_w,
        upward_w,
        downward_w,
        keyval,
        queries,
        probs,
        mixed_low,
        keep,
        send,
    ) = attend(
        corners_of(),
        layer_parts,
        [x_mine[0], x_other[0]],
        [x_mine[2], x_other[2]],
        bias_query,
        bias_keyval,
        segment,
        pick_segment,
        hidden,
    )
    count = rows * POS
    half_shapes = [shape((count // 2, D)), shape((count // 2, D))]
    row_shape, low_shape = shape((count, D)), shape((count, D), bf16)
    first_normed, first_inv, first_out, first_low, upper_pre, acted_low, keep, send = call(
        forward_kernel,
        [
            row_shape,
            shape((count, 1)),
            row_shape,
            low_shape,
            shape((count, hidden)),
            shape((count, hidden), bf16),
            *half_shapes,
        ],
        [],
        [*sum_halves(keep, send, mp), x_mine[1], x_other[1], affine_one, bias_up, upward_w, downward_w],
        "forward",
    )

    second_normed, second_inv, picked_low, top_feature, logits, stats = call(
        logits_kernel,
        [
            row_shape,
            shape((count, 1)),
            low_shape,
            shape((1, 128)),
            shape((vocab, count)),
            shape((8, count)),
        ],
        [],
        [*sum_halves(keep, send, mp), first_out, affine_two, target_codes, *table_parts],
        "logits",
    )
    everyone = [stats] + [swap(stats, "mp", mp, bit) for bit in range(1, mp)]
    grad_logits, loss_part, keep, send = call(
        head_kernel,
        [shape((vocab, count), bf16), shape((1, 128)), *half_shapes],
        [],
        [*everyone, target_codes, logits, *table_parts],
        "head",
    )

    grad_pre2, branch_grad, upper_grad, sums_two, upper_sums, keep, send = call(
        backward_kernel,
        [
            row_shape,
            low_shape,
            shape((count, hidden), bf16),
            shape((3, D)),
            shape((1, hidden)),
            *half_shapes,
        ],
        [],
        [
            *sum_halves(keep, send, mp),
            second_normed,
            second_inv,
            affine_two[1:2],
            upper_pre,
            upward_w,
            downward_w,
        ],
        "backward",
    )
    keep, send, sums_one, query_sums, keyval_sums, attended_grad, query_grad, keyval_grad = call(
        back_attention_kernel,
        [
            shape((tokens // 2, D)),
            shape((tokens // 2, D)),
            shape((3, D)),
            shape((1, inner)),
            shape((1, 2 * inner)),
            low_shape,
            shape((count, inner), bf16),
            shape((tokens, 2 * inner), bf16),
        ],
        [loss_positions.reshape(-1), rank_first.reshape(1)],
        [
            *sum_halves(keep, send, mp),
            grad_pre2,
            first_normed,
            first_inv,
            affine_one[1:2],
            joined_w,
            output_w,
            keyval,
            queries,
            probs,
        ],
        "back_attention",
        [pltpu.VMEM((count, D), f32)],
        VMEM_MOST,
    )
    groups = dp if fast else 1
    layer_grad = call(
        back_weights_kernel,
        [shape((blocks // groups, KB, KB), bf16)] * groups,
        corners_of(),
        [
            x_mine[0],
            x_other[0],
            keyval_grad,
            x_mine[2],
            x_other[2],
            query_grad,
            mixed_low,
            attended_grad,
            acted_low,
            branch_grad,
            first_low,
            upper_grad,
        ],
        "back_weights",
        [pltpu.VMEM((D + inner, 3 * inner + 2 * hidden), bf16)],
        VMEM_MOST,
    )

    def quarters_of(value):
        return (
            lax.dynamic_slice_in_dim(value, high_bit * share, share, 0),
            lax.dynamic_slice_in_dim(value, (1 - high_bit) * share, share, 0),
        )

    own_words = lax.dynamic_slice_in_dim(words, high_bit * share, share, 0)
    own_places = lax.dynamic_slice_in_dim(places[0], high_bit * share, share, 0)

    def embedding(keep, came):
        return call(
            embedding_kernel,
            [shape((share, D)), shape((2, D)), shape((1, 128))],
            [],
            [keep, came, own_words, own_places, tail[0:1]],
            "embedding",
        )

    def ordered(one, two, bit):
        return jax.tree.map(
            lambda a, b: jnp.where(
                bit == 0, jnp.concatenate([a, b], 0), jnp.concatenate([b, a], 0)
            ),
            one,
            two,
        )

    def embedding_far(keep, send):
        keep, send = quarters_of(keep + swap(send, "mp", mp, 1))
        return keep, swap(half_float(send), "mp", mp, 2)

    def own_embedding(keep, far):
        grad, sums, limit = embedding(keep, float_half(far))
        return half_float(grad, limit[0, 0]), sums, limit

    def all_embedding(sent, far):
        sent = ordered(sent, far, high_bit)
        near = swap(sent, "mp", mp, 1)
        values, scales = jax.tree.map(lambda a, b: jnp.concatenate([a, b], 0), sent, near)
        whole = values.astype(f32).reshape(mp, share, D) * scales[:, :1, None]
        whole = whole.reshape(tokens, D)
        return split(whole, 2)

    def vector_of(sums_zero, limit):
        def spread(part, width, start):
            return lax.dynamic_update_slice_in_dim(jnp.zeros((1, width), f32), part, start, 1)

        bound = share * limit[:, :1] + rank_first * count * top_feature[:, :1]
        return jnp.concatenate(
            [
                sums_zero,
                spread(query_sums, D, model_rank * inner),
                spread(keyval_sums[:, inner:], D, model_rank * inner),
                sums_one[2:3] * rank_first,
                sums_one[0:2] * rank_first,
                spread(upper_sums, FF, model_rank * hidden).reshape(ff_rows, D),
                sums_two[2:3] * rank_first,
                sums_two[0:2] * rank_first,
                jnp.concatenate(
                    [
                        jnp.broadcast_to(loss_part[:, :1] * rank_first, (1, D // 2)),
                        jnp.broadcast_to(bound, (1, D // 2)),
                    ],
                    axis=1,
                ),
            ],
            axis=0,
        )

    place_rows = LEN // mp
    per_owner = place_rows // dp
    place_codes = offset.reshape(1, -1) - model_rank * place_rows
    place_codes = jnp.where(
        (place_codes >= 0) & (place_codes < place_rows),
        place_of(place_codes // per_owner) * per_owner + place_codes % per_owner,
        -1,
    )

    def place_gradient(upper, lower):
        return call(
            place_kernel,
            shape((place_rows, D)),
            [],
            [place_codes, upper, lower],
            "place_gradient",
        )

    def shampoo_products(total):
        scale = power_scale(jnp.max(jnp.abs(total)))
        gradient = total[None] / scale
        return (
            scale,
            jnp.einsum("...ij,...kj->...ik", gradient, gradient, precision=HIGH),
            jnp.einsum("...ji,...jk->...ik", gradient, gradient, precision=HIGH),
            jnp.einsum(
                "...ij,...jk->...ik",
                jnp.einsum("...ij,...jk->...ik", root_left, gradient, precision=HIGH),
                root_right,
                precision=HIGH,
            ),
        )

    def reduce_step(parts, k, moving, kind, beside):
        met = along_x(parts[2 * k + 1].astype(kind))
        if moving is None:
            met, beside = fence(met, beside)
            return parts[2 * k].astype(f32) + met.astype(f32), beside
        came = ring_step(moving.astype(kind))
        met, came, beside = fence(met, came, beside)
        return parts[2 * k].astype(f32) + came.astype(f32) + met.astype(f32), beside

    if fast:
        total, far = reduce_step(layer_grad, 1, None, bf16, embedding_far(keep, send))
        keep, far = far
        sent, sums_zero, limit_here = own_embedding(keep, far)
        far = swap(sent, "mp", mp, 2)
        total, beside = reduce_step(
            layer_grad, 2, total, bf16, (sent, far, sums_zero, limit_here)
        )
        sent, far, sums_zero, limit_here = beside
        upper, lower = all_embedding(sent, far)
        vector_part = vector_of(sums_zero, limit_here)
        vector_part = near_sum(vector_part, dp, mp)
        total, beside = reduce_step(
            layer_grad, 3, total, bf16, (upper, lower, vector_part)
        )
        upper, lower, vector_part = beside
        vector_part = far_sum(vector_part, dp)
        place_grad = place_gradient(upper, lower)
        table_grad = table_gradient(codes[None], upper, lower, grad_logits, picked_low)
        layer_total, beside = reduce_step(
            layer_grad, 0, total, bf16, (vector_part, place_grad, table_grad)
        )
        vector_part, place_grad, table_grad = beside
        scale_all = power_scale(vector_part[-1, D // 2])
        inverse = 1.0 / scale_all

        parts = table_grad.reshape(dp, VOC_PAD, D)[:, :VOC_DEV] * inverse
        place_sent = (place_grad.reshape(dp, per_owner, D) * inverse).astype(f16)
        arrived = [place_sent[0]]
        for r in range(1, dp):
            pairs = [
                (i, 2 * ((i // 2 - r // 2) % RING) + (i % 2 + r % 2) % 2) for i in range(dp)
            ]
            arrived.append(lax.ppermute(place_sent[r], "dp", pairs))
        layer_scale, gram_left, gram_right, shaped = shampoo_products(layer_total)
        total, arrived = reduce_step(parts, 1, None, f16, arrived)
        place_total = sum(one.astype(f32) for one in arrived)
        sent = place_total.astype(f16)
        steps = [sent]
        for shift in range(1, RING):
            pairs = [(i, (i + 2 * shift) % dp) for i in range(dp)]
            steps.append(lax.ppermute(sent, "dp", pairs))
        total, beside = reduce_step(parts, 2, total, f16, (steps, place_total, gram_left))
        steps, place_total, gram_left = beside
        steps = jnp.stack(steps[::-1] * 2)
        steps = lax.dynamic_slice_in_dim(steps, (RING - 1 - z_here) % RING, RING, 0)
        near = along_x(steps)
        total, beside = reduce_step(parts, 3, total, f16, (steps, near, gram_right))
        steps, near, gram_right = beside

        def sided(one, two, bit):
            return jnp.where(bit == 0, jnp.stack([one, two]), jnp.stack([two, one]))

        place_all = sided(steps, near, x_here).transpose(1, 0, 2, 3)
        place_all = place_all.reshape(place_rows, D)
        near = swap(place_all, "mp", mp, 2)
        table_total, beside = reduce_step(
            parts, 0, total, f16, (place_all, near, shaped)
        )
        place_all, near, shaped = beside
        table_total = table_total * scale_all
        place_total = place_total * scale_all
        place_all = sided(place_all, near, high_bit)
        place_all = sided(place_all, swap(place_all, "mp", mp, 1), low_bit)
        place_sum = place_all.transpose(1, 0, 2, 3).reshape(LEN, D).astype(f32) * scale_all
    else:
        layer_total = lax.psum_scatter(
            layer_grad[0].astype(f32), "dp", scatter_dimension=0, tiled=True
        )
        layer_scale, gram_left, gram_right, shaped = shampoo_products(layer_total)
        sent, sums_zero, limit_here = own_embedding(*embedding_far(keep, send))
        upper, lower = all_embedding(sent, swap(sent, "mp", mp, 2))
        vector_part = butterfly(vector_of(sums_zero, limit_here), jnp.add, dp, mp)
        table_grad = table_gradient(codes[None], upper, lower, grad_logits, picked_low)
        table_total = lax.psum_scatter(table_grad, "dp", scatter_dimension=0, tiled=True)[:VOC_DEV]
        place_total = lax.psum_scatter(
            place_gradient(upper, lower), "dp", scatter_dimension=0, tiled=True
        )
        place_sum = lax.all_gather(
            lax.all_gather(place_total, "dp", axis=0, tiled=True), "mp", axis=0, tiled=True
        )
    tail_sum, loss_sum = vector_part[:-1], vector_part[-1, 0]

    squares = (
        jnp.sum(layer_total * layer_total)
        + jnp.sum(table_total * table_total)
        + jnp.sum(place_total * place_total)
    )
    squares = jnp.broadcast_to(squares, (1, 128))
    if fast:
        squares = far_sum(near_sum(squares, dp, mp), dp)[0, 0]
    else:
        squares = butterfly(squares, jnp.add, dp, mp)[0, 0]
    squares = squares + jnp.sum(tail_sum * tail_sum)
    grad_norm = jnp.sqrt(squares)
    count_all = rows * dp * POS
    limit = CLIP_FACTOR * math.sqrt(count_all)
    factor = jnp.minimum(1.0, limit / grad_norm)
    shrink = factor * layer_scale

    left_new = STAT_DECAY * stats_left + (1.0 - STAT_DECAY) * (shrink * shrink) * gram_left
    right_new = STAT_DECAY * stats_right + (1.0 - STAT_DECAY) * (shrink * shrink) * gram_right
    layer_new = layer_master - RATE_SHAMPOO * (shaped * shrink + DECAY_LAYER * layer_master)

    table_new, table_one, table_two = adam_step(
        table_master, table_first, table_second, table_total * factor, DECAY_TABLE
    )
    vector_sum = jnp.concatenate([place_sum, tail_sum], axis=0)
    vector_new, vector_one, vector_two = adam_step(
        vector_master, vector_first, vector_second, vector_sum * factor, 0.0
    )
    loss = loss_sum / f32(count_all)
    return (
        loss,
        grad_norm,
        layer_new,
        left_new,
        right_new,
        table_new,
        table_one,
        table_two,
        vector_new,
        vector_one,
        vector_two,
    )


def solution(mesh):
    blocks = P("mp", "dp", None, None)
    vocab = P(("dp", "mp"), None)
    rows = P("dp", None)
    return jax.shard_map(
        local,
        mesh=mesh,
        in_specs=(rows,) * 4 + (P(),) + (blocks,) * 5 + (vocab,) * 3 + (P(),) * 3,
        out_specs=(P(), P()) + (blocks,) * 3 + (vocab,) * 3 + (P(),) * 3,
        check_vma=False,
    )
```

```python
import functools
import math

import jax
import jax.numpy as jnp
from jax import lax
from jax.experimental import pallas as pl
from jax.experimental.pallas import tpu as pltpu
from jax.sharding import PartitionSpec as P

D = 1024
HEADS = 16
HD = 64
FF = 4096
VOC_DEV = 197
VOC_PAD = 208
LEN = 512
POS = 80
KB = 128
STRIP = 1664

HIGH = lax.Precision.HIGH
EPS_NORM = 1e-05
EPS_ADAM = 1e-08
BETA_FIRST = 0.5
BETA_SECOND = 0.5
RATE_ADAM = 0.01
RATE_SHAMPOO = 0.03
DECAY_TABLE = 0.01
DECAY_LAYER = 0.01
STAT_DECAY = 0.5
CLIP_FACTOR = 16.0
MASK_FILL = -1000000000.0
RING = 4
VMEM_SPARE = 60 << 20
VMEM_MOST = 60 << 20

f32 = jnp.float32
bf16 = jnp.bfloat16
f16 = jnp.float16


def swap(value, axis, ways, bit):
    pairs = [(i, i ^ bit) for i in range(ways)]
    return jax.tree.map(lambda part: lax.ppermute(part, axis, pairs), value)


def ring_step(value):
    pairs = [(i, (i + 2) % (2 * RING)) for i in range(2 * RING)]
    return lax.ppermute(value, "dp", pairs)


def after(values, *others):
    if not others:
        return values
    flat, tree = jax.tree.flatten(values)
    tied = lax.optimization_barrier(tuple(flat) + tuple(others))
    return jax.tree.unflatten(tree, tied[: len(flat)])


def along_x(value):
    return swap(value, "dp", 2 * RING, 1)


def fence(*values):
    return lax.optimization_barrier(values)


def half_float(value, bound=None):
    scale = power_scale(jnp.max(jnp.abs(value)) if bound is None else bound)
    return (value / scale).astype(f16), jnp.broadcast_to(scale, (1, 128))


def float_half(pair):
    return pair[0].astype(f32) * pair[1][0, 0]


def sum_halves(keep, send, ways):
    keep = keep + swap(send, "mp", ways, 1)
    keep = keep + swap(keep, "mp", ways, 2)
    return keep, swap(keep, "mp", ways, 1)


def mp_sum(value, mp):
    near = [swap(value, "mp", mp, bit) for bit in range(1, mp)]
    return (value + near[0]) + (near[1] + near[2])


def x_sum(value, dp):
    return value + swap(value, "dp", dp, 1)


def z_sum(value, dp):
    far = [swap(value, "dp", dp, 2 * bit) for bit in range(1, RING)]
    return (value + far[0]) + (far[1] + far[2])


def butterfly(value, combine, dp, mp, both=True):
    axes = [("mp", mp)] + ([("dp", dp)] if both else [])
    for axis, ways in axes:
        bit = 1
        while bit < ways:
            value = combine(value, swap(value, axis, ways, bit))
            bit *= 2
    return value


def gelu_exact(values):
    return 0.5 * values * (1.0 + lax.erf(values * 0.7071067811865476))


def gelu_slope(values):
    cumulative = 0.5 * (1.0 + lax.erf(values * 0.7071067811865476))
    density = jnp.exp(-0.5 * values * values) * 0.3989422804014327
    return cumulative + values * density


def norm_forward(values, norm_gain, norm_shift):
    row_mean = jnp.mean(values, axis=-1, keepdims=True)
    centered = values - row_mean
    variance = jnp.mean(centered * centered, axis=-1, keepdims=True)
    inv_dev = lax.rsqrt(variance + EPS_NORM)
    normed = centered * inv_dev
    return (normed * norm_gain + norm_shift, normed, inv_dev)


def norm_backward(grad_out, normed, inv_dev, norm_gain):
    scaled = grad_out * norm_gain
    grad_in = inv_dev * (
        scaled
        - jnp.mean(scaled, axis=-1, keepdims=True)
        - normed * jnp.mean(scaled * normed, axis=-1, keepdims=True)
    )
    return (grad_in, jnp.sum(grad_out * normed, axis=0), jnp.sum(grad_out, axis=0))


def seq_ends_of(lengths):
    return jnp.stack(
        [jnp.sum(lengths[:, : s + 1], axis=1) for s in range(lengths.shape[1])], axis=1
    )


def positions_of(lengths):
    ends = seq_ends_of(lengths)
    places = jnp.arange(LEN, dtype=jnp.int32)
    passed = places[None, :, None] >= ends[:, None, :]
    segment = jnp.sum(passed.astype(jnp.int32), axis=2)
    start = jnp.max(jnp.where(passed, ends[:, None, :], 0), axis=2)
    return (segment, places[None, :] - start)


def adam_step(master, moment_one, moment_two, gradient, weight_decay):
    new_one = BETA_FIRST * moment_one + (1.0 - BETA_FIRST) * gradient
    new_two = BETA_SECOND * moment_two + (1.0 - BETA_SECOND) * gradient * gradient
    new_master = master - RATE_ADAM * (
        new_one / (jnp.sqrt(new_two) + EPS_ADAM) + weight_decay * master
    )
    return (new_master, new_one, new_two)


def product(left_side, right_side):
    return jnp.dot(left_side, right_side, preferred_element_type=f32)


def against_rows(left_side, right_side):
    return lax.dot_general(
        left_side, right_side, (((1,), (1,)), ((), ())), preferred_element_type=f32
    )


def over_rows(left_side, right_side):
    return lax.dot_general(
        left_side, right_side, (((0,), (0,)), ((), ())), preferred_element_type=f32
    )


def hit_matrix(codes, count, kind=bf16):
    return (codes[:, None] == jnp.arange(count, dtype=jnp.int32)[None, :]).astype(kind)


def split(values, parts):
    made = []
    for _ in range(parts):
        part = lax.reduce_precision(values, 8, 7)
        made.append(part.astype(bf16))
        values = values - part
    return made


def rows_exact(hits, parts):
    upper, middle, lower = parts
    return product(hits, upper) + product(hits, middle) + product(hits, lower)


def power_scale(bound):
    safe = jnp.clip(bound, 1e-30, 1e38)
    return jnp.exp2(jnp.ceil(jnp.log2(safe)) - 14.0)


SMEM = pl.BlockSpec(memory_space=pltpu.SMEM)
VMEM = pl.BlockSpec(memory_space=pltpu.VMEM)
ANY = pl.BlockSpec(memory_space=pl.ANY)


def params(*arrays, spare=VMEM_SPARE):
    total = spare
    for one in arrays:
        *lead, rows, columns = one.shape
        size = jnp.dtype(one.dtype).itemsize
        tile = 32 // size
        total += math.prod(lead) * -(-rows // tile) * tile * -(-columns // 128) * 128 * size
    return pltpu.CompilerParams(vmem_limit_bytes=min(total, VMEM_MOST))


COST = pl.CostEstimate(flops=1, bytes_accessed=1, transcendentals=0)


def shape(dims, kind=f32):
    return jax.ShapeDtypeStruct(dims, kind)


def call(kernel, outs, scalars, arrays, name, scratch=(), spare=VMEM_SPARE):
    return pl.pallas_call(
        kernel,
        out_shape=outs,
        in_specs=[SMEM] * len(scalars) + [VMEM] * len(arrays),
        out_specs=jax.tree.map(lambda _: VMEM, outs),
        scratch_shapes=list(scratch),
        compiler_params=params(*jax.tree.leaves(outs), *arrays, *scratch, spare=spare),
        cost_estimate=COST,
        name=name,
    )(*scalars, *arrays)


def both_halves(mine, other):
    return jnp.concatenate([mine, other], axis=0)


def part_halves(value, keep, send):
    half = value.shape[0] // 2
    keep[...] = value[:half]
    send[...] = value[half:]


def strips(pieces):
    base = 0
    for piece in pieces:
        for start in range(0, piece.shape[0], STRIP):
            size = min(STRIP, piece.shape[0] - start)
            yield base + start, piece, slice(start, start + size)
        base += piece.shape[0]


def embed_kernel(codes, *refs):
    pieces, words, table = refs[:-2], refs[-2], refs[-1]
    for base, piece, rows in strips(pieces):
        table[base : base + rows.stop - rows.start, :] = piece[rows, :]
    step = 256
    for begin in range(0, words.shape[0], step):
        part = slice(begin, begin + step)
        column = lax.broadcasted_iota(jnp.int32, (step, table.shape[0]), 1)
        hits = jnp.where(codes[part, :] == column, 1.0, 0.0).astype(bf16)
        words[part, :] = product(hits, table[...]).astype(bf16)


def embed_strips_kernel(codes, piece, words, total):
    step = pl.program_id(0)

    @pl.when(step == 0)
    def _():
        total[...] = jnp.zeros_like(total)

    size = piece.shape[0]
    column = lax.broadcasted_iota(jnp.int32, (codes.shape[0], size), 1) + step * size
    hits = jnp.where(codes[...] == column, 1.0, 0.0).astype(bf16)
    total[...] += product(hits, piece[...])

    @pl.when(step == pl.num_programs(0) - 1)
    def _():
        words[...] = total[...].astype(bf16)


def embed(codes, pieces):
    tokens = codes.shape[0]
    out = shape((tokens, D), bf16)
    if len(pieces) > 1:
        vocab = sum(piece.shape[0] for piece in pieces)
        scratch = [pltpu.VMEM((vocab, D), bf16)]
        return call(embed_kernel, out, [], [codes, *pieces], "embed", scratch, VMEM_MOST)
    return pl.pallas_call(
        embed_strips_kernel,
        grid=(pieces[0].shape[0] // STRIP,),
        out_shape=out,
        in_specs=[
            pl.BlockSpec((tokens, 1), lambda r: (0, 0)),
            pl.BlockSpec((STRIP, D), lambda r: (r, 0)),
        ],
        out_specs=pl.BlockSpec((tokens, D), lambda r: (0, 0)),
        scratch_shapes=[pltpu.VMEM((tokens, D), f32)],
        compiler_params=pltpu.CompilerParams(vmem_limit_bytes=32 << 20),
        cost_estimate=COST,
        name="embed",
    )(codes, *pieces)


def normalize_kernel(flat, words, places, affine, x_low, picked, picked_low, *rest):
    x_out = rest[-1]
    step = 128
    for begin in range(0, words.shape[0], step):
        part = slice(begin, begin + step)
        out, _, _ = norm_forward(
            words[part, :].astype(f32) + places[part, :], affine[0:1, :], affine[1:2, :]
        )
        x_out[part, :] = out
        x_low[part, :] = out.astype(bf16)

    def pick_row(p, carry):
        picked[pl.ds(p, 1), :] = x_out[pl.ds(flat[p], 1), :]
        return carry

    lax.fori_loop(0, picked.shape[0], pick_row, 0, unroll=8)
    picked_low[...] = picked[...].astype(bf16)


def head_pair(values, lanes):
    zero = jnp.zeros_like(values)
    return jnp.concatenate([jnp.where(lanes, values, zero), jnp.where(lanes, zero, values)], axis=0)


def attend_kernel(groups, downs, acrosses, *refs):
    pieces, refs = refs[:groups], refs[groups:]
    (
        x_mine,
        x_other,
        picked_mine,
        picked_other,
        bias_query,
        bias_keyval,
        segment,
        pick_segment,
        joined_w,
        output_w,
        upward_w,
        downward_w,
        keyval,
        query,
        probs,
        mixed,
        keep,
        send,
        stacked,
        dense,
        x_low,
        sems,
        out_sems,
    ) = refs
    rows = segment.shape[0]
    inner = query.shape[1]
    hidden = upward_w.shape[1]
    sizes = [piece.shape[0] for piece in pieces]
    starts = [sum(sizes[:g]) for g in range(groups)]
    loads = [
        pltpu.make_async_copy(piece, stacked.at[pl.ds(start, size)], sems.at[g])
        for g, (piece, start, size) in enumerate(zip(pieces, starts, sizes))
    ]
    half = x_low.shape[0] // 2
    loads_x = [
        pltpu.make_async_copy(x_mine, x_low.at[pl.ds(0, half)], sems.at[groups]),
        pltpu.make_async_copy(x_other, x_low.at[pl.ds(half, half)], sems.at[groups + 1]),
    ]
    for load in loads + loads_x:
        load.start()
    for g, load in enumerate(loads):
        load.wait()
        for t in range(starts[g], starts[g] + sizes[g]):
            down = pl.multiple_of(downs[t], KB)
            across = pl.multiple_of(acrosses[t], KB)
            dense[pl.ds(down, KB), pl.ds(across, KB)] = stacked[t]
    start_up, start_down = 3 * inner, 3 * inner + hidden
    stores = [
        pltpu.make_async_copy(dense.at[down, across], out, out_sems.at[n])
        for n, (out, down, across) in enumerate(
            (
                (joined_w, pl.ds(0, D), pl.ds(0, start_up)),
                (output_w, pl.ds(D, inner), pl.ds(0, D)),
                (upward_w, pl.ds(0, D), pl.ds(start_up, hidden)),
                (downward_w, pl.ds(0, hidden), pl.ds(start_down, D)),
            )
        )
    ]
    for store in stores:
        store.start()
    for load in loads_x:
        load.wait()
    pairs = inner // KB
    picked_low = both_halves(picked_mine[...], picked_other[...])
    query[...] = (product(picked_low, dense[:D, :inner]) + bias_query[...]).astype(bf16)
    lanes = lax.broadcasted_iota(jnp.int32, (POS, KB), 1) < HD
    for r in range(rows):
        part = slice(r * LEN, (r + 1) * LEN)
        picks = slice(r * POS, (r + 1) * POS)
        keyval[part, :] = (
            product(x_low[part, :], dense[:D, inner:start_up]) + bias_keyval[...]
        ).astype(bf16)
        same = pick_segment[picks, :] == segment[r : r + 1, :]
        same = jnp.concatenate([same, same], axis=0)
        for pair in range(pairs):
            cut = slice(pair * KB, (pair + 1) * KB)
            cut_v = slice(inner + pair * KB, inner + (pair + 1) * KB)
            both = head_pair(query[picks, cut], lanes)
            scores = against_rows(both, keyval[part, cut]) * HD ** (-0.5)
            scores = jnp.where(same, scores, MASK_FILL)
            raised = jnp.exp(scores - jnp.max(scores, axis=-1, keepdims=True))
            part_probs = raised / jnp.sum(raised, axis=-1, keepdims=True)
            probs[r * pairs + pair] = part_probs
            out = product(part_probs.astype(bf16), keyval[part, cut_v])
            mixed[picks, cut] = jnp.where(lanes, out[:POS], out[POS:]).astype(bf16)
    part_halves(product(mixed[...], dense[D:, :D]), keep, send)
    for store in stores:
        store.wait()


def attend(corners, pieces, x_halves, picked_halves, bias_query, bias_keyval, segment, pick_segment, hidden):
    rows = segment.shape[0]
    inner = bias_query.shape[1]
    tokens, picks = 2 * x_halves[0].shape[0], 2 * picked_halves[0].shape[0]
    groups = len(pieces)
    total = sum(piece.shape[0] for piece in pieces)
    scratch = [
        pltpu.VMEM((total, KB, KB), bf16),
        pltpu.VMEM((D + inner, 3 * inner + 2 * hidden), bf16),
        pltpu.VMEM((tokens, D), bf16),
    ]
    outs = [
            shape((D, 3 * inner), bf16),
            shape((inner, D), bf16),
            shape((D, hidden), bf16),
            shape((hidden, D), bf16),
            shape((tokens, 2 * inner), bf16),
            shape((picks, inner), bf16),
            shape((rows * inner // KB, 2 * POS, LEN)),
            shape((picks, inner), bf16),
            shape((picks // 2, D)),
            shape((picks // 2, D)),
    ]
    return pl.pallas_call(
        functools.partial(attend_kernel, groups),
        out_shape=outs,
        in_specs=[SMEM] * 2 + [ANY] * (groups + 2) + [VMEM] * 6,
        out_specs=[ANY] * 4 + [VMEM] * 6,
        scratch_shapes=scratch
        + [pltpu.SemaphoreType.DMA((groups + 2,)), pltpu.SemaphoreType.DMA((4,))],
        compiler_params=params(spare=VMEM_MOST),
        cost_estimate=COST,
        name="attend",
    )(*corners, *pieces, *x_halves, *picked_halves, bias_query, bias_keyval, segment, pick_segment)


def forward_kernel(
    mine,
    other,
    picked_mine,
    picked_other,
    affine,
    bias_up,
    upward_w,
    downward_w,
    normed_out,
    inv_out,
    first,
    first_low,
    upper_pre,
    acted,
    keep,
    send,
):
    attended = both_halves(mine[...], other[...]) + affine[0:1, :]
    out, normed, inv = norm_forward(
        both_halves(picked_mine[...], picked_other[...]) + attended,
        affine[1:2, :],
        affine[2:3, :],
    )
    normed_out[...] = normed
    inv_out[...] = inv
    first[...] = out
    first_low[...] = out.astype(bf16)
    upper = product(first_low[...], upward_w[...]) + bias_up[...]
    upper_pre[...] = upper
    acted[...] = gelu_exact(upper).astype(bf16)
    part_halves(product(acted[...], downward_w[...]), keep, send)


def logits_kernel(mine, other, first, affine, target, *refs):
    pieces, refs = refs[:-6], refs[-6:]
    normed_out, inv_out, picked_low, top_feature, logits, stats = refs
    branch = both_halves(mine[...], other[...]) + affine[0:1, :]
    out, normed, inv = norm_forward(first[...] + branch, affine[1:2, :], affine[2:3, :])
    normed_out[...] = normed
    inv_out[...] = inv
    picked_low[...] = out.astype(bf16)
    top_feature[...] = jnp.broadcast_to(jnp.max(jnp.abs(out)), top_feature.shape)
    count = out.shape[0]
    top = jnp.full((1, count), -jnp.inf, f32)
    chosen = jnp.zeros((1, count), f32)
    for base, piece, rows in strips(pieces):
        size = rows.stop - rows.start
        part = against_rows(piece[rows, :], picked_low[...])
        row = lax.broadcasted_iota(jnp.int32, (size, count), 0) + base
        part = jnp.where(row % VOC_PAD < VOC_DEV, part, -jnp.inf)
        logits[base : base + size, :] = part
        top = jnp.maximum(top, jnp.max(part, axis=0, keepdims=True))
        hit = jnp.where(row == target[...], part, 0.0)
        chosen = chosen + jnp.sum(hit, axis=0, keepdims=True)
    total = jnp.zeros((1, count), f32)
    for base, piece, rows in strips(pieces):
        part = logits[base : base + rows.stop - rows.start, :]
        total = total + jnp.sum(jnp.exp(part - top), axis=0, keepdims=True)
    stats[0:1, :] = top
    stats[1:2, :] = total
    stats[2:3, :] = chosen
    stats[3:8, :] = jnp.zeros((5, count), f32)


def head_kernel(own, near, far, across, target, logits, *refs):
    pieces, refs = refs[:-4], refs[-4:]
    grad_logits, loss, keep, send = refs
    count = target.shape[1]
    middle = count // 2

    def turned(one):
        return jnp.concatenate([one[:, middle:], one[:, :middle]], axis=1)

    everyone = (own[...], turned(near[...]), far[...], turned(across[...]))
    top = functools.reduce(jnp.maximum, [one[0:1, :] for one in everyone])
    parts = [one[1:2, :] * jnp.exp(one[0:1, :] - top) for one in everyone]
    total = (parts[0] + parts[1]) + (parts[2] + parts[3])
    chosen = [one[2:3, :] for one in everyone]
    chosen = (chosen[0] + chosen[1]) + (chosen[2] + chosen[3])
    losses = jnp.sum(jnp.log(total) + top - chosen, axis=1, keepdims=True)
    loss[...] = jnp.broadcast_to(losses, loss.shape)
    back = jnp.zeros((count, D), f32)
    for base, piece, rows in strips(pieces):
        size = rows.stop - rows.start
        row = lax.broadcasted_iota(jnp.int32, (size, count), 0) + base
        hit = jnp.where(row == target[...], 1.0, 0.0)
        part = logits[base : base + size, :]
        part = (jnp.exp(part - top) / total - hit).astype(bf16)
        grad_logits[base : base + size, :] = part
        back = back + over_rows(part, piece[rows, :])
    part_halves(back, keep, send)


def backward_kernel(
    mine,
    other,
    normed,
    inv,
    gain,
    upper_pre,
    upward_w,
    downward_w,
    grad_pre2,
    branch_grad,
    upper_grad,
    row_sums,
    upper_sums,
    keep,
    send,
):
    grad_out = both_halves(mine[...], other[...])
    grad_in, gain_sum, shift_sum = norm_backward(grad_out, normed[...], inv[...], gain[...])
    grad_pre2[...] = grad_in
    branch_grad[...] = grad_in.astype(bf16)
    row_sums[0:1, :] = gain_sum[None]
    row_sums[1:2, :] = shift_sum[None]
    row_sums[2:3, :] = jnp.sum(branch_grad[...].astype(f32), axis=0, keepdims=True)
    upper = against_rows(branch_grad[...], downward_w[...]) * gelu_slope(upper_pre[...])
    upper_grad[...] = upper.astype(bf16)
    upper_sums[...] = jnp.sum(upper_grad[...].astype(f32), axis=0, keepdims=True)
    part_halves(against_rows(upper_grad[...], upward_w[...]), keep, send)


def back_attention_kernel(
    positions,
    rank_first,
    mine,
    other,
    grad_pre2,
    first_normed,
    first_inv,
    gain,
    joined_w,
    output_w,
    keyval,
    query,
    probs,
    keep,
    send,
    row_sums,
    query_sums,
    keyval_sums,
    attended_grad,
    query_grad,
    keyval_grad,
    pick_grad,
):
    picks, inner = query.shape
    rows = picks // POS
    pairs = inner // KB
    scale = HD ** (-0.5)
    grad_out = both_halves(mine[...], other[...]) + grad_pre2[...]
    grad_pre1, gain_sum, shift_sum = norm_backward(
        grad_out, first_normed[...], first_inv[...], gain[...]
    )
    attended_grad[...] = grad_pre1.astype(bf16)
    row_sums[0:1, :] = gain_sum[None]
    row_sums[1:2, :] = shift_sum[None]
    row_sums[2:3, :] = jnp.sum(attended_grad[...].astype(f32), axis=0, keepdims=True)
    mixed_grad = against_rows(attended_grad[...], output_w[...]).astype(bf16)
    lanes = lax.broadcasted_iota(jnp.int32, (POS, KB), 1) < HD
    for r in range(rows):
        part = slice(r * LEN, (r + 1) * LEN)
        here = slice(r * POS, (r + 1) * POS)
        for pair in range(pairs):
            cut = slice(pair * KB, (pair + 1) * KB)
            cut_v = slice(inner + pair * KB, inner + (pair + 1) * KB)
            part_probs = probs[r * pairs + pair]
            out_grad = head_pair(mixed_grad[here, cut], lanes)
            both = head_pair(query[here, cut], lanes)
            probs_grad = against_rows(out_grad, keyval[part, cut_v])
            inner_sum = jnp.sum(probs_grad * part_probs, axis=-1, keepdims=True)
            scores_grad = (part_probs * (probs_grad - inner_sum)).astype(bf16)
            back = product(scores_grad, keyval[part, cut])
            query_grad[here, cut] = (jnp.where(lanes, back[:POS], back[POS:]) * scale).astype(bf16)
            keyval_grad[part, cut] = (over_rows(scores_grad, both) * scale).astype(bf16)
            keyval_grad[part, cut_v] = over_rows(part_probs.astype(bf16), out_grad).astype(bf16)
    query_sums[...] = jnp.sum(query_grad[...].astype(f32), axis=0, keepdims=True)
    keyval_sums[...] = jnp.sum(keyval_grad[...].astype(f32), axis=0, keepdims=True)
    pick_grad[...] = (
        against_rows(query_grad[...], joined_w[:, :inner]) + grad_pre1 * rank_first[0]
    )
    for row, out in ((1, send), (0, keep)):
        out[...] = against_rows(keyval_grad[row * LEN : (row + 1) * LEN, :], joined_w[:, inner:])

        def add_row(p, carry):
            spot = positions[row * POS + p]
            out[pl.ds(spot, 1), :] += pick_grad[pl.ds(row * POS + p, 1), :]
            return carry

        lax.fori_loop(0, POS, add_row, 0, unroll=8)


def back_weights_kernel(
    downs,
    acrosses,
    x_mine,
    x_other,
    keyval_grad,
    picked_mine,
    picked_other,
    query_grad,
    mixed,
    attended_grad,
    acted,
    branch_grad,
    first_low,
    upper_grad,
    *rest,
):
    packed, dense = rest[:-1], rest[-1]
    inner = query_grad.shape[1]
    low = dense.dtype
    picked_low = both_halves(picked_mine[...], picked_other[...])
    dense[:D, :inner] = over_rows(picked_low, query_grad[...]).astype(low)
    half = x_mine.shape[0]
    joined = over_rows(x_mine[...], keyval_grad[:half, :])
    joined = joined + over_rows(x_other[...], keyval_grad[half:, :])
    dense[:D, inner : 3 * inner] = joined.astype(low)
    start_up, start_down = 3 * inner, 3 * inner + upper_grad.shape[1]
    dense[:D, start_up:start_down] = over_rows(first_low[...], upper_grad[...]).astype(low)
    dense[:D, start_down:] = over_rows(acted[...], branch_grad[...]).astype(low)
    dense[D:, :D] = over_rows(mixed[...], attended_grad[...]).astype(low)
    spot = 0
    for out in packed:
        for t in range(out.shape[0]):
            down = pl.multiple_of(downs[spot], KB)
            across = pl.multiple_of(acrosses[spot], KB)
            out[t] = dense[pl.ds(down, KB), pl.ds(across, KB)]
            spot += 1


def tile_corners(natural, inner, hidden):
    count_joined, count_output = D // KB * 3 * inner // KB, inner // KB * D // KB
    count_up = D // KB * hidden // KB
    n_joined = natural
    n_output = natural - count_joined
    n_up = n_output - count_output
    n_down = n_up - count_up
    wide_joined, wide, wide_up = 3 * inner // KB, D // KB, hidden // KB
    down = jnp.where(
        n_output < 0,
        n_joined // wide_joined * KB,
        jnp.where(
            n_up < 0,
            D + n_output // wide * KB,
            jnp.where(n_down < 0, n_up // wide_up * KB, n_down // wide * KB),
        ),
    )
    across = jnp.where(
        n_output < 0,
        n_joined % wide_joined * KB,
        jnp.where(
            n_up < 0,
            n_output % wide * KB,
            jnp.where(
                n_down < 0,
                3 * inner + n_up % wide_up * KB,
                3 * inner + hidden + n_down % wide * KB,
            ),
        ),
    )
    return down, across


def embedding_kernel(keep, came, words, places, gain, grad, sums, top):
    _, normed, inv = norm_forward(words[...].astype(f32) + places[...], gain[...], gain[...])
    grad_in, gain_sum, shift_sum = norm_backward(
        keep[...] + came[...], normed, inv, gain[...]
    )
    grad[...] = grad_in
    sums[0:1, :] = gain_sum[None]
    sums[1:2, :] = shift_sum[None]
    top[...] = jnp.broadcast_to(jnp.max(jnp.abs(grad_in)), top.shape)


def table_kernel(
    codes, place_codes, upper, lower, grad_logits, picked_low, grad, place_grad, hits
):
    rows, place_rows = grad.shape[0], place_grad.shape[0]

    @pl.when(pl.program_id(1) == 0)
    def _():
        row = lax.broadcasted_iota(jnp.int32, (rows, hits.shape[1]), 0)
        row = row + pl.program_id(0) * rows
        hits[:rows, :] = jnp.where(row == codes[...], 1.0, 0.0).astype(bf16)
        row = lax.broadcasted_iota(jnp.int32, (place_rows, hits.shape[1]), 0)
        hits[rows:, :] = jnp.where(row == place_codes[...], 1.0, 0.0).astype(bf16)

    total = product(hits[...], upper[...]) + product(hits[...], lower[...])
    grad[...] = total[:rows] + product(grad_logits[...], picked_low[...])
    place_grad[...] = total[rows:]


def parts_kernel(codes, place_codes, upper, lower, grad_logits, picked_low, grad, hits):
    parts, each, _ = grad.shape
    vocab = grad_logits.shape[0]
    place_rows = hits.shape[0] - vocab
    own = place_rows // parts

    @pl.when(pl.program_id(0) == 0)
    def _():
        row = lax.broadcasted_iota(jnp.int32, (vocab, hits.shape[1]), 0)
        hits[:vocab, :] = jnp.where(row == codes[...], 1.0, 0.0).astype(bf16)
        row = lax.broadcasted_iota(jnp.int32, (place_rows, hits.shape[1]), 0)
        hits[vocab:, :] = jnp.where(row == place_codes[...], 1.0, 0.0).astype(bf16)

    total = product(hits[...], upper[...]) + product(hits[...], lower[...])
    words = total[:vocab] + product(grad_logits[...], picked_low[...])
    for r in range(parts):
        grad[r, :VOC_PAD, :] = words[r * VOC_PAD : (r + 1) * VOC_PAD]
        grad[r, VOC_PAD:each, :] = total[vocab + r * own : vocab + (r + 1) * own]


def parts_gradient(parts, codes, place_codes, place_rows, upper, lower, grad_logits, picked_low):
    vocab, picks = grad_logits.shape
    tokens = upper.shape[0]
    wide = 256
    each = (vocab + place_rows) // parts

    def columns(high):
        return pl.BlockSpec((high, wide), lambda c: (0, c))

    row_of_codes = pl.BlockSpec((1, tokens), lambda c: (0, 0))
    return pl.pallas_call(
        parts_kernel,
        grid=(D // wide,),
        out_shape=shape((parts, each, D)),
        in_specs=[
            row_of_codes,
            row_of_codes,
            columns(tokens),
            columns(tokens),
            pl.BlockSpec((vocab, picks), lambda c: (0, 0)),
            columns(picks),
        ],
        out_specs=pl.BlockSpec((parts, each, wide), lambda c: (0, 0, c)),
        scratch_shapes=[pltpu.VMEM((vocab + place_rows, tokens), bf16)],
        compiler_params=pltpu.CompilerParams(vmem_limit_bytes=32 << 20),
        cost_estimate=COST,
        name="table_gradient",
    )(codes, place_codes, upper, lower, grad_logits, picked_low)


def table_gradient(codes, place_codes, place_rows, upper, lower, grad_logits, picked_low):
    vocab, picks = grad_logits.shape
    tokens = upper.shape[0]
    wide = 256

    def columns(high):
        return pl.BlockSpec((high, wide), lambda r, c: (0, c))

    row_of_codes = pl.BlockSpec((1, tokens), lambda r, c: (0, 0))
    return pl.pallas_call(
        table_kernel,
        grid=(vocab // STRIP, D // wide),
        out_shape=[shape((vocab, D)), shape((place_rows, D))],
        in_specs=[
            row_of_codes,
            row_of_codes,
            columns(tokens),
            columns(tokens),
            pl.BlockSpec((STRIP, picks), lambda r, c: (r, 0)),
            columns(picks),
        ],
        out_specs=[pl.BlockSpec((STRIP, wide), lambda r, c: (r, c)), columns(place_rows)],
        scratch_shapes=[pltpu.VMEM((STRIP + place_rows, tokens), bf16)],
        compiler_params=pltpu.CompilerParams(vmem_limit_bytes=32 << 20),
        cost_estimate=COST,
        name="table_gradient",
    )(codes, place_codes, upper, lower, grad_logits, picked_low)


def local(
    input_ids,
    seq_lengths,
    loss_positions,
    targets,
    block_owner,
    layer_master,
    stats_left,
    stats_right,
    root_left,
    root_right,
    table_master,
    table_first,
    table_second,
    vector_master,
    vector_first,
    vector_second,
):
    mp = lax.axis_size("mp")
    dp = lax.axis_size("dp")
    fast = dp == 2 * RING
    model_rank = lax.axis_index("mp")
    data_rank = lax.axis_index("dp")
    inner = D // mp
    ff_rows = FF // D
    hidden = FF // mp
    rows = input_ids.shape[0]
    tokens = rows * LEN
    share = tokens // mp
    own_blocks = layer_master.shape[1]
    blocks = own_blocks * dp

    if fast:
        z_here, x_here = data_rank // 2, data_rank % 2

        def place_of(owner):
            return 2 * ((z_here - owner // 2) % RING) + (owner % 2 + x_here) % 2
    else:

        def place_of(owner):
            return owner

    low_bit, high_bit = model_rank % 2, model_rank // 2

    def turned(array):
        return jnp.where(low_bit == 0, array, array[::-1])

    input_ids, seq_lengths = turned(input_ids), turned(seq_lengths)
    loss_positions, targets = turned(loss_positions), turned(targets)
    rank_first = (model_rank == 0).astype(f32)
    tail = vector_master[LEN:]
    bias_query = lax.dynamic_slice_in_dim(tail[2], model_rank * inner, inner)[None]
    bias_value = lax.dynamic_slice_in_dim(tail[3], model_rank * inner, inner)
    bias_keyval = jnp.concatenate([jnp.zeros((inner,), f32), bias_value])[None]
    bias_up = lax.dynamic_slice_in_dim(tail[7 : 7 + ff_rows].reshape(FF), model_rank * hidden, hidden)[None]
    affine_zero, affine_one = tail[0:2], tail[4:7]
    affine_two = tail[7 + ff_rows : 10 + ff_rows]

    segment, offset = positions_of(seq_lengths)
    pick_segment = jnp.sum(
        (seq_ends_of(seq_lengths)[:, None, :] <= loss_positions[:, :, None]).astype(jnp.int32), axis=2
    ).reshape(-1, 1)

    def codes_of(ids):
        part = ids // VOC_DEV
        code = place_of(part // mp) * VOC_PAD + ids % VOC_DEV
        return jnp.where(part % mp == model_rank, code, -1)

    codes = codes_of(input_ids.reshape(-1))
    target_codes = codes_of(targets.reshape(1, -1))

    def corners_of():
        number = jnp.arange(blocks, dtype=jnp.int32)
        if fast:
            part = number // own_blocks
            owner = 2 * ((z_here - part // 2) % RING) + (part % 2 + x_here) % 2
            taken = owner * own_blocks + number % own_blocks
            order = jnp.sum(
                jnp.where(taken[:, None] == number[None, :], block_owner[None, :], 0), axis=1
            )
        else:
            order = block_owner
        return tile_corners(order, inner, hidden)

    table_low = jnp.pad(table_master.astype(bf16), ((0, VOC_PAD - VOC_DEV), (0, 0)))
    layer_low = layer_master[0].astype(bf16)
    vocab = dp * VOC_PAD
    words_half = tokens // 2
    def places_of(row, parts):
        return rows_exact(hit_matrix(offset[row], LEN), parts)

    def own_of(words):
        return [
            lax.dynamic_slice_in_dim(value, high_bit * share, share, 0)
            for value in (words, places[0])
        ]

    def normalize(row, words):
        return call(
            normalize_kernel,
            [
                shape((words_half, D), bf16),
                shape((POS, D)),
                shape((POS, D), bf16),
            ],
            [row_positions[row]],
            [words, places[row], affine_zero],
            "normalize",
            [pltpu.VMEM((words_half, D), f32)],
        )

    send_codes, keep_codes = codes[words_half:, None], codes[:words_half, None]
    place_rows = LEN // mp
    per_owner = place_rows // dp
    place_codes = offset.reshape(1, -1) - model_rank * place_rows
    place_codes = jnp.where(
        (place_codes >= 0) & (place_codes < place_rows),
        place_of(place_codes // per_owner) * per_owner + place_codes % per_owner,
        -1,
    )
    small = (
        affine_zero,
        affine_one,
        affine_two,
        affine_zero[0:1],
        affine_one[1:2],
        affine_two[1:2],
        bias_query,
        bias_keyval,
        bias_up,
        [loss_positions[row] for row in range(rows)],
        loss_positions.reshape(-1),
        rank_first.reshape(1),
        corners_of(),
        segment,
        pick_segment,
        codes[None],
        target_codes,
        place_codes,
        send_codes,
        keep_codes,
    )
    if fast:
        place_parts = split(vector_master[:LEN], 3)
        moved, met, place_parts, layer_low = fence(
            ring_step(table_low), along_x(table_low), place_parts, layer_low
        )
        held, crossed = [table_low, moved], [met]
        places = [places_of(row, place_parts) for row in range(rows)]
        moved, met, places = fence(ring_step(held[1]), along_x(held[1]), places)
        held.append(moved)
        crossed.append(met)
        moved, met, small = fence(ring_step(held[2]), along_x(held[2]), small)
        held.append(moved)
        crossed.append(met)
    (
        affine_zero,
        affine_one,
        affine_two,
        gain_zero,
        gain_one,
        gain_two,
        bias_query,
        bias_keyval,
        bias_up,
        row_positions,
        all_positions,
        rank_one,
        corners,
        segment,
        pick_segment,
        code_row,
        target_codes,
        place_codes,
        send_codes,
        keep_codes,
    ) = small
    if fast:
        cut = 96
        moved, met, *last = fence(
            ring_step(layer_low),
            along_x(layer_low),
            along_x(held[RING - 1][:cut]),
            ring_step(crossed[RING - 2][cut:]),
        )
        table_parts = [piece for pair in zip(held, crossed) for piece in pair]
        table_parts += [held[RING - 1], *last]
        held, crossed = [layer_low, moved], [met]
        send = embed(send_codes, table_parts)
        near = swap(send, "mp", mp, 1)
        keep = embed(keep_codes, table_parts) + near
        moved, met, keep = fence(ring_step(held[1]), along_x(held[1]), keep)
        held.append(moved)
        crossed.append(met)
        far = swap(keep, "mp", mp, 2)
        moved, met, keep, far = fence(ring_step(held[2]), along_x(held[2]), keep, far)
        held.append(moved)
        crossed.append(met)
        words = keep + far
        near = swap(words, "mp", mp, 1)
        x_mine, x_other = normalize(0, words), normalize(1, near)
        own_words, own_places = own_of(words)
        cut = own_blocks // 2
        *last, x_mine, x_other, own_words, own_places = fence(
            along_x(held[3][:cut]),
            ring_step(crossed[2][cut:]),
            x_mine,
            x_other,
            own_words,
            own_places,
        )
        layer_parts = [piece for pair in zip(held, crossed) for piece in pair]
        layer_parts += [held[3], *last]
    else:
        place_parts = split(vector_master[:LEN], 3)
        places = [places_of(row, place_parts) for row in range(rows)]
        table_parts = [lax.all_gather(table_low, "dp", axis=0, tiled=True)]
        layer_parts = [lax.all_gather(layer_low, "dp", axis=0, tiled=True)]
        keep, send = embed(keep_codes, table_parts), embed(send_codes, table_parts)
        words, near = sum_halves(keep, send, mp)
        x_mine, x_other = normalize(0, words), normalize(1, near)
        own_words, own_places = own_of(words)

    (
        joined_w,
        output_w,
        upward_w,
        downward_w,
        keyval,
        queries,
        probs,
        mixed_low,
        keep,
        send,
    ) = attend(
        corners,
        layer_parts,
        [x_mine[0], x_other[0]],
        [x_mine[2], x_other[2]],
        bias_query,
        bias_keyval,
        segment,
        pick_segment,
        hidden,
    )
    count = rows * POS
    half_shapes = [shape((count // 2, D)), shape((count // 2, D))]
    row_shape, low_shape = shape((count, D)), shape((count, D), bf16)
    first_normed, first_inv, first_out, first_low, upper_pre, acted_low, keep, send = call(
        forward_kernel,
        [
            row_shape,
            shape((count, 1)),
            row_shape,
            low_shape,
            shape((count, hidden)),
            shape((count, hidden), bf16),
            *half_shapes,
        ],
        [],
        [*sum_halves(keep, send, mp), x_mine[1], x_other[1], affine_one, bias_up, upward_w, downward_w],
        "forward",
    )

    second_normed, second_inv, picked_low, top_feature, logits, stats = call(
        logits_kernel,
        [
            row_shape,
            shape((count, 1)),
            low_shape,
            shape((1, 128)),
            shape((vocab, count)),
            shape((8, count)),
        ],
        [],
        [*sum_halves(keep, send, mp), first_out, affine_two, target_codes, *table_parts],
        "logits",
    )
    everyone = [stats] + [swap(stats, "mp", mp, bit) for bit in range(1, mp)]
    grad_logits, loss_part, keep, send = call(
        head_kernel,
        [shape((vocab, count), bf16), shape((1, 128)), *half_shapes],
        [],
        [*everyone, target_codes, logits, *table_parts],
        "head",
    )

    grad_pre2, branch_grad, upper_grad, sums_two, upper_sums, keep, send = call(
        backward_kernel,
        [
            row_shape,
            low_shape,
            shape((count, hidden), bf16),
            shape((3, D)),
            shape((1, hidden)),
            *half_shapes,
        ],
        [],
        [
            *sum_halves(keep, send, mp),
            second_normed,
            second_inv,
            gain_two,
            upper_pre,
            upward_w,
            downward_w,
        ],
        "backward",
    )
    keep, send, sums_one, query_sums, keyval_sums, attended_grad, query_grad, keyval_grad = call(
        back_attention_kernel,
        [
            shape((tokens // 2, D)),
            shape((tokens // 2, D)),
            shape((3, D)),
            shape((1, inner)),
            shape((1, 2 * inner)),
            low_shape,
            shape((count, inner), bf16),
            shape((tokens, 2 * inner), bf16),
        ],
        [all_positions, rank_one],
        [
            *sum_halves(keep, send, mp),
            grad_pre2,
            first_normed,
            first_inv,
            gain_one,
            joined_w,
            output_w,
            keyval,
            queries,
            probs,
        ],
        "back_attention",
        [pltpu.VMEM((count, D), f32)],
        VMEM_MOST,
    )
    groups = dp if fast else 1
    layer_grad = call(
        back_weights_kernel,
        [shape((blocks // groups, KB, KB), bf16)] * groups,
        corners,
        [
            x_mine[0],
            x_other[0],
            keyval_grad,
            x_mine[2],
            x_other[2],
            query_grad,
            mixed_low,
            attended_grad,
            acted_low,
            branch_grad,
            first_low,
            upper_grad,
        ],
        "back_weights",
        [pltpu.VMEM((D + inner, 3 * inner + 2 * hidden), bf16)],
        VMEM_MOST,
    )

    def quarters_of(value):
        return (
            lax.dynamic_slice_in_dim(value, high_bit * share, share, 0),
            lax.dynamic_slice_in_dim(value, (1 - high_bit) * share, share, 0),
        )

    def embedding(keep, came):
        return call(
            embedding_kernel,
            [shape((share, D)), shape((2, D)), shape((1, 128))],
            [],
            [keep, came, own_words, own_places, gain_zero],
            "embedding",
            spare=8 << 20,
        )

    def ordered(one, two, bit):
        return jax.tree.map(
            lambda a, b: jnp.where(
                bit == 0, jnp.concatenate([a, b], 0), jnp.concatenate([b, a], 0)
            ),
            one,
            two,
        )

    def embedding_far(keep, send):
        keep, send = quarters_of(keep + swap(send, "mp", mp, 1))
        return keep, swap(half_float(send), "mp", mp, 2)

    def own_embedding(keep, far):
        grad, sums, limit = embedding(keep, float_half(far))
        return half_float(grad, limit[0, 0]), sums, limit

    def all_embedding(sent, far):
        sent = ordered(sent, far, high_bit)
        near = swap(sent, "mp", mp, 1)
        values, scales = jax.tree.map(lambda a, b: jnp.concatenate([a, b], 0), sent, near)
        whole = values.astype(f32).reshape(mp, share, D) * scales[:, :1, None]
        whole = whole.reshape(tokens, D)
        return split(whole, 2)

    def vector_of(sums_zero, limit):
        def spread(part, width, start):
            return lax.dynamic_update_slice_in_dim(jnp.zeros((1, width), f32), part, start, 1)

        bound = share * limit[:, :1] + rank_first * count * top_feature[:, :1]
        return jnp.concatenate(
            [
                sums_zero,
                spread(query_sums, D, model_rank * inner),
                spread(keyval_sums[:, inner:], D, model_rank * inner),
                sums_one[2:3] * rank_first,
                sums_one[0:2] * rank_first,
                spread(upper_sums, FF, model_rank * hidden).reshape(ff_rows, D),
                sums_two[2:3] * rank_first,
                sums_two[0:2] * rank_first,
                jnp.concatenate(
                    [
                        jnp.broadcast_to(loss_part[:, :1] * rank_first, (1, D // 2)),
                        jnp.broadcast_to(bound, (1, D // 2)),
                    ],
                    axis=1,
                ),
            ],
            axis=0,
        )

    def shampoo_products(total):
        scale = power_scale(jnp.max(jnp.abs(total)))
        gradient = total[None] / scale
        return (
            scale,
            jnp.einsum("...ij,...kj->...ik", gradient, gradient, precision=HIGH),
            jnp.einsum("...ji,...jk->...ik", gradient, gradient, precision=HIGH),
            jnp.einsum(
                "...ij,...jk->...ik",
                jnp.einsum("...ij,...jk->...ik", root_left, gradient, precision=HIGH),
                root_right,
                precision=HIGH,
            ),
        )

    def reduce_step(parts, k, moving, kind, beside, factor=None):
        def scaled(part):
            part = part.astype(f32)
            return part if factor is None else part * factor

        met = along_x(scaled(parts[2 * k + 1]).astype(kind))
        if moving is None:
            met, beside = fence(met, beside)
            return scaled(parts[2 * k]) + met.astype(f32), beside
        came = ring_step(moving.astype(kind))
        met, came, beside = fence(met, came, beside)
        return scaled(parts[2 * k]) + came.astype(f32) + met.astype(f32), beside

    if fast:
        total, far = reduce_step(layer_grad, 1, None, bf16, embedding_far(keep, send))
        keep, far = far
        sent, sums_zero, limit_here = own_embedding(keep, far)
        far = swap(sent, "mp", mp, 2)
        total, beside = reduce_step(
            layer_grad, 2, total, bf16, (sent, far, sums_zero, limit_here)
        )
        sent, far, sums_zero, limit_here = beside
        upper, lower = all_embedding(sent, far)
        vector_part = vector_of(sums_zero, limit_here)
        vector_part = mp_sum(vector_part, mp)
        total, beside = reduce_step(
            layer_grad, 3, total, bf16, (upper, lower, vector_part)
        )
        upper, lower, vector_part = beside
        vector_part = z_sum(x_sum(vector_part, dp), dp)
        parts = parts_gradient(
            dp, code_row, place_codes, place_rows, upper, lower, grad_logits, picked_low
        )
        layer_total, beside = reduce_step(layer_grad, 0, total, bf16, (parts, vector_part))
        parts, vector_part = beside
        scale_all = power_scale(vector_part[-1, D // 2])
        inverse = 1.0 / scale_all

        layer_scale, gram_left, gram_right, shaped = shampoo_products(layer_total)
        squares = jnp.sum(layer_total * layer_total)
        total, beside = reduce_step(
            parts, 1, None, f16, (gram_left, squares, layer_scale), inverse
        )
        gram_left, squares, layer_scale = beside
        total, gram_right = reduce_step(parts, 2, total, f16, gram_right, inverse)
        total, shaped = reduce_step(parts, 3, total, f16, shaped, inverse)
        total, _ = reduce_step(parts, 0, total, f16, (), inverse)
        table_total = total[:VOC_DEV] * scale_all
        place_total = total[VOC_PAD:] * scale_all
        squares = squares + jnp.sum(table_total * table_total)
        squares = jnp.broadcast_to(squares + jnp.sum(place_total * place_total), (1, 128))

        def sided(one, two, bit):
            return jnp.where(bit == 0, jnp.stack([one, two]), jnp.stack([two, one]))

        squares = z_sum(squares, dp)
        steps = [total[VOC_PAD:].astype(f16)]
        for shift in range(1, RING):
            pairs = [(i, (i + 2 * shift) % dp) for i in range(dp)]
            steps.append(lax.ppermute(steps[0], "dp", pairs))
        squares, steps = fence(squares, steps)
        squares = x_sum(squares, dp)
        steps = jnp.stack(steps[::-1] * 2)
        steps = lax.dynamic_slice_in_dim(steps, (RING - 1 - z_here) % RING, RING, 0)
        squares, steps, near = fence(squares, steps, along_x(steps))
        squares = mp_sum(squares, mp)
        place_all = sided(steps, near, x_here).transpose(1, 0, 2, 3)
        place_all = place_all.reshape(place_rows, D)
        squares, place_all, near = fence(squares, place_all, swap(place_all, "mp", mp, 2))
        place_all = sided(place_all, near, high_bit)
        place_all = sided(place_all, swap(place_all, "mp", mp, 1), low_bit)
        place_sum = place_all.transpose(1, 0, 2, 3).reshape(LEN, D).astype(f32) * scale_all
        squares = squares[0, 0]
    else:
        layer_total = lax.psum_scatter(
            layer_grad[0].astype(f32), "dp", scatter_dimension=0, tiled=True
        )
        layer_scale, gram_left, gram_right, shaped = shampoo_products(layer_total)
        sent, sums_zero, limit_here = own_embedding(*embedding_far(keep, send))
        upper, lower = all_embedding(sent, swap(sent, "mp", mp, 2))
        vector_part = butterfly(vector_of(sums_zero, limit_here), jnp.add, dp, mp)
        table_grad, place_grad = table_gradient(
            code_row, place_codes, place_rows, upper, lower, grad_logits, picked_low
        )
        table_total = lax.psum_scatter(table_grad, "dp", scatter_dimension=0, tiled=True)[:VOC_DEV]
        place_total = lax.psum_scatter(place_grad, "dp", scatter_dimension=0, tiled=True)
        place_sum = lax.all_gather(
            lax.all_gather(place_total, "dp", axis=0, tiled=True), "mp", axis=0, tiled=True
        )
        squares = jnp.sum(layer_total * layer_total) + jnp.sum(table_total * table_total)
        squares = jnp.broadcast_to(squares + jnp.sum(place_total * place_total), (1, 128))
        squares = butterfly(squares, jnp.add, dp, mp)[0, 0]
    tail_sum, loss_sum = vector_part[:-1], vector_part[-1, 0]

    squares = squares + jnp.sum(tail_sum * tail_sum)
    grad_norm = jnp.sqrt(squares)
    count_all = rows * dp * POS
    limit = CLIP_FACTOR * math.sqrt(count_all)
    factor = jnp.minimum(1.0, limit / grad_norm)
    shrink = factor * layer_scale

    left_new = STAT_DECAY * stats_left + (1.0 - STAT_DECAY) * (shrink * shrink) * gram_left
    right_new = STAT_DECAY * stats_right + (1.0 - STAT_DECAY) * (shrink * shrink) * gram_right
    layer_new = layer_master - RATE_SHAMPOO * (shaped * shrink + DECAY_LAYER * layer_master)

    table_new, table_one, table_two = adam_step(
        table_master, table_first, table_second, table_total * factor, DECAY_TABLE
    )
    vector_sum = jnp.concatenate([place_sum, tail_sum], axis=0)
    vector_new, vector_one, vector_two = adam_step(
        vector_master, vector_first, vector_second, vector_sum * factor, 0.0
    )
    loss = loss_sum / f32(count_all)
    return (
        loss,
        grad_norm,
        layer_new,
        left_new,
        right_new,
        table_new,
        table_one,
        table_two,
        vector_new,
        vector_one,
        vector_two,
    )


def solution(mesh):
    blocks = P("mp", "dp", None, None)
    vocab = P(("dp", "mp"), None)
    rows = P("dp", None)
    return jax.shard_map(
        local,
        mesh=mesh,
        in_specs=(rows,) * 4 + (P(),) + (blocks,) * 5 + (vocab,) * 3 + (P(),) * 3,
        out_specs=(P(), P()) + (blocks,) * 3 + (vocab,) * 3 + (P(),) * 3,
        check_vma=False,
    )
```

```python
import functools
import math

import jax
import jax.numpy as jnp
from jax import lax
from jax.experimental import pallas as pl
from jax.experimental.pallas import tpu as pltpu
from jax.sharding import PartitionSpec as P

D = 1024
HEADS = 16
HD = 64
FF = 4096
VOC_DEV = 197
VOC_PAD = 208
LEN = 512
POS = 80
KB = 128
STRIP = 1664

HIGH = lax.Precision.HIGH
EPS_NORM = 1e-05
EPS_ADAM = 1e-08
BETA_FIRST = 0.5
BETA_SECOND = 0.5
RATE_ADAM = 0.01
RATE_SHAMPOO = 0.03
DECAY_TABLE = 0.01
DECAY_LAYER = 0.01
STAT_DECAY = 0.5
CLIP_FACTOR = 16.0
MASK_FILL = -1000000000.0
RING = 4
VMEM_SPARE = 60 << 20
VMEM_MOST = 60 << 20

f32 = jnp.float32
bf16 = jnp.bfloat16
f16 = jnp.float16


def swap(value, axis, ways, bit):
    pairs = [(i, i ^ bit) for i in range(ways)]
    return jax.tree.map(lambda part: lax.ppermute(part, axis, pairs), value)


def ring_step(value):
    pairs = [(i, (i + 2) % (2 * RING)) for i in range(2 * RING)]
    return lax.ppermute(value, "dp", pairs)


def after(values, *others):
    if not others:
        return values
    flat, tree = jax.tree.flatten(values)
    tied = lax.optimization_barrier(tuple(flat) + tuple(others))
    return jax.tree.unflatten(tree, tied[: len(flat)])


def along_x(value):
    return swap(value, "dp", 2 * RING, 1)


def fence(*values):
    return lax.optimization_barrier(values)


def half_float(value, bound=None):
    scale = power_scale(jnp.max(jnp.abs(value)) if bound is None else bound)
    return (value / scale).astype(f16), jnp.broadcast_to(scale, (1, 128))


def float_half(pair):
    return pair[0].astype(f32) * pair[1][0, 0]


def sum_halves(keep, send, ways):
    keep = keep + swap(send, "mp", ways, 1)
    keep = keep + swap(keep, "mp", ways, 2)
    return keep, swap(keep, "mp", ways, 1)


def mp_sum(value, mp):
    near = [swap(value, "mp", mp, bit) for bit in range(1, mp)]
    return (value + near[0]) + (near[1] + near[2])


def x_sum(value, dp):
    return value + swap(value, "dp", dp, 1)


def z_sum(value, dp):
    far = [swap(value, "dp", dp, 2 * bit) for bit in range(1, RING)]
    return (value + far[0]) + (far[1] + far[2])


def butterfly(value, combine, dp, mp, both=True):
    axes = [("mp", mp)] + ([("dp", dp)] if both else [])
    for axis, ways in axes:
        bit = 1
        while bit < ways:
            value = combine(value, swap(value, axis, ways, bit))
            bit *= 2
    return value


def gelu_exact(values):
    return 0.5 * values * (1.0 + lax.erf(values * 0.7071067811865476))


def gelu_slope(values):
    cumulative = 0.5 * (1.0 + lax.erf(values * 0.7071067811865476))
    density = jnp.exp(-0.5 * values * values) * 0.3989422804014327
    return cumulative + values * density


def norm_forward(values, norm_gain, norm_shift):
    row_mean = jnp.mean(values, axis=-1, keepdims=True)
    centered = values - row_mean
    variance = jnp.mean(centered * centered, axis=-1, keepdims=True)
    inv_dev = lax.rsqrt(variance + EPS_NORM)
    normed = centered * inv_dev
    return (normed * norm_gain + norm_shift, normed, inv_dev)


def norm_backward(grad_out, normed, inv_dev, norm_gain):
    scaled = grad_out * norm_gain
    grad_in = inv_dev * (
        scaled
        - jnp.mean(scaled, axis=-1, keepdims=True)
        - normed * jnp.mean(scaled * normed, axis=-1, keepdims=True)
    )
    return (grad_in, jnp.sum(grad_out * normed, axis=0), jnp.sum(grad_out, axis=0))


def seq_ends_of(lengths):
    return jnp.stack(
        [jnp.sum(lengths[:, : s + 1], axis=1) for s in range(lengths.shape[1])], axis=1
    )


def positions_of(lengths):
    ends = seq_ends_of(lengths)
    places = jnp.arange(LEN, dtype=jnp.int32)
    passed = places[None, :, None] >= ends[:, None, :]
    segment = jnp.sum(passed.astype(jnp.int32), axis=2)
    start = jnp.max(jnp.where(passed, ends[:, None, :], 0), axis=2)
    return (segment, places[None, :] - start)


def adam_step(master, moment_one, moment_two, gradient, weight_decay):
    new_one = BETA_FIRST * moment_one + (1.0 - BETA_FIRST) * gradient
    new_two = BETA_SECOND * moment_two + (1.0 - BETA_SECOND) * gradient * gradient
    new_master = master - RATE_ADAM * (
        new_one / (jnp.sqrt(new_two) + EPS_ADAM) + weight_decay * master
    )
    return (new_master, new_one, new_two)


def product(left_side, right_side):
    return jnp.dot(left_side, right_side, preferred_element_type=f32)


def against_rows(left_side, right_side):
    return lax.dot_general(
        left_side, right_side, (((1,), (1,)), ((), ())), preferred_element_type=f32
    )


def over_rows(left_side, right_side):
    return lax.dot_general(
        left_side, right_side, (((0,), (0,)), ((), ())), preferred_element_type=f32
    )


def hit_matrix(codes, count, kind=bf16):
    return (codes[:, None] == jnp.arange(count, dtype=jnp.int32)[None, :]).astype(kind)


def split(values, parts):
    made = []
    for _ in range(parts):
        part = lax.reduce_precision(values, 8, 7)
        made.append(part.astype(bf16))
        values = values - part
    return made


def rows_exact(hits, parts):
    upper, middle, lower = parts
    return product(hits, upper) + product(hits, middle) + product(hits, lower)


def power_scale(bound):
    safe = jnp.clip(bound, 1e-30, 1e38)
    return jnp.exp2(jnp.ceil(jnp.log2(safe)) - 14.0)


SMEM = pl.BlockSpec(memory_space=pltpu.SMEM)
VMEM = pl.BlockSpec(memory_space=pltpu.VMEM)
ANY = pl.BlockSpec(memory_space=pl.ANY)


def params(*arrays, spare=VMEM_SPARE):
    total = spare
    for one in arrays:
        *lead, rows, columns = one.shape
        size = jnp.dtype(one.dtype).itemsize
        tile = 32 // size
        total += math.prod(lead) * -(-rows // tile) * tile * -(-columns // 128) * 128 * size
    return pltpu.CompilerParams(vmem_limit_bytes=min(total, VMEM_MOST))


COST = pl.CostEstimate(flops=1, bytes_accessed=1, transcendentals=0)


def shape(dims, kind=f32):
    return jax.ShapeDtypeStruct(dims, kind)


def call(kernel, outs, scalars, arrays, name, scratch=(), spare=VMEM_SPARE):
    return pl.pallas_call(
        kernel,
        out_shape=outs,
        in_specs=[SMEM] * len(scalars) + [VMEM] * len(arrays),
        out_specs=jax.tree.map(lambda _: VMEM, outs),
        scratch_shapes=list(scratch),
        compiler_params=params(*jax.tree.leaves(outs), *arrays, *scratch, spare=spare),
        cost_estimate=COST,
        name=name,
    )(*scalars, *arrays)


def both_halves(mine, other):
    return jnp.concatenate([mine, other], axis=0)


def part_halves(value, keep, send):
    half = value.shape[0] // 2
    keep[...] = value[:half]
    send[...] = value[half:]


def strips(pieces):
    base = 0
    for piece in pieces:
        for start in range(0, piece.shape[0], STRIP):
            size = min(STRIP, piece.shape[0] - start)
            yield base + start, piece, slice(start, start + size)
        base += piece.shape[0]


def embed_kernel(codes, *refs):
    pieces, words, table = refs[:-2], refs[-2], refs[-1]
    for base, piece, rows in strips(pieces):
        table[base : base + rows.stop - rows.start, :] = piece[rows, :]
    step = 256
    for begin in range(0, words.shape[0], step):
        part = slice(begin, begin + step)
        column = lax.broadcasted_iota(jnp.int32, (step, table.shape[0]), 1)
        hits = jnp.where(codes[part, :] == column, 1.0, 0.0).astype(bf16)
        words[part, :] = product(hits, table[...]).astype(bf16)


def embed_strips_kernel(codes, piece, words, total):
    step = pl.program_id(0)

    @pl.when(step == 0)
    def _():
        total[...] = jnp.zeros_like(total)

    size = piece.shape[0]
    column = lax.broadcasted_iota(jnp.int32, (codes.shape[0], size), 1) + step * size
    hits = jnp.where(codes[...] == column, 1.0, 0.0).astype(bf16)
    total[...] += product(hits, piece[...])

    @pl.when(step == pl.num_programs(0) - 1)
    def _():
        words[...] = total[...].astype(bf16)


def embed(codes, pieces):
    tokens = codes.shape[0]
    out = shape((tokens, D), bf16)
    if len(pieces) > 1:
        vocab = sum(piece.shape[0] for piece in pieces)
        scratch = [pltpu.VMEM((vocab, D), bf16)]
        return call(embed_kernel, out, [], [codes, *pieces], "embed", scratch, VMEM_MOST)
    return pl.pallas_call(
        embed_strips_kernel,
        grid=(pieces[0].shape[0] // STRIP,),
        out_shape=out,
        in_specs=[
            pl.BlockSpec((tokens, 1), lambda r: (0, 0)),
            pl.BlockSpec((STRIP, D), lambda r: (r, 0)),
        ],
        out_specs=pl.BlockSpec((tokens, D), lambda r: (0, 0)),
        scratch_shapes=[pltpu.VMEM((tokens, D), f32)],
        compiler_params=pltpu.CompilerParams(vmem_limit_bytes=32 << 20),
        cost_estimate=COST,
        name="embed",
    )(codes, *pieces)


def normalize_kernel(flat, words, places, affine, x_low, picked, picked_low, *rest):
    x_out = rest[-1]
    step = 128
    for begin in range(0, words.shape[0], step):
        part = slice(begin, begin + step)
        out, _, _ = norm_forward(
            words[part, :].astype(f32) + places[part, :], affine[0:1, :], affine[1:2, :]
        )
        x_out[part, :] = out
        x_low[part, :] = out.astype(bf16)

    def pick_row(p, carry):
        picked[pl.ds(p, 1), :] = x_out[pl.ds(flat[p], 1), :]
        return carry

    lax.fori_loop(0, picked.shape[0], pick_row, 0, unroll=8)
    picked_low[...] = picked[...].astype(bf16)


def head_pair(values, lanes):
    zero = jnp.zeros_like(values)
    return jnp.concatenate([jnp.where(lanes, values, zero), jnp.where(lanes, zero, values)], axis=0)


def attend_kernel(groups, downs, acrosses, *refs):
    pieces, refs = refs[:groups], refs[groups:]
    (
        x_mine,
        x_other,
        picked_mine,
        picked_other,
        bias_query,
        bias_keyval,
        segment,
        pick_segment,
        joined_w,
        output_w,
        upward_w,
        downward_w,
        keyval,
        query,
        probs,
        mixed,
        keep,
        send,
        stacked,
        dense,
        x_low,
        sems,
        out_sems,
    ) = refs
    rows = segment.shape[0]
    inner = query.shape[1]
    hidden = upward_w.shape[1]
    sizes = [piece.shape[0] for piece in pieces]
    starts = [sum(sizes[:g]) for g in range(groups)]
    loads = [
        pltpu.make_async_copy(piece, stacked.at[pl.ds(start, size)], sems.at[g])
        for g, (piece, start, size) in enumerate(zip(pieces, starts, sizes))
    ]
    half = x_low.shape[0] // 2
    loads_x = [
        pltpu.make_async_copy(x_mine, x_low.at[pl.ds(0, half)], sems.at[groups]),
        pltpu.make_async_copy(x_other, x_low.at[pl.ds(half, half)], sems.at[groups + 1]),
    ]
    for load in loads + loads_x:
        load.start()
    for g, load in enumerate(loads):
        load.wait()
        for t in range(starts[g], starts[g] + sizes[g]):
            down = pl.multiple_of(downs[t], KB)
            across = pl.multiple_of(acrosses[t], KB)
            dense[pl.ds(down, KB), pl.ds(across, KB)] = stacked[t]
    start_up, start_down = 3 * inner, 3 * inner + hidden
    stores = [
        pltpu.make_async_copy(dense.at[down, across], out, out_sems.at[n])
        for n, (out, down, across) in enumerate(
            (
                (joined_w, pl.ds(0, D), pl.ds(0, start_up)),
                (output_w, pl.ds(D, inner), pl.ds(0, D)),
                (upward_w, pl.ds(0, D), pl.ds(start_up, hidden)),
                (downward_w, pl.ds(0, hidden), pl.ds(start_down, D)),
            )
        )
    ]
    for store in stores:
        store.start()
    for load in loads_x:
        load.wait()
    pairs = inner // KB
    picked_low = both_halves(picked_mine[...], picked_other[...])
    query[...] = (product(picked_low, dense[:D, :inner]) + bias_query[...]).astype(bf16)
    lanes = lax.broadcasted_iota(jnp.int32, (POS, KB), 1) < HD
    for r in range(rows):
        part = slice(r * LEN, (r + 1) * LEN)
        picks = slice(r * POS, (r + 1) * POS)
        keyval[part, :] = (
            product(x_low[part, :], dense[:D, inner:start_up]) + bias_keyval[...]
        ).astype(bf16)
        same = pick_segment[picks, :] == segment[r : r + 1, :]
        same = jnp.concatenate([same, same], axis=0)
        for pair in range(pairs):
            cut = slice(pair * KB, (pair + 1) * KB)
            cut_v = slice(inner + pair * KB, inner + (pair + 1) * KB)
            both = head_pair(query[picks, cut], lanes)
            scores = against_rows(both, keyval[part, cut]) * HD ** (-0.5)
            scores = jnp.where(same, scores, MASK_FILL)
            raised = jnp.exp(scores - jnp.max(scores, axis=-1, keepdims=True))
            part_probs = raised / jnp.sum(raised, axis=-1, keepdims=True)
            probs[r * pairs + pair] = part_probs
            out = product(part_probs.astype(bf16), keyval[part, cut_v])
            mixed[picks, cut] = jnp.where(lanes, out[:POS], out[POS:]).astype(bf16)
    part_halves(product(mixed[...], dense[D:, :D]), keep, send)
    for store in stores:
        store.wait()


def attend(corners, pieces, x_halves, picked_halves, bias_query, bias_keyval, segment, pick_segment, hidden):
    rows = segment.shape[0]
    inner = bias_query.shape[1]
    tokens, picks = 2 * x_halves[0].shape[0], 2 * picked_halves[0].shape[0]
    groups = len(pieces)
    total = sum(piece.shape[0] for piece in pieces)
    scratch = [
        pltpu.VMEM((total, KB, KB), bf16),
        pltpu.VMEM((D + inner, 3 * inner + 2 * hidden), bf16),
        pltpu.VMEM((tokens, D), bf16),
    ]
    outs = [
            shape((D, 3 * inner), bf16),
            shape((inner, D), bf16),
            shape((D, hidden), bf16),
            shape((hidden, D), bf16),
            shape((tokens, 2 * inner), bf16),
            shape((picks, inner), bf16),
            shape((rows * inner // KB, 2 * POS, LEN)),
            shape((picks, inner), bf16),
            shape((picks // 2, D)),
            shape((picks // 2, D)),
    ]
    return pl.pallas_call(
        functools.partial(attend_kernel, groups),
        out_shape=outs,
        in_specs=[SMEM] * 2 + [ANY] * (groups + 2) + [VMEM] * 6,
        out_specs=[ANY] * 4 + [VMEM] * 6,
        scratch_shapes=scratch
        + [pltpu.SemaphoreType.DMA((groups + 2,)), pltpu.SemaphoreType.DMA((4,))],
        compiler_params=params(spare=VMEM_MOST),
        cost_estimate=COST,
        name="attend",
    )(*corners, *pieces, *x_halves, *picked_halves, bias_query, bias_keyval, segment, pick_segment)


def forward_kernel(
    mine,
    other,
    picked_mine,
    picked_other,
    affine,
    bias_up,
    upward_w,
    downward_w,
    normed_out,
    inv_out,
    first,
    first_low,
    upper_pre,
    acted,
    keep,
    send,
):
    attended = both_halves(mine[...], other[...]) + affine[0:1, :]
    out, normed, inv = norm_forward(
        both_halves(picked_mine[...], picked_other[...]) + attended,
        affine[1:2, :],
        affine[2:3, :],
    )
    normed_out[...] = normed
    inv_out[...] = inv
    first[...] = out
    first_low[...] = out.astype(bf16)
    upper = product(first_low[...], upward_w[...]) + bias_up[...]
    upper_pre[...] = upper
    acted[...] = gelu_exact(upper).astype(bf16)
    part_halves(product(acted[...], downward_w[...]), keep, send)


def logits_kernel(mine, other, first, affine, target, *refs):
    pieces, refs = refs[:-6], refs[-6:]
    normed_out, inv_out, picked_low, top_feature, logits, stats = refs
    branch = both_halves(mine[...], other[...]) + affine[0:1, :]
    out, normed, inv = norm_forward(first[...] + branch, affine[1:2, :], affine[2:3, :])
    normed_out[...] = normed
    inv_out[...] = inv
    picked_low[...] = out.astype(bf16)
    top_feature[...] = jnp.broadcast_to(jnp.max(jnp.abs(out)), top_feature.shape)
    count = out.shape[0]
    top = jnp.full((1, count), -jnp.inf, f32)
    chosen = jnp.zeros((1, count), f32)
    for base, piece, rows in strips(pieces):
        size = rows.stop - rows.start
        part = against_rows(piece[rows, :], picked_low[...])
        row = lax.broadcasted_iota(jnp.int32, (size, count), 0) + base
        part = jnp.where(row % VOC_PAD < VOC_DEV, part, -jnp.inf)
        logits[base : base + size, :] = part
        top = jnp.maximum(top, jnp.max(part, axis=0, keepdims=True))
        hit = jnp.where(row == target[...], part, 0.0)
        chosen = chosen + jnp.sum(hit, axis=0, keepdims=True)
    total = jnp.zeros((1, count), f32)
    for base, piece, rows in strips(pieces):
        part = logits[base : base + rows.stop - rows.start, :]
        total = total + jnp.sum(jnp.exp(part - top), axis=0, keepdims=True)
    stats[0:1, :] = top
    stats[1:2, :] = total
    stats[2:3, :] = chosen
    stats[3:8, :] = jnp.zeros((5, count), f32)


def head_kernel(own, near, far, across, target, logits, *refs):
    pieces, refs = refs[:-4], refs[-4:]
    grad_logits, loss, keep, send = refs
    count = target.shape[1]
    middle = count // 2

    def turned(one):
        return jnp.concatenate([one[:, middle:], one[:, :middle]], axis=1)

    everyone = (own[...], turned(near[...]), far[...], turned(across[...]))
    top = functools.reduce(jnp.maximum, [one[0:1, :] for one in everyone])
    parts = [one[1:2, :] * jnp.exp(one[0:1, :] - top) for one in everyone]
    total = (parts[0] + parts[1]) + (parts[2] + parts[3])
    chosen = [one[2:3, :] for one in everyone]
    chosen = (chosen[0] + chosen[1]) + (chosen[2] + chosen[3])
    losses = jnp.sum(jnp.log(total) + top - chosen, axis=1, keepdims=True)
    loss[...] = jnp.broadcast_to(losses, loss.shape)
    back = jnp.zeros((count, D), f32)
    for base, piece, rows in strips(pieces):
        size = rows.stop - rows.start
        row = lax.broadcasted_iota(jnp.int32, (size, count), 0) + base
        hit = jnp.where(row == target[...], 1.0, 0.0)
        part = logits[base : base + size, :]
        part = (jnp.exp(part - top) / total - hit).astype(bf16)
        grad_logits[base : base + size, :] = part
        back = back + over_rows(part, piece[rows, :])
    part_halves(back, keep, send)


def backward_kernel(
    mine,
    other,
    normed,
    inv,
    gain,
    upper_pre,
    upward_w,
    downward_w,
    grad_pre2,
    branch_grad,
    upper_grad,
    row_sums,
    upper_sums,
    keep,
    send,
):
    grad_out = both_halves(mine[...], other[...])
    grad_in, gain_sum, shift_sum = norm_backward(grad_out, normed[...], inv[...], gain[...])
    grad_pre2[...] = grad_in
    branch_grad[...] = grad_in.astype(bf16)
    row_sums[0:1, :] = gain_sum[None]
    row_sums[1:2, :] = shift_sum[None]
    row_sums[2:3, :] = jnp.sum(branch_grad[...].astype(f32), axis=0, keepdims=True)
    upper = against_rows(branch_grad[...], downward_w[...]) * gelu_slope(upper_pre[...])
    upper_grad[...] = upper.astype(bf16)
    upper_sums[...] = jnp.sum(upper_grad[...].astype(f32), axis=0, keepdims=True)
    part_halves(against_rows(upper_grad[...], upward_w[...]), keep, send)


def back_attention_kernel(
    positions,
    rank_first,
    mine,
    other,
    grad_pre2,
    first_normed,
    first_inv,
    gain,
    joined_w,
    output_w,
    keyval,
    query,
    probs,
    keep,
    send,
    row_sums,
    query_sums,
    keyval_sums,
    attended_grad,
    query_grad,
    keyval_grad,
    pick_grad,
):
    picks, inner = query.shape
    rows = picks // POS
    pairs = inner // KB
    scale = HD ** (-0.5)
    grad_out = both_halves(mine[...], other[...]) + grad_pre2[...]
    grad_pre1, gain_sum, shift_sum = norm_backward(
        grad_out, first_normed[...], first_inv[...], gain[...]
    )
    attended_grad[...] = grad_pre1.astype(bf16)
    row_sums[0:1, :] = gain_sum[None]
    row_sums[1:2, :] = shift_sum[None]
    row_sums[2:3, :] = jnp.sum(attended_grad[...].astype(f32), axis=0, keepdims=True)
    mixed_grad = against_rows(attended_grad[...], output_w[...]).astype(bf16)
    lanes = lax.broadcasted_iota(jnp.int32, (POS, KB), 1) < HD
    for r in range(rows):
        part = slice(r * LEN, (r + 1) * LEN)
        here = slice(r * POS, (r + 1) * POS)
        for pair in range(pairs):
            cut = slice(pair * KB, (pair + 1) * KB)
            cut_v = slice(inner + pair * KB, inner + (pair + 1) * KB)
            part_probs = probs[r * pairs + pair]
            out_grad = head_pair(mixed_grad[here, cut], lanes)
            both = head_pair(query[here, cut], lanes)
            probs_grad = against_rows(out_grad, keyval[part, cut_v])
            inner_sum = jnp.sum(probs_grad * part_probs, axis=-1, keepdims=True)
            scores_grad = (part_probs * (probs_grad - inner_sum)).astype(bf16)
            back = product(scores_grad, keyval[part, cut])
            query_grad[here, cut] = (jnp.where(lanes, back[:POS], back[POS:]) * scale).astype(bf16)
            keyval_grad[part, cut] = (over_rows(scores_grad, both) * scale).astype(bf16)
            keyval_grad[part, cut_v] = over_rows(part_probs.astype(bf16), out_grad).astype(bf16)
    query_sums[...] = jnp.sum(query_grad[...].astype(f32), axis=0, keepdims=True)
    keyval_sums[...] = jnp.sum(keyval_grad[...].astype(f32), axis=0, keepdims=True)
    pick_grad[...] = (
        against_rows(query_grad[...], joined_w[:, :inner]) + grad_pre1 * rank_first[0]
    )
    for row, out in ((1, send), (0, keep)):
        out[...] = against_rows(keyval_grad[row * LEN : (row + 1) * LEN, :], joined_w[:, inner:])

        def add_row(p, carry):
            spot = positions[row * POS + p]
            out[pl.ds(spot, 1), :] += pick_grad[pl.ds(row * POS + p, 1), :]
            return carry

        lax.fori_loop(0, POS, add_row, 0, unroll=8)


def back_weights_kernel(
    downs,
    acrosses,
    x_mine,
    x_other,
    keyval_grad,
    picked_mine,
    picked_other,
    query_grad,
    mixed,
    attended_grad,
    acted,
    branch_grad,
    first_low,
    upper_grad,
    *rest,
):
    packed, dense = rest[:-1], rest[-1]
    inner = query_grad.shape[1]
    low = dense.dtype
    picked_low = both_halves(picked_mine[...], picked_other[...])
    dense[:D, :inner] = over_rows(picked_low, query_grad[...]).astype(low)
    half = x_mine.shape[0]
    joined = over_rows(x_mine[...], keyval_grad[:half, :])
    joined = joined + over_rows(x_other[...], keyval_grad[half:, :])
    dense[:D, inner : 3 * inner] = joined.astype(low)
    start_up, start_down = 3 * inner, 3 * inner + upper_grad.shape[1]
    dense[:D, start_up:start_down] = over_rows(first_low[...], upper_grad[...]).astype(low)
    dense[:D, start_down:] = over_rows(acted[...], branch_grad[...]).astype(low)
    dense[D:, :D] = over_rows(mixed[...], attended_grad[...]).astype(low)
    spot = 0
    for out in packed:
        for t in range(out.shape[0]):
            down = pl.multiple_of(downs[spot], KB)
            across = pl.multiple_of(acrosses[spot], KB)
            out[t] = dense[pl.ds(down, KB), pl.ds(across, KB)]
            spot += 1


def tile_corners(natural, inner, hidden):
    count_joined, count_output = D // KB * 3 * inner // KB, inner // KB * D // KB
    count_up = D // KB * hidden // KB
    n_joined = natural
    n_output = natural - count_joined
    n_up = n_output - count_output
    n_down = n_up - count_up
    wide_joined, wide, wide_up = 3 * inner // KB, D // KB, hidden // KB
    down = jnp.where(
        n_output < 0,
        n_joined // wide_joined * KB,
        jnp.where(
            n_up < 0,
            D + n_output // wide * KB,
            jnp.where(n_down < 0, n_up // wide_up * KB, n_down // wide * KB),
        ),
    )
    across = jnp.where(
        n_output < 0,
        n_joined % wide_joined * KB,
        jnp.where(
            n_up < 0,
            n_output % wide * KB,
            jnp.where(
                n_down < 0,
                3 * inner + n_up % wide_up * KB,
                3 * inner + hidden + n_down % wide * KB,
            ),
        ),
    )
    return down, across


def embedding_kernel(keep, came, words, places, gain, grad, sums, top):
    _, normed, inv = norm_forward(words[...].astype(f32) + places[...], gain[...], gain[...])
    grad_in, gain_sum, shift_sum = norm_backward(
        keep[...] + came[...], normed, inv, gain[...]
    )
    grad[...] = grad_in
    sums[0:1, :] = gain_sum[None]
    sums[1:2, :] = shift_sum[None]
    top[...] = jnp.broadcast_to(jnp.max(jnp.abs(grad_in)), top.shape)


def table_kernel(
    codes, place_codes, upper, lower, grad_logits, picked_low, grad, place_grad, hits
):
    rows, place_rows = grad.shape[0], place_grad.shape[0]

    @pl.when(pl.program_id(1) == 0)
    def _():
        row = lax.broadcasted_iota(jnp.int32, (rows, hits.shape[1]), 0)
        row = row + pl.program_id(0) * rows
        hits[:rows, :] = jnp.where(row == codes[...], 1.0, 0.0).astype(bf16)
        row = lax.broadcasted_iota(jnp.int32, (place_rows, hits.shape[1]), 0)
        hits[rows:, :] = jnp.where(row == place_codes[...], 1.0, 0.0).astype(bf16)

    total = product(hits[...], upper[...]) + product(hits[...], lower[...])
    grad[...] = total[:rows] + product(grad_logits[...], picked_low[...])
    place_grad[...] = total[rows:]


def parts_kernel(codes, place_codes, *refs):
    *quarters, grad_logits, picked_low, grad, hits = refs
    parts, each, _ = grad.shape
    vocab = grad_logits.shape[0]
    place_rows = hits.shape[0] - vocab
    own = place_rows // parts

    @pl.when(pl.program_id(0) == 0)
    def _():
        row = lax.broadcasted_iota(jnp.int32, (vocab, hits.shape[1]), 0)
        hits[:vocab, :] = jnp.where(row == codes[...], 1.0, 0.0).astype(bf16)
        row = lax.broadcasted_iota(jnp.int32, (place_rows, hits.shape[1]), 0)
        hits[vocab:, :] = jnp.where(row == place_codes[...], 1.0, 0.0).astype(bf16)

    values = jnp.concatenate([quarter[...] for quarter in quarters], axis=0)
    upper = values.astype(bf16)
    lower = (values - upper.astype(f32)).astype(bf16)
    total = product(hits[...], upper) + product(hits[...], lower)
    words = total[:vocab] + product(grad_logits[...], picked_low[...])
    for r in range(parts):
        grad[r, :VOC_PAD, :] = words[r * VOC_PAD : (r + 1) * VOC_PAD]
        grad[r, VOC_PAD:each, :] = total[vocab + r * own : vocab + (r + 1) * own]


def parts_gradient(parts, codes, place_codes, place_rows, quarters, grad_logits, picked_low):
    vocab, picks = grad_logits.shape
    tokens = codes.shape[1]
    wide = 256
    each = (vocab + place_rows) // parts

    def columns(high):
        return pl.BlockSpec((high, wide), lambda c: (0, c))

    row_of_codes = pl.BlockSpec((1, tokens), lambda c: (0, 0))
    return pl.pallas_call(
        parts_kernel,
        grid=(D // wide,),
        out_shape=shape((parts, each, D)),
        in_specs=[
            row_of_codes,
            row_of_codes,
            *[columns(quarter.shape[0]) for quarter in quarters],
            pl.BlockSpec((vocab, picks), lambda c: (0, 0)),
            columns(picks),
        ],
        out_specs=pl.BlockSpec((parts, each, wide), lambda c: (0, 0, c)),
        scratch_shapes=[pltpu.VMEM((vocab + place_rows, tokens), bf16)],
        compiler_params=pltpu.CompilerParams(vmem_limit_bytes=36 << 20),
        cost_estimate=COST,
        name="table_gradient",
    )(codes, place_codes, *quarters, grad_logits, picked_low)


def table_gradient(codes, place_codes, place_rows, upper, lower, grad_logits, picked_low):
    vocab, picks = grad_logits.shape
    tokens = upper.shape[0]
    wide = 256

    def columns(high):
        return pl.BlockSpec((high, wide), lambda r, c: (0, c))

    row_of_codes = pl.BlockSpec((1, tokens), lambda r, c: (0, 0))
    return pl.pallas_call(
        table_kernel,
        grid=(vocab // STRIP, D // wide),
        out_shape=[shape((vocab, D)), shape((place_rows, D))],
        in_specs=[
            row_of_codes,
            row_of_codes,
            columns(tokens),
            columns(tokens),
            pl.BlockSpec((STRIP, picks), lambda r, c: (r, 0)),
            columns(picks),
        ],
        out_specs=[pl.BlockSpec((STRIP, wide), lambda r, c: (r, c)), columns(place_rows)],
        scratch_shapes=[pltpu.VMEM((STRIP + place_rows, tokens), bf16)],
        compiler_params=pltpu.CompilerParams(vmem_limit_bytes=32 << 20),
        cost_estimate=COST,
        name="table_gradient",
    )(codes, place_codes, upper, lower, grad_logits, picked_low)


def local(
    input_ids,
    seq_lengths,
    loss_positions,
    targets,
    block_owner,
    layer_master,
    stats_left,
    stats_right,
    root_left,
    root_right,
    table_master,
    table_first,
    table_second,
    vector_master,
    vector_first,
    vector_second,
):
    mp = lax.axis_size("mp")
    dp = lax.axis_size("dp")
    fast = dp == 2 * RING
    model_rank = lax.axis_index("mp")
    data_rank = lax.axis_index("dp")
    inner = D // mp
    ff_rows = FF // D
    hidden = FF // mp
    rows = input_ids.shape[0]
    tokens = rows * LEN
    share = tokens // mp
    own_blocks = layer_master.shape[1]
    blocks = own_blocks * dp

    if fast:
        z_here, x_here = data_rank // 2, data_rank % 2

        def place_of(owner):
            return 2 * ((z_here - owner // 2) % RING) + (owner % 2 + x_here) % 2
    else:

        def place_of(owner):
            return owner

    low_bit, high_bit = model_rank % 2, model_rank // 2

    def turned(array):
        return jnp.where(low_bit == 0, array, array[::-1])

    input_ids, seq_lengths = turned(input_ids), turned(seq_lengths)
    loss_positions, targets = turned(loss_positions), turned(targets)
    rank_first = (model_rank == 0).astype(f32)
    tail = vector_master[LEN:]
    bias_query = lax.dynamic_slice_in_dim(tail[2], model_rank * inner, inner)[None]
    bias_value = lax.dynamic_slice_in_dim(tail[3], model_rank * inner, inner)
    bias_keyval = jnp.concatenate([jnp.zeros((inner,), f32), bias_value])[None]
    bias_up = lax.dynamic_slice_in_dim(tail[7 : 7 + ff_rows].reshape(FF), model_rank * hidden, hidden)[None]
    affine_zero, affine_one = tail[0:2], tail[4:7]
    affine_two = tail[7 + ff_rows : 10 + ff_rows]

    segment, offset = positions_of(seq_lengths)
    pick_segment = jnp.sum(
        (seq_ends_of(seq_lengths)[:, None, :] <= loss_positions[:, :, None]).astype(jnp.int32), axis=2
    ).reshape(-1, 1)

    def codes_of(ids):
        part = ids // VOC_DEV
        code = place_of(part // mp) * VOC_PAD + ids % VOC_DEV
        return jnp.where(part % mp == model_rank, code, -1)

    codes = codes_of(input_ids.reshape(-1))
    target_codes = codes_of(targets.reshape(1, -1))

    def corners_of():
        number = jnp.arange(blocks, dtype=jnp.int32)
        if fast:
            part = number // own_blocks
            owner = 2 * ((z_here - part // 2) % RING) + (part % 2 + x_here) % 2
            taken = owner * own_blocks + number % own_blocks
            order = jnp.sum(
                jnp.where(taken[:, None] == number[None, :], block_owner[None, :], 0), axis=1
            )
        else:
            order = block_owner
        return tile_corners(order, inner, hidden)

    table_low = jnp.pad(table_master.astype(bf16), ((0, VOC_PAD - VOC_DEV), (0, 0)))
    layer_low = layer_master[0].astype(bf16)
    vocab = dp * VOC_PAD
    words_half = tokens // 2
    def places_of(row, parts):
        return rows_exact(hit_matrix(offset[row], LEN), parts)

    def own_of(words):
        return [
            lax.dynamic_slice_in_dim(value, high_bit * share, share, 0)
            for value in (words, places[0])
        ]

    def normalize(row, words):
        return call(
            normalize_kernel,
            [
                shape((words_half, D), bf16),
                shape((POS, D)),
                shape((POS, D), bf16),
            ],
            [row_positions[row]],
            [words, places[row], affine_zero],
            "normalize",
            [pltpu.VMEM((words_half, D), f32)],
        )

    send_codes, keep_codes = codes[words_half:, None], codes[:words_half, None]
    place_rows = LEN // mp
    per_owner = place_rows // dp
    place_codes = offset.reshape(1, -1) - model_rank * place_rows
    place_codes = jnp.where(
        (place_codes >= 0) & (place_codes < place_rows),
        place_of(place_codes // per_owner) * per_owner + place_codes % per_owner,
        -1,
    )
    def by_quarters(codes):
        codes = codes.reshape(rows, mp // 2, share)
        return jnp.where(high_bit == 0, codes, codes[:, ::-1]).reshape(1, -1)

    small = (
        affine_zero,
        affine_one,
        affine_two,
        affine_zero[0:1],
        affine_one[1:2],
        affine_two[1:2],
        bias_query,
        bias_keyval,
        bias_up,
        [loss_positions[row] for row in range(rows)],
        loss_positions.reshape(-1),
        rank_first.reshape(1),
        corners_of(),
        segment,
        pick_segment,
        by_quarters(codes),
        target_codes,
        by_quarters(place_codes),
        send_codes,
        keep_codes,
    )
    if fast:
        place_parts = split(vector_master[:LEN], 3)
        moved, met, place_parts, layer_low = fence(
            ring_step(table_low), along_x(table_low), place_parts, layer_low
        )
        held, crossed = [table_low, moved], [met]
        places = [places_of(row, place_parts) for row in range(rows)]
        moved, met, places = fence(ring_step(held[1]), along_x(held[1]), places)
        held.append(moved)
        crossed.append(met)
        moved, met, small = fence(ring_step(held[2]), along_x(held[2]), small)
        held.append(moved)
        crossed.append(met)
    (
        affine_zero,
        affine_one,
        affine_two,
        gain_zero,
        gain_one,
        gain_two,
        bias_query,
        bias_keyval,
        bias_up,
        row_positions,
        all_positions,
        rank_one,
        corners,
        segment,
        pick_segment,
        code_row,
        target_codes,
        place_codes,
        send_codes,
        keep_codes,
    ) = small
    if fast:
        cut = 96
        moved, met, *last = fence(
            ring_step(layer_low),
            along_x(layer_low),
            along_x(held[RING - 1][:cut]),
            ring_step(crossed[RING - 2][cut:]),
        )
        table_parts = [piece for pair in zip(held, crossed) for piece in pair]
        table_parts += [held[RING - 1], *last]
        held, crossed = [layer_low, moved], [met]
        send = embed(send_codes, table_parts)
        near = swap(send, "mp", mp, 1)
        keep = embed(keep_codes, table_parts) + near
        moved, met, keep = fence(ring_step(held[1]), along_x(held[1]), keep)
        held.append(moved)
        crossed.append(met)
        far = swap(keep, "mp", mp, 2)
        moved, met, keep, far = fence(ring_step(held[2]), along_x(held[2]), keep, far)
        held.append(moved)
        crossed.append(met)
        words = keep + far
        near = swap(words, "mp", mp, 1)
        x_mine, x_other = normalize(0, words), normalize(1, near)
        own_words, own_places = own_of(words)
        cut = own_blocks // 2
        *last, x_mine, x_other, own_words, own_places = fence(
            along_x(held[3][:cut]),
            ring_step(crossed[2][cut:]),
            x_mine,
            x_other,
            own_words,
            own_places,
        )
        layer_parts = [piece for pair in zip(held, crossed) for piece in pair]
        layer_parts += [held[3], *last]
    else:
        place_parts = split(vector_master[:LEN], 3)
        places = [places_of(row, place_parts) for row in range(rows)]
        table_parts = [lax.all_gather(table_low, "dp", axis=0, tiled=True)]
        layer_parts = [lax.all_gather(layer_low, "dp", axis=0, tiled=True)]
        keep, send = embed(keep_codes, table_parts), embed(send_codes, table_parts)
        words, near = sum_halves(keep, send, mp)
        x_mine, x_other = normalize(0, words), normalize(1, near)
        own_words, own_places = own_of(words)

    (
        joined_w,
        output_w,
        upward_w,
        downward_w,
        keyval,
        queries,
        probs,
        mixed_low,
        keep,
        send,
    ) = attend(
        corners,
        layer_parts,
        [x_mine[0], x_other[0]],
        [x_mine[2], x_other[2]],
        bias_query,
        bias_keyval,
        segment,
        pick_segment,
        hidden,
    )
    count = rows * POS
    half_shapes = [shape((count // 2, D)), shape((count // 2, D))]
    row_shape, low_shape = shape((count, D)), shape((count, D), bf16)
    first_normed, first_inv, first_out, first_low, upper_pre, acted_low, keep, send = call(
        forward_kernel,
        [
            row_shape,
            shape((count, 1)),
            row_shape,
            low_shape,
            shape((count, hidden)),
            shape((count, hidden), bf16),
            *half_shapes,
        ],
        [],
        [*sum_halves(keep, send, mp), x_mine[1], x_other[1], affine_one, bias_up, upward_w, downward_w],
        "forward",
        spare=8 << 20,
    )

    second_normed, second_inv, picked_low, top_feature, logits, stats = call(
        logits_kernel,
        [
            row_shape,
            shape((count, 1)),
            low_shape,
            shape((1, 128)),
            shape((vocab, count)),
            shape((8, count)),
        ],
        [],
        [*sum_halves(keep, send, mp), first_out, affine_two, target_codes, *table_parts],
        "logits",
        spare=8 << 20,
    )
    everyone = [stats] + [swap(stats, "mp", mp, bit) for bit in range(1, mp)]
    grad_logits, loss_part, keep, send = call(
        head_kernel,
        [shape((vocab, count), bf16), shape((1, 128)), *half_shapes],
        [],
        [*everyone, target_codes, logits, *table_parts],
        "head",
        spare=8 << 20,
    )

    grad_pre2, branch_grad, upper_grad, sums_two, upper_sums, keep, send = call(
        backward_kernel,
        [
            row_shape,
            low_shape,
            shape((count, hidden), bf16),
            shape((3, D)),
            shape((1, hidden)),
            *half_shapes,
        ],
        [],
        [
            *sum_halves(keep, send, mp),
            second_normed,
            second_inv,
            gain_two,
            upper_pre,
            upward_w,
            downward_w,
        ],
        "backward",
        spare=8 << 20,
    )
    keep, send, sums_one, query_sums, keyval_sums, attended_grad, query_grad, keyval_grad = call(
        back_attention_kernel,
        [
            shape((tokens // 2, D)),
            shape((tokens // 2, D)),
            shape((3, D)),
            shape((1, inner)),
            shape((1, 2 * inner)),
            low_shape,
            shape((count, inner), bf16),
            shape((tokens, 2 * inner), bf16),
        ],
        [all_positions, rank_one],
        [
            *sum_halves(keep, send, mp),
            grad_pre2,
            first_normed,
            first_inv,
            gain_one,
            joined_w,
            output_w,
            keyval,
            queries,
            probs,
        ],
        "back_attention",
        [pltpu.VMEM((count, D), f32)],
        10 << 20,
    )
    groups = dp if fast else 1
    layer_grad = call(
        back_weights_kernel,
        [shape((blocks // groups, KB, KB), bf16)] * groups,
        corners,
        [
            x_mine[0],
            x_other[0],
            keyval_grad,
            x_mine[2],
            x_other[2],
            query_grad,
            mixed_low,
            attended_grad,
            acted_low,
            branch_grad,
            first_low,
            upper_grad,
        ],
        "back_weights",
        [pltpu.VMEM((D + inner, 3 * inner + 2 * hidden), bf16)],
        VMEM_MOST,
    )

    def quarters_of(value):
        return (
            lax.dynamic_slice_in_dim(value, high_bit * share, share, 0),
            lax.dynamic_slice_in_dim(value, (1 - high_bit) * share, share, 0),
        )

    def embedding(keep, came):
        return call(
            embedding_kernel,
            [shape((share, D)), shape((2, D)), shape((1, 128))],
            [],
            [keep, came, own_words, own_places, gain_zero],
            "embedding",
            spare=8 << 20,
        )

    def embedding_far(keep, send):
        keep, send = quarters_of(keep + swap(send, "mp", mp, 1))
        return keep, swap(half_float(send), "mp", mp, 2)

    def own_embedding(keep, far):
        grad, sums, limit = embedding(keep, float_half(far))
        return half_float(grad, limit[0, 0]), sums, limit

    def all_embedding(sent, far, near):
        return [float_half(pair) for pair in (sent, far, *near)]

    def vector_of(sums_zero, limit):
        def spread(part, width, start):
            return lax.dynamic_update_slice_in_dim(jnp.zeros((1, width), f32), part, start, 1)

        bound = share * limit[:, :1] + rank_first * count * top_feature[:, :1]
        return jnp.concatenate(
            [
                sums_zero,
                spread(query_sums, D, model_rank * inner),
                spread(keyval_sums[:, inner:], D, model_rank * inner),
                sums_one[2:3] * rank_first,
                sums_one[0:2] * rank_first,
                spread(upper_sums, FF, model_rank * hidden).reshape(ff_rows, D),
                sums_two[2:3] * rank_first,
                sums_two[0:2] * rank_first,
                jnp.concatenate(
                    [
                        jnp.broadcast_to(loss_part[:, :1] * rank_first, (1, D // 2)),
                        jnp.broadcast_to(bound, (1, D // 2)),
                    ],
                    axis=1,
                ),
            ],
            axis=0,
        )

    def shampoo_products(total):
        scale = power_scale(jnp.max(jnp.abs(total)))
        gradient = total[None] / scale
        return (
            scale,
            jnp.einsum("...ij,...kj->...ik", gradient, gradient, precision=HIGH),
            jnp.einsum("...ji,...jk->...ik", gradient, gradient, precision=HIGH),
            jnp.einsum(
                "...ij,...jk->...ik",
                jnp.einsum("...ij,...jk->...ik", root_left, gradient, precision=HIGH),
                root_right,
                precision=HIGH,
            ),
        )

    def reduce_step(parts, k, moving, kind, beside):
        met = along_x(parts[2 * k + 1].astype(kind))
        if moving is None:
            met, beside = fence(met, beside)
            return parts[2 * k].astype(f32) + met.astype(f32), beside
        came = ring_step(moving.astype(kind))
        met, came, beside = fence(met, came, beside)
        return parts[2 * k].astype(f32) + came.astype(f32) + met.astype(f32), beside

    if fast:
        total, far = reduce_step(layer_grad, 1, None, bf16, embedding_far(keep, send))
        keep, far = far
        sent, sums_zero, limit_here = own_embedding(keep, far)
        far = swap(sent, "mp", mp, 2)
        total, beside = reduce_step(
            layer_grad, 2, total, bf16, (sent, far, sums_zero, limit_here)
        )
        sent, far, sums_zero, limit_here = beside
        near = swap((sent, far), "mp", mp, 1)
        vector_part = mp_sum(vector_of(sums_zero, limit_here), mp)
        total, beside = reduce_step(
            layer_grad, 3, total, bf16, (sent, far, near, vector_part)
        )
        *embed_parts, vector_part = beside
        vector_part = z_sum(x_sum(vector_part, dp), dp)
        parts = parts_gradient(
            dp,
            code_row,
            place_codes,
            place_rows,
            all_embedding(*embed_parts),
            grad_logits,
            picked_low,
        )
        layer_total, beside = reduce_step(layer_grad, 0, total, bf16, (parts, vector_part))
        parts, vector_part = beside
        scale_all = power_scale(vector_part[-1, D // 2])
        inverse = 1.0 / scale_all

        def leaving(k):
            return (parts[2 * k + 1] * inverse).astype(f16)

        met, ready, parts, layer_total = fence(
            along_x(leaving(1)), leaving(2), parts, layer_total
        )
        total = parts[2] * inverse + met.astype(f32)
        layer_scale, gram_left, gram_right, shaped = shampoo_products(layer_total)
        squares = jnp.sum(layer_total * layer_total)
        met, came, ready, parts, squares, layer_scale, gram_left = fence(
            along_x(ready),
            ring_step(total.astype(f16)),
            leaving(3),
            parts,
            squares,
            layer_scale,
            gram_left,
        )
        total = parts[4] * inverse + came.astype(f32) + met.astype(f32)
        met, came, ready, parts, gram_right = fence(
            along_x(ready), ring_step(total.astype(f16)), leaving(0), parts, gram_right
        )
        total = parts[6] * inverse + came.astype(f32) + met.astype(f32)
        met, came, parts, shaped = fence(
            along_x(ready), ring_step(total.astype(f16)), parts, shaped
        )
        total = parts[0] * inverse + came.astype(f32) + met.astype(f32)
        table_total = total[:VOC_DEV] * scale_all
        place_total = total[VOC_PAD:] * scale_all
        squares = squares + jnp.sum(table_total * table_total)
        squares = jnp.broadcast_to(squares + jnp.sum(place_total * place_total), (1, 128))

        def sided(one, two, bit):
            return jnp.where(bit == 0, jnp.stack([one, two]), jnp.stack([two, one]))

        squares = z_sum(squares, dp)
        steps = [total[VOC_PAD:].astype(f16)]
        for shift in range(1, RING):
            pairs = [(i, (i + 2 * shift) % dp) for i in range(dp)]
            steps.append(lax.ppermute(steps[0], "dp", pairs))
        squares, steps = fence(squares, steps)
        squares = x_sum(squares, dp)
        steps = jnp.stack(steps[::-1] * 2)
        steps = lax.dynamic_slice_in_dim(steps, (RING - 1 - z_here) % RING, RING, 0)
        squares, steps, near = fence(squares, steps, along_x(steps))
        squares = mp_sum(squares, mp)
        place_all = sided(steps, near, x_here).transpose(1, 0, 2, 3)
        place_all = place_all.reshape(place_rows, D)
        place_all = sided(place_all, swap(place_all, "mp", mp, 2), high_bit)
        place_all = sided(place_all, swap(place_all, "mp", mp, 1), low_bit)
        place_sum = place_all.transpose(1, 0, 2, 3).reshape(LEN, D).astype(f32) * scale_all
        squares = squares[0, 0]
    else:
        layer_total = lax.psum_scatter(
            layer_grad[0].astype(f32), "dp", scatter_dimension=0, tiled=True
        )
        layer_scale, gram_left, gram_right, shaped = shampoo_products(layer_total)
        sent, sums_zero, limit_here = own_embedding(*embedding_far(keep, send))
        far = swap(sent, "mp", mp, 2)
        embed_parts = all_embedding(sent, far, swap((sent, far), "mp", mp, 1))
        upper, lower = split(jnp.concatenate(embed_parts, axis=0), 2)
        vector_part = butterfly(vector_of(sums_zero, limit_here), jnp.add, dp, mp)
        table_grad, place_grad = table_gradient(
            code_row, place_codes, place_rows, upper, lower, grad_logits, picked_low
        )
        table_total = lax.psum_scatter(table_grad, "dp", scatter_dimension=0, tiled=True)[:VOC_DEV]
        place_total = lax.psum_scatter(place_grad, "dp", scatter_dimension=0, tiled=True)
        place_sum = lax.all_gather(
            lax.all_gather(place_total, "dp", axis=0, tiled=True), "mp", axis=0, tiled=True
        )
        squares = jnp.sum(layer_total * layer_total) + jnp.sum(table_total * table_total)
        squares = jnp.broadcast_to(squares + jnp.sum(place_total * place_total), (1, 128))
        squares = butterfly(squares, jnp.add, dp, mp)[0, 0]
    tail_sum, loss_sum = vector_part[:-1], vector_part[-1, 0]

    squares = squares + jnp.sum(tail_sum * tail_sum)
    grad_norm = jnp.sqrt(squares)
    count_all = rows * dp * POS
    limit = CLIP_FACTOR * math.sqrt(count_all)
    factor = jnp.minimum(1.0, limit / grad_norm)
    shrink = factor * layer_scale

    left_new = STAT_DECAY * stats_left + (1.0 - STAT_DECAY) * (shrink * shrink) * gram_left
    right_new = STAT_DECAY * stats_right + (1.0 - STAT_DECAY) * (shrink * shrink) * gram_right
    layer_new = layer_master - RATE_SHAMPOO * (shaped * shrink + DECAY_LAYER * layer_master)

    table_new, table_one, table_two = adam_step(
        table_master, table_first, table_second, table_total * factor, DECAY_TABLE
    )
    vector_sum = jnp.concatenate([place_sum, tail_sum], axis=0)
    vector_new, vector_one, vector_two = adam_step(
        vector_master, vector_first, vector_second, vector_sum * factor, 0.0
    )
    loss = loss_sum / f32(count_all)
    return (
        loss,
        grad_norm,
        layer_new,
        left_new,
        right_new,
        table_new,
        table_one,
        table_two,
        vector_new,
        vector_one,
        vector_two,
    )


def solution(mesh):
    blocks = P("mp", "dp", None, None)
    vocab = P(("dp", "mp"), None)
    rows = P("dp", None)
    return jax.shard_map(
        local,
        mesh=mesh,
        in_specs=(rows,) * 4 + (P(),) + (blocks,) * 5 + (vocab,) * 3 + (P(),) * 3,
        out_specs=(P(), P()) + (blocks,) * 3 + (vocab,) * 3 + (P(),) * 3,
        check_vma=False,
    )
```

```python
import functools
import math

import jax
import jax.numpy as jnp
from jax import lax
from jax.experimental import pallas as pl
from jax.experimental.pallas import tpu as pltpu
from jax.sharding import PartitionSpec as P

D = 1024
HEADS = 16
HD = 64
FF = 4096
VOC_DEV = 197
VOC_PAD = 208
LEN = 512
POS = 80
KB = 128
STRIP = 1664

HIGH = lax.Precision.HIGH
EPS_NORM = 1e-05
EPS_ADAM = 1e-08
BETA_FIRST = 0.5
BETA_SECOND = 0.5
RATE_ADAM = 0.01
RATE_SHAMPOO = 0.03
DECAY_TABLE = 0.01
DECAY_LAYER = 0.01
STAT_DECAY = 0.5
CLIP_FACTOR = 16.0
MASK_FILL = -1000000000.0
RING = 4
VMEM_SPARE = 60 << 20
VMEM_MOST = 60 << 20

f32 = jnp.float32
bf16 = jnp.bfloat16
f16 = jnp.float16


def swap(value, axis, ways, bit):
    pairs = [(i, i ^ bit) for i in range(ways)]
    return jax.tree.map(lambda part: lax.ppermute(part, axis, pairs), value)


def ring_step(value):
    pairs = [(i, (i + 2) % (2 * RING)) for i in range(2 * RING)]
    return lax.ppermute(value, "dp", pairs)


def after(values, *others):
    if not others:
        return values
    flat, tree = jax.tree.flatten(values)
    tied = lax.optimization_barrier(tuple(flat) + tuple(others))
    return jax.tree.unflatten(tree, tied[: len(flat)])


def along_x(value):
    return swap(value, "dp", 2 * RING, 1)


def fence(*values):
    return lax.optimization_barrier(values)


def half_float(value, bound=None):
    scale = power_scale(jnp.max(jnp.abs(value)) if bound is None else bound)
    return (value / scale).astype(f16), jnp.broadcast_to(scale, (1, 128))


def float_half(pair):
    return pair[0].astype(f32) * pair[1][0, 0]


def sum_halves(keep, send, ways):
    keep = keep + swap(send, "mp", ways, 1)
    keep = keep + swap(keep, "mp", ways, 2)
    return keep, swap(keep, "mp", ways, 1)


def mp_sum(value, mp):
    near = [swap(value, "mp", mp, bit) for bit in range(1, mp)]
    return (value + near[0]) + (near[1] + near[2])


def x_sum(value, dp):
    return value + swap(value, "dp", dp, 1)


def z_sum(value, dp):
    far = [swap(value, "dp", dp, 2 * bit) for bit in range(1, RING)]
    return (value + far[0]) + (far[1] + far[2])


def butterfly(value, combine, dp, mp, both=True):
    axes = [("mp", mp)] + ([("dp", dp)] if both else [])
    for axis, ways in axes:
        bit = 1
        while bit < ways:
            value = combine(value, swap(value, axis, ways, bit))
            bit *= 2
    return value


def gelu_exact(values):
    return 0.5 * values * (1.0 + lax.erf(values * 0.7071067811865476))


def gelu_slope(values):
    cumulative = 0.5 * (1.0 + lax.erf(values * 0.7071067811865476))
    density = jnp.exp(-0.5 * values * values) * 0.3989422804014327
    return cumulative + values * density


def norm_forward(values, norm_gain, norm_shift):
    row_mean = jnp.mean(values, axis=-1, keepdims=True)
    centered = values - row_mean
    variance = jnp.mean(centered * centered, axis=-1, keepdims=True)
    inv_dev = lax.rsqrt(variance + EPS_NORM)
    normed = centered * inv_dev
    return (normed * norm_gain + norm_shift, normed, inv_dev)


def norm_backward(grad_out, normed, inv_dev, norm_gain):
    scaled = grad_out * norm_gain
    grad_in = inv_dev * (
        scaled
        - jnp.mean(scaled, axis=-1, keepdims=True)
        - normed * jnp.mean(scaled * normed, axis=-1, keepdims=True)
    )
    return (grad_in, jnp.sum(grad_out * normed, axis=0), jnp.sum(grad_out, axis=0))


def seq_ends_of(lengths):
    return jnp.stack(
        [jnp.sum(lengths[:, : s + 1], axis=1) for s in range(lengths.shape[1])], axis=1
    )


def positions_of(lengths):
    ends = seq_ends_of(lengths)
    places = jnp.arange(LEN, dtype=jnp.int32)
    passed = places[None, :, None] >= ends[:, None, :]
    segment = jnp.sum(passed.astype(jnp.int32), axis=2)
    start = jnp.max(jnp.where(passed, ends[:, None, :], 0), axis=2)
    return (segment, places[None, :] - start)


def adam_step(master, moment_one, moment_two, gradient, weight_decay):
    new_one = BETA_FIRST * moment_one + (1.0 - BETA_FIRST) * gradient
    new_two = BETA_SECOND * moment_two + (1.0 - BETA_SECOND) * gradient * gradient
    new_master = master - RATE_ADAM * (
        new_one / (jnp.sqrt(new_two) + EPS_ADAM) + weight_decay * master
    )
    return (new_master, new_one, new_two)


def product(left_side, right_side):
    return jnp.dot(left_side, right_side, preferred_element_type=f32)


def against_rows(left_side, right_side):
    return lax.dot_general(
        left_side, right_side, (((1,), (1,)), ((), ())), preferred_element_type=f32
    )


def over_rows(left_side, right_side):
    return lax.dot_general(
        left_side, right_side, (((0,), (0,)), ((), ())), preferred_element_type=f32
    )


def hit_matrix(codes, count, kind=bf16):
    return (codes[:, None] == jnp.arange(count, dtype=jnp.int32)[None, :]).astype(kind)


def split(values, parts):
    made = []
    for _ in range(parts):
        part = lax.reduce_precision(values, 8, 7)
        made.append(part.astype(bf16))
        values = values - part
    return made


def rows_exact(hits, parts):
    upper, middle, lower = parts
    return product(hits, upper) + product(hits, middle) + product(hits, lower)


def power_scale(bound):
    safe = jnp.clip(bound, 1e-30, 1e38)
    return jnp.exp2(jnp.ceil(jnp.log2(safe)) - 14.0)


SMEM = pl.BlockSpec(memory_space=pltpu.SMEM)
VMEM = pl.BlockSpec(memory_space=pltpu.VMEM)
ANY = pl.BlockSpec(memory_space=pl.ANY)


def params(*arrays, spare=VMEM_SPARE):
    total = spare
    for one in arrays:
        *lead, rows, columns = one.shape
        size = jnp.dtype(one.dtype).itemsize
        tile = 32 // size
        total += math.prod(lead) * -(-rows // tile) * tile * -(-columns // 128) * 128 * size
    return pltpu.CompilerParams(vmem_limit_bytes=min(total, VMEM_MOST))


COST = pl.CostEstimate(flops=1, bytes_accessed=1, transcendentals=0)


def shape(dims, kind=f32):
    return jax.ShapeDtypeStruct(dims, kind)


def call(kernel, outs, scalars, arrays, name, scratch=(), spare=VMEM_SPARE):
    return pl.pallas_call(
        kernel,
        out_shape=outs,
        in_specs=[SMEM] * len(scalars) + [VMEM] * len(arrays),
        out_specs=jax.tree.map(lambda _: VMEM, outs),
        scratch_shapes=list(scratch),
        compiler_params=params(*jax.tree.leaves(outs), *arrays, *scratch, spare=spare),
        cost_estimate=COST,
        name=name,
    )(*scalars, *arrays)


def both_halves(mine, other):
    return jnp.concatenate([mine, other], axis=0)


def part_halves(value, keep, send):
    half = value.shape[0] // 2
    keep[...] = value[:half]
    send[...] = value[half:]


def strips(pieces):
    base = 0
    for piece in pieces:
        for start in range(0, piece.shape[0], STRIP):
            size = min(STRIP, piece.shape[0] - start)
            yield base + start, piece, slice(start, start + size)
        base += piece.shape[0]


def embed_kernel(codes, *refs):
    pieces, words, table = refs[:-2], refs[-2], refs[-1]
    for base, piece, rows in strips(pieces):
        table[base : base + rows.stop - rows.start, :] = piece[rows, :]
    step = 256
    for begin in range(0, words.shape[0], step):
        part = slice(begin, begin + step)
        column = lax.broadcasted_iota(jnp.int32, (step, table.shape[0]), 1)
        hits = jnp.where(codes[part, :] == column, 1.0, 0.0).astype(bf16)
        words[part, :] = product(hits, table[...]).astype(bf16)


def embed_strips_kernel(codes, piece, words, total):
    step = pl.program_id(0)

    @pl.when(step == 0)
    def _():
        total[...] = jnp.zeros_like(total)

    size = piece.shape[0]
    column = lax.broadcasted_iota(jnp.int32, (codes.shape[0], size), 1) + step * size
    hits = jnp.where(codes[...] == column, 1.0, 0.0).astype(bf16)
    total[...] += product(hits, piece[...])

    @pl.when(step == pl.num_programs(0) - 1)
    def _():
        words[...] = total[...].astype(bf16)


def embed(codes, pieces):
    tokens = codes.shape[0]
    out = shape((tokens, D), bf16)
    if len(pieces) > 1:
        vocab = sum(piece.shape[0] for piece in pieces)
        scratch = [pltpu.VMEM((vocab, D), bf16)]
        return call(embed_kernel, out, [], [codes, *pieces], "embed", scratch, VMEM_MOST)
    return pl.pallas_call(
        embed_strips_kernel,
        grid=(pieces[0].shape[0] // STRIP,),
        out_shape=out,
        in_specs=[
            pl.BlockSpec((tokens, 1), lambda r: (0, 0)),
            pl.BlockSpec((STRIP, D), lambda r: (r, 0)),
        ],
        out_specs=pl.BlockSpec((tokens, D), lambda r: (0, 0)),
        scratch_shapes=[pltpu.VMEM((tokens, D), f32)],
        compiler_params=pltpu.CompilerParams(vmem_limit_bytes=32 << 20),
        cost_estimate=COST,
        name="embed",
    )(codes, *pieces)


def normalize_kernel(flat, words, places, affine, x_low, picked, picked_low, *rest):
    x_out = rest[-1]
    step = 128
    for begin in range(0, words.shape[0], step):
        part = slice(begin, begin + step)
        out, _, _ = norm_forward(
            words[part, :].astype(f32) + places[part, :], affine[0:1, :], affine[1:2, :]
        )
        x_out[part, :] = out
        x_low[part, :] = out.astype(bf16)

    def pick_row(p, carry):
        picked[pl.ds(p, 1), :] = x_out[pl.ds(flat[p], 1), :]
        return carry

    lax.fori_loop(0, picked.shape[0], pick_row, 0, unroll=8)
    picked_low[...] = picked[...].astype(bf16)


def head_pair(values, lanes):
    zero = jnp.zeros_like(values)
    return jnp.concatenate([jnp.where(lanes, values, zero), jnp.where(lanes, zero, values)], axis=0)


def attend_kernel(groups, downs, acrosses, *refs):
    pieces, refs = refs[:groups], refs[groups:]
    (
        x_mine,
        x_other,
        picked_mine,
        picked_other,
        bias_query,
        bias_keyval,
        segment,
        pick_segment,
        joined_w,
        output_w,
        upward_w,
        downward_w,
        keyval,
        query,
        probs,
        mixed,
        keep,
        send,
        stacked,
        dense,
        x_low,
        sems,
        out_sems,
    ) = refs
    rows = segment.shape[0]
    inner = query.shape[1]
    hidden = upward_w.shape[1]
    sizes = [piece.shape[0] for piece in pieces]
    starts = [sum(sizes[:g]) for g in range(groups)]
    loads = [
        pltpu.make_async_copy(piece, stacked.at[pl.ds(start, size)], sems.at[g])
        for g, (piece, start, size) in enumerate(zip(pieces, starts, sizes))
    ]
    half = x_low.shape[0] // 2
    loads_x = [
        pltpu.make_async_copy(x_mine, x_low.at[pl.ds(0, half)], sems.at[groups]),
        pltpu.make_async_copy(x_other, x_low.at[pl.ds(half, half)], sems.at[groups + 1]),
    ]
    for load in loads + loads_x:
        load.start()
    for g, load in enumerate(loads):
        load.wait()
        for t in range(starts[g], starts[g] + sizes[g]):
            down = pl.multiple_of(downs[t], KB)
            across = pl.multiple_of(acrosses[t], KB)
            dense[pl.ds(down, KB), pl.ds(across, KB)] = stacked[t]
    start_up, start_down = 3 * inner, 3 * inner + hidden
    stores = [
        pltpu.make_async_copy(dense.at[down, across], out, out_sems.at[n])
        for n, (out, down, across) in enumerate(
            (
                (joined_w, pl.ds(0, D), pl.ds(0, start_up)),
                (output_w, pl.ds(D, inner), pl.ds(0, D)),
                (upward_w, pl.ds(0, D), pl.ds(start_up, hidden)),
                (downward_w, pl.ds(0, hidden), pl.ds(start_down, D)),
            )
        )
    ]
    for store in stores:
        store.start()
    for load in loads_x:
        load.wait()
    pairs = inner // KB
    picked_low = both_halves(picked_mine[...], picked_other[...])
    query[...] = (product(picked_low, dense[:D, :inner]) + bias_query[...]).astype(bf16)
    lanes = lax.broadcasted_iota(jnp.int32, (POS, KB), 1) < HD
    for r in range(rows):
        part = slice(r * LEN, (r + 1) * LEN)
        picks = slice(r * POS, (r + 1) * POS)
        keyval[part, :] = (
            product(x_low[part, :], dense[:D, inner:start_up]) + bias_keyval[...]
        ).astype(bf16)
        same = pick_segment[picks, :] == segment[r : r + 1, :]
        same = jnp.concatenate([same, same], axis=0)
        for pair in range(pairs):
            cut = slice(pair * KB, (pair + 1) * KB)
            cut_v = slice(inner + pair * KB, inner + (pair + 1) * KB)
            both = head_pair(query[picks, cut], lanes)
            scores = against_rows(both, keyval[part, cut]) * HD ** (-0.5)
            scores = jnp.where(same, scores, MASK_FILL)
            raised = jnp.exp(scores - jnp.max(scores, axis=-1, keepdims=True))
            part_probs = raised / jnp.sum(raised, axis=-1, keepdims=True)
            probs[r * pairs + pair] = part_probs
            out = product(part_probs.astype(bf16), keyval[part, cut_v])
            mixed[picks, cut] = jnp.where(lanes, out[:POS], out[POS:]).astype(bf16)
    part_halves(product(mixed[...], dense[D:, :D]), keep, send)
    for store in stores:
        store.wait()


def attend(corners, pieces, x_halves, picked_halves, bias_query, bias_keyval, segment, pick_segment, hidden):
    rows = segment.shape[0]
    inner = bias_query.shape[1]
    tokens, picks = 2 * x_halves[0].shape[0], 2 * picked_halves[0].shape[0]
    groups = len(pieces)
    total = sum(piece.shape[0] for piece in pieces)
    scratch = [
        pltpu.VMEM((total, KB, KB), bf16),
        pltpu.VMEM((D + inner, 3 * inner + 2 * hidden), bf16),
        pltpu.VMEM((tokens, D), bf16),
    ]
    outs = [
            shape((D, 3 * inner), bf16),
            shape((inner, D), bf16),
            shape((D, hidden), bf16),
            shape((hidden, D), bf16),
            shape((tokens, 2 * inner), bf16),
            shape((picks, inner), bf16),
            shape((rows * inner // KB, 2 * POS, LEN)),
            shape((picks, inner), bf16),
            shape((picks // 2, D)),
            shape((picks // 2, D)),
    ]
    return pl.pallas_call(
        functools.partial(attend_kernel, groups),
        out_shape=outs,
        in_specs=[SMEM] * 2 + [ANY] * (groups + 2) + [VMEM] * 6,
        out_specs=[ANY] * 4 + [VMEM] * 6,
        scratch_shapes=scratch
        + [pltpu.SemaphoreType.DMA((groups + 2,)), pltpu.SemaphoreType.DMA((4,))],
        compiler_params=params(spare=36 << 20),
        cost_estimate=COST,
        name="attend",
    )(*corners, *pieces, *x_halves, *picked_halves, bias_query, bias_keyval, segment, pick_segment)


def forward_kernel(
    mine,
    other,
    picked_mine,
    picked_other,
    affine,
    bias_up,
    upward_w,
    downward_w,
    normed_out,
    inv_out,
    first,
    first_low,
    upper_pre,
    acted,
    keep,
    send,
):
    attended = both_halves(mine[...], other[...]) + affine[0:1, :]
    out, normed, inv = norm_forward(
        both_halves(picked_mine[...], picked_other[...]) + attended,
        affine[1:2, :],
        affine[2:3, :],
    )
    normed_out[...] = normed
    inv_out[...] = inv
    first[...] = out
    first_low[...] = out.astype(bf16)
    upper = product(first_low[...], upward_w[...]) + bias_up[...]
    upper_pre[...] = upper
    acted[...] = gelu_exact(upper).astype(bf16)
    part_halves(product(acted[...], downward_w[...]), keep, send)


def logits_kernel(mine, other, first, affine, target, *refs):
    pieces, refs = refs[:-6], refs[-6:]
    normed_out, inv_out, picked_low, top_feature, logits, stats = refs
    branch = both_halves(mine[...], other[...]) + affine[0:1, :]
    out, normed, inv = norm_forward(first[...] + branch, affine[1:2, :], affine[2:3, :])
    normed_out[...] = normed
    inv_out[...] = inv
    picked_low[...] = out.astype(bf16)
    top_feature[...] = jnp.broadcast_to(jnp.max(jnp.abs(out)), top_feature.shape)
    count = out.shape[0]
    top = jnp.full((1, count), -jnp.inf, f32)
    chosen = jnp.zeros((1, count), f32)
    for base, piece, rows in strips(pieces):
        size = rows.stop - rows.start
        part = against_rows(piece[rows, :], picked_low[...])
        row = lax.broadcasted_iota(jnp.int32, (size, count), 0) + base
        part = jnp.where(row % VOC_PAD < VOC_DEV, part, -jnp.inf)
        logits[base : base + size, :] = part
        top = jnp.maximum(top, jnp.max(part, axis=0, keepdims=True))
        hit = jnp.where(row == target[...], part, 0.0)
        chosen = chosen + jnp.sum(hit, axis=0, keepdims=True)
    total = jnp.zeros((1, count), f32)
    for base, piece, rows in strips(pieces):
        part = logits[base : base + rows.stop - rows.start, :]
        total = total + jnp.sum(jnp.exp(part - top), axis=0, keepdims=True)
    stats[0:1, :] = top
    stats[1:2, :] = total
    stats[2:3, :] = chosen
    stats[3:8, :] = jnp.zeros((5, count), f32)


def head_kernel(own, near, far, across, target, logits, *refs):
    pieces, refs = refs[:-4], refs[-4:]
    grad_logits, loss, keep, send = refs
    count = target.shape[1]
    middle = count // 2

    def turned(one):
        return jnp.concatenate([one[:, middle:], one[:, :middle]], axis=1)

    everyone = (own[...], turned(near[...]), far[...], turned(across[...]))
    top = functools.reduce(jnp.maximum, [one[0:1, :] for one in everyone])
    parts = [one[1:2, :] * jnp.exp(one[0:1, :] - top) for one in everyone]
    total = (parts[0] + parts[1]) + (parts[2] + parts[3])
    chosen = [one[2:3, :] for one in everyone]
    chosen = (chosen[0] + chosen[1]) + (chosen[2] + chosen[3])
    losses = jnp.sum(jnp.log(total) + top - chosen, axis=1, keepdims=True)
    loss[...] = jnp.broadcast_to(losses, loss.shape)
    back = jnp.zeros((count, D), f32)
    for base, piece, rows in strips(pieces):
        size = rows.stop - rows.start
        row = lax.broadcasted_iota(jnp.int32, (size, count), 0) + base
        hit = jnp.where(row == target[...], 1.0, 0.0)
        part = logits[base : base + size, :]
        part = (jnp.exp(part - top) / total - hit).astype(bf16)
        grad_logits[base : base + size, :] = part
        back = back + over_rows(part, piece[rows, :])
    part_halves(back, keep, send)


def backward_kernel(
    mine,
    other,
    normed,
    inv,
    gain,
    upper_pre,
    upward_w,
    downward_w,
    grad_pre2,
    branch_grad,
    upper_grad,
    row_sums,
    upper_sums,
    keep,
    send,
):
    grad_out = both_halves(mine[...], other[...])
    grad_in, gain_sum, shift_sum = norm_backward(grad_out, normed[...], inv[...], gain[...])
    grad_pre2[...] = grad_in
    branch_grad[...] = grad_in.astype(bf16)
    row_sums[0:1, :] = gain_sum[None]
    row_sums[1:2, :] = shift_sum[None]
    row_sums[2:3, :] = jnp.sum(branch_grad[...].astype(f32), axis=0, keepdims=True)
    upper = against_rows(branch_grad[...], downward_w[...]) * gelu_slope(upper_pre[...])
    upper_grad[...] = upper.astype(bf16)
    upper_sums[...] = jnp.sum(upper_grad[...].astype(f32), axis=0, keepdims=True)
    part_halves(against_rows(upper_grad[...], upward_w[...]), keep, send)


def back_attention_kernel(
    positions,
    rank_first,
    mine,
    other,
    grad_pre2,
    first_normed,
    first_inv,
    gain,
    joined_w,
    output_w,
    keyval,
    query,
    probs,
    keep,
    send,
    row_sums,
    query_sums,
    keyval_sums,
    attended_grad,
    query_grad,
    keyval_grad,
    pick_grad,
):
    picks, inner = query.shape
    rows = picks // POS
    pairs = inner // KB
    scale = HD ** (-0.5)
    grad_out = both_halves(mine[...], other[...]) + grad_pre2[...]
    grad_pre1, gain_sum, shift_sum = norm_backward(
        grad_out, first_normed[...], first_inv[...], gain[...]
    )
    attended_grad[...] = grad_pre1.astype(bf16)
    row_sums[0:1, :] = gain_sum[None]
    row_sums[1:2, :] = shift_sum[None]
    row_sums[2:3, :] = jnp.sum(attended_grad[...].astype(f32), axis=0, keepdims=True)
    mixed_grad = against_rows(attended_grad[...], output_w[...]).astype(bf16)
    lanes = lax.broadcasted_iota(jnp.int32, (POS, KB), 1) < HD
    for r in range(rows):
        part = slice(r * LEN, (r + 1) * LEN)
        here = slice(r * POS, (r + 1) * POS)
        for pair in range(pairs):
            cut = slice(pair * KB, (pair + 1) * KB)
            cut_v = slice(inner + pair * KB, inner + (pair + 1) * KB)
            part_probs = probs[r * pairs + pair]
            out_grad = head_pair(mixed_grad[here, cut], lanes)
            both = head_pair(query[here, cut], lanes)
            probs_grad = against_rows(out_grad, keyval[part, cut_v])
            inner_sum = jnp.sum(probs_grad * part_probs, axis=-1, keepdims=True)
            scores_grad = (part_probs * (probs_grad - inner_sum)).astype(bf16)
            back = product(scores_grad, keyval[part, cut])
            query_grad[here, cut] = (jnp.where(lanes, back[:POS], back[POS:]) * scale).astype(bf16)
            keyval_grad[part, cut] = (over_rows(scores_grad, both) * scale).astype(bf16)
            keyval_grad[part, cut_v] = over_rows(part_probs.astype(bf16), out_grad).astype(bf16)
    query_sums[...] = jnp.sum(query_grad[...].astype(f32), axis=0, keepdims=True)
    keyval_sums[...] = jnp.sum(keyval_grad[...].astype(f32), axis=0, keepdims=True)
    pick_grad[...] = (
        against_rows(query_grad[...], joined_w[:, :inner]) + grad_pre1 * rank_first[0]
    )
    for row, out in ((1, send), (0, keep)):
        out[...] = against_rows(keyval_grad[row * LEN : (row + 1) * LEN, :], joined_w[:, inner:])

        def add_row(p, carry):
            spot = positions[row * POS + p]
            out[pl.ds(spot, 1), :] += pick_grad[pl.ds(row * POS + p, 1), :]
            return carry

        lax.fori_loop(0, POS, add_row, 0, unroll=8)


def back_weights_kernel(
    downs,
    acrosses,
    x_mine,
    x_other,
    keyval_grad,
    picked_mine,
    picked_other,
    query_grad,
    mixed,
    attended_grad,
    acted,
    branch_grad,
    first_low,
    upper_grad,
    *rest,
):
    packed, dense = rest[:-1], rest[-1]
    inner = query_grad.shape[1]
    low = dense.dtype
    picked_low = both_halves(picked_mine[...], picked_other[...])
    dense[:D, :inner] = over_rows(picked_low, query_grad[...]).astype(low)
    half = x_mine.shape[0]
    joined = over_rows(x_mine[...], keyval_grad[:half, :])
    joined = joined + over_rows(x_other[...], keyval_grad[half:, :])
    dense[:D, inner : 3 * inner] = joined.astype(low)
    start_up, start_down = 3 * inner, 3 * inner + upper_grad.shape[1]
    dense[:D, start_up:start_down] = over_rows(first_low[...], upper_grad[...]).astype(low)
    dense[:D, start_down:] = over_rows(acted[...], branch_grad[...]).astype(low)
    dense[D:, :D] = over_rows(mixed[...], attended_grad[...]).astype(low)
    spot = 0
    for out in packed:
        for t in range(out.shape[0]):
            down = pl.multiple_of(downs[spot], KB)
            across = pl.multiple_of(acrosses[spot], KB)
            out[t] = dense[pl.ds(down, KB), pl.ds(across, KB)]
            spot += 1


def tile_corners(natural, inner, hidden):
    count_joined, count_output = D // KB * 3 * inner // KB, inner // KB * D // KB
    count_up = D // KB * hidden // KB
    n_joined = natural
    n_output = natural - count_joined
    n_up = n_output - count_output
    n_down = n_up - count_up
    wide_joined, wide, wide_up = 3 * inner // KB, D // KB, hidden // KB
    down = jnp.where(
        n_output < 0,
        n_joined // wide_joined * KB,
        jnp.where(
            n_up < 0,
            D + n_output // wide * KB,
            jnp.where(n_down < 0, n_up // wide_up * KB, n_down // wide * KB),
        ),
    )
    across = jnp.where(
        n_output < 0,
        n_joined % wide_joined * KB,
        jnp.where(
            n_up < 0,
            n_output % wide * KB,
            jnp.where(
                n_down < 0,
                3 * inner + n_up % wide_up * KB,
                3 * inner + hidden + n_down % wide * KB,
            ),
        ),
    )
    return down, across


def embedding_kernel(keep, came, words, places, gain, grad, sums, top):
    _, normed, inv = norm_forward(words[...].astype(f32) + places[...], gain[...], gain[...])
    grad_in, gain_sum, shift_sum = norm_backward(
        keep[...] + came[...], normed, inv, gain[...]
    )
    grad[...] = grad_in
    sums[0:1, :] = gain_sum[None]
    sums[1:2, :] = shift_sum[None]
    top[...] = jnp.broadcast_to(jnp.max(jnp.abs(grad_in)), top.shape)


def table_kernel(
    codes, place_codes, upper, lower, grad_logits, picked_low, grad, place_grad, hits
):
    rows, place_rows = grad.shape[0], place_grad.shape[0]

    @pl.when(pl.program_id(1) == 0)
    def _():
        row = lax.broadcasted_iota(jnp.int32, (rows, hits.shape[1]), 0)
        row = row + pl.program_id(0) * rows
        hits[:rows, :] = jnp.where(row == codes[...], 1.0, 0.0).astype(bf16)
        row = lax.broadcasted_iota(jnp.int32, (place_rows, hits.shape[1]), 0)
        hits[rows:, :] = jnp.where(row == place_codes[...], 1.0, 0.0).astype(bf16)

    total = product(hits[...], upper[...]) + product(hits[...], lower[...])
    grad[...] = total[:rows] + product(grad_logits[...], picked_low[...])
    place_grad[...] = total[rows:]


def parts_kernel(codes, place_codes, *refs):
    *quarters, grad_logits, picked_low, grad, hits = refs
    parts, each, _ = grad.shape
    vocab = grad_logits.shape[0]
    place_rows = hits.shape[0] - vocab
    own = place_rows // parts

    @pl.when(pl.program_id(0) == 0)
    def _():
        row = lax.broadcasted_iota(jnp.int32, (vocab, hits.shape[1]), 0)
        hits[:vocab, :] = jnp.where(row == codes[...], 1.0, 0.0).astype(bf16)
        row = lax.broadcasted_iota(jnp.int32, (place_rows, hits.shape[1]), 0)
        hits[vocab:, :] = jnp.where(row == place_codes[...], 1.0, 0.0).astype(bf16)

    values = jnp.concatenate([quarter[...] for quarter in quarters], axis=0)
    upper = values.astype(bf16)
    lower = (values - upper.astype(f32)).astype(bf16)
    total = product(hits[...], upper) + product(hits[...], lower)
    words = total[:vocab] + product(grad_logits[...], picked_low[...])
    for r in range(parts):
        grad[r, :VOC_PAD, :] = words[r * VOC_PAD : (r + 1) * VOC_PAD]
        grad[r, VOC_PAD:each, :] = total[vocab + r * own : vocab + (r + 1) * own]


def parts_gradient(parts, codes, place_codes, place_rows, quarters, grad_logits, picked_low):
    vocab, picks = grad_logits.shape
    tokens = codes.shape[1]
    wide = 256
    each = (vocab + place_rows) // parts

    def columns(high):
        return pl.BlockSpec((high, wide), lambda c: (0, c))

    row_of_codes = pl.BlockSpec((1, tokens), lambda c: (0, 0))
    return pl.pallas_call(
        parts_kernel,
        grid=(D // wide,),
        out_shape=shape((parts, each, D)),
        in_specs=[
            row_of_codes,
            row_of_codes,
            *[columns(quarter.shape[0]) for quarter in quarters],
            pl.BlockSpec((vocab, picks), lambda c: (0, 0)),
            columns(picks),
        ],
        out_specs=pl.BlockSpec((parts, each, wide), lambda c: (0, 0, c)),
        scratch_shapes=[pltpu.VMEM((vocab + place_rows, tokens), bf16)],
        compiler_params=pltpu.CompilerParams(vmem_limit_bytes=36 << 20),
        cost_estimate=COST,
        name="table_gradient",
    )(codes, place_codes, *quarters, grad_logits, picked_low)


def table_gradient(codes, place_codes, place_rows, upper, lower, grad_logits, picked_low):
    vocab, picks = grad_logits.shape
    tokens = upper.shape[0]
    wide = 256

    def columns(high):
        return pl.BlockSpec((high, wide), lambda r, c: (0, c))

    row_of_codes = pl.BlockSpec((1, tokens), lambda r, c: (0, 0))
    return pl.pallas_call(
        table_kernel,
        grid=(vocab // STRIP, D // wide),
        out_shape=[shape((vocab, D)), shape((place_rows, D))],
        in_specs=[
            row_of_codes,
            row_of_codes,
            columns(tokens),
            columns(tokens),
            pl.BlockSpec((STRIP, picks), lambda r, c: (r, 0)),
            columns(picks),
        ],
        out_specs=[pl.BlockSpec((STRIP, wide), lambda r, c: (r, c)), columns(place_rows)],
        scratch_shapes=[pltpu.VMEM((STRIP + place_rows, tokens), bf16)],
        compiler_params=pltpu.CompilerParams(vmem_limit_bytes=32 << 20),
        cost_estimate=COST,
        name="table_gradient",
    )(codes, place_codes, upper, lower, grad_logits, picked_low)


def local(
    input_ids,
    seq_lengths,
    loss_positions,
    targets,
    block_owner,
    layer_master,
    stats_left,
    stats_right,
    root_left,
    root_right,
    table_master,
    table_first,
    table_second,
    vector_master,
    vector_first,
    vector_second,
):
    mp = lax.axis_size("mp")
    dp = lax.axis_size("dp")
    fast = dp == 2 * RING
    model_rank = lax.axis_index("mp")
    data_rank = lax.axis_index("dp")
    inner = D // mp
    ff_rows = FF // D
    hidden = FF // mp
    rows = input_ids.shape[0]
    tokens = rows * LEN
    share = tokens // mp
    own_blocks = layer_master.shape[1]
    blocks = own_blocks * dp

    if fast:
        z_here, x_here = data_rank // 2, data_rank % 2

        def place_of(owner):
            return 2 * ((z_here - owner // 2) % RING) + (owner % 2 + x_here) % 2
    else:

        def place_of(owner):
            return owner

    low_bit, high_bit = model_rank % 2, model_rank // 2

    def turned(array):
        return jnp.where(low_bit == 0, array, array[::-1])

    input_ids, seq_lengths = turned(input_ids), turned(seq_lengths)
    loss_positions, targets = turned(loss_positions), turned(targets)
    rank_first = (model_rank == 0).astype(f32)
    tail = vector_master[LEN:]
    bias_query = lax.dynamic_slice_in_dim(tail[2], model_rank * inner, inner)[None]
    bias_value = lax.dynamic_slice_in_dim(tail[3], model_rank * inner, inner)
    bias_keyval = jnp.concatenate([jnp.zeros((inner,), f32), bias_value])[None]
    bias_up = lax.dynamic_slice_in_dim(tail[7 : 7 + ff_rows].reshape(FF), model_rank * hidden, hidden)[None]
    affine_zero, affine_one = tail[0:2], tail[4:7]
    affine_two = tail[7 + ff_rows : 10 + ff_rows]

    segment, offset = positions_of(seq_lengths)
    pick_segment = jnp.sum(
        (seq_ends_of(seq_lengths)[:, None, :] <= loss_positions[:, :, None]).astype(jnp.int32), axis=2
    ).reshape(-1, 1)

    def codes_of(ids):
        part = ids // VOC_DEV
        code = place_of(part // mp) * VOC_PAD + ids % VOC_DEV
        return jnp.where(part % mp == model_rank, code, -1)

    codes = codes_of(input_ids.reshape(-1))
    target_codes = codes_of(targets.reshape(1, -1))

    def corners_of():
        number = jnp.arange(blocks, dtype=jnp.int32)
        if fast:
            part = number // own_blocks
            owner = 2 * ((z_here - part // 2) % RING) + (part % 2 + x_here) % 2
            taken = owner * own_blocks + number % own_blocks
            order = jnp.sum(
                jnp.where(taken[:, None] == number[None, :], block_owner[None, :], 0), axis=1
            )
        else:
            order = block_owner
        return tile_corners(order, inner, hidden)

    table_low = jnp.pad(table_master.astype(bf16), ((0, VOC_PAD - VOC_DEV), (0, 0)))
    layer_low = layer_master[0].astype(bf16)
    vocab = dp * VOC_PAD
    words_half = tokens // 2
    def places_of(row, parts):
        return rows_exact(hit_matrix(offset[row], LEN), parts)

    def own_of(words):
        return [
            lax.dynamic_slice_in_dim(value, high_bit * share, share, 0)
            for value in (words, places[0])
        ]

    def normalize(row, words):
        return call(
            normalize_kernel,
            [
                shape((words_half, D), bf16),
                shape((POS, D)),
                shape((POS, D), bf16),
            ],
            [row_positions[row]],
            [words, places[row], affine_zero],
            "normalize",
            [pltpu.VMEM((words_half, D), f32)],
            8 << 20,
        )

    send_codes, keep_codes = codes[words_half:, None], codes[:words_half, None]
    place_rows = LEN // mp
    per_owner = place_rows // dp
    place_codes = offset.reshape(1, -1) - model_rank * place_rows
    place_codes = jnp.where(
        (place_codes >= 0) & (place_codes < place_rows),
        place_of(place_codes // per_owner) * per_owner + place_codes % per_owner,
        -1,
    )
    def by_quarters(codes):
        codes = codes.reshape(rows, mp // 2, share)
        return jnp.where(high_bit == 0, codes, codes[:, ::-1]).reshape(1, -1)

    small = (
        affine_zero,
        affine_one,
        affine_two,
        affine_zero[0:1],
        affine_one[1:2],
        affine_two[1:2],
        bias_query,
        bias_keyval,
        bias_up,
        [loss_positions[row] for row in range(rows)],
        loss_positions.reshape(-1),
        rank_first.reshape(1),
        corners_of(),
        segment,
        pick_segment,
        by_quarters(codes),
        target_codes,
        by_quarters(place_codes),
        send_codes,
        keep_codes,
    )
    if fast:
        place_parts = split(vector_master[:LEN], 3)
        moved, met, place_parts, layer_low = fence(
            ring_step(table_low), along_x(table_low), place_parts, layer_low
        )
        held, crossed = [table_low, moved], [met]
        places = [places_of(row, place_parts) for row in range(rows)]
        moved, met, places = fence(ring_step(held[1]), along_x(held[1]), places)
        held.append(moved)
        crossed.append(met)
        moved, met, small = fence(ring_step(held[2]), along_x(held[2]), small)
        held.append(moved)
        crossed.append(met)
    (
        affine_zero,
        affine_one,
        affine_two,
        gain_zero,
        gain_one,
        gain_two,
        bias_query,
        bias_keyval,
        bias_up,
        row_positions,
        all_positions,
        rank_one,
        corners,
        segment,
        pick_segment,
        code_row,
        target_codes,
        place_codes,
        send_codes,
        keep_codes,
    ) = small
    if fast:
        cut = 96
        moved, met, *last = fence(
            ring_step(layer_low),
            along_x(layer_low),
            along_x(held[RING - 1][:cut]),
            ring_step(crossed[RING - 2][cut:]),
        )
        table_parts = [piece for pair in zip(held, crossed) for piece in pair]
        table_parts += [held[RING - 1], *last]
        held, crossed = [layer_low, moved], [met]
        send = embed(send_codes, table_parts)
        near = swap(send, "mp", mp, 1)
        keep = embed(keep_codes, table_parts) + near
        moved, met, keep = fence(ring_step(held[1]), along_x(held[1]), keep)
        held.append(moved)
        crossed.append(met)
        far = swap(keep, "mp", mp, 2)
        moved, met, keep, far = fence(ring_step(held[2]), along_x(held[2]), keep, far)
        held.append(moved)
        crossed.append(met)
        words = keep + far
        near = swap(words, "mp", mp, 1)
        x_mine, x_other = normalize(0, words), normalize(1, near)
        own_words, own_places = own_of(words)
        cut = own_blocks // 2
        *last, x_mine, x_other, own_words, own_places = fence(
            along_x(held[3][:cut]),
            ring_step(crossed[2][cut:]),
            x_mine,
            x_other,
            own_words,
            own_places,
        )
        layer_parts = [piece for pair in zip(held, crossed) for piece in pair]
        layer_parts += [held[3], *last]
    else:
        place_parts = split(vector_master[:LEN], 3)
        places = [places_of(row, place_parts) for row in range(rows)]
        table_parts = [lax.all_gather(table_low, "dp", axis=0, tiled=True)]
        layer_parts = [lax.all_gather(layer_low, "dp", axis=0, tiled=True)]
        keep, send = embed(keep_codes, table_parts), embed(send_codes, table_parts)
        words, near = sum_halves(keep, send, mp)
        x_mine, x_other = normalize(0, words), normalize(1, near)
        own_words, own_places = own_of(words)

    (
        joined_w,
        output_w,
        upward_w,
        downward_w,
        keyval,
        queries,
        probs,
        mixed_low,
        keep,
        send,
    ) = attend(
        corners,
        layer_parts,
        [x_mine[0], x_other[0]],
        [x_mine[2], x_other[2]],
        bias_query,
        bias_keyval,
        segment,
        pick_segment,
        hidden,
    )
    count = rows * POS
    half_shapes = [shape((count // 2, D)), shape((count // 2, D))]
    row_shape, low_shape = shape((count, D)), shape((count, D), bf16)
    first_normed, first_inv, first_out, first_low, upper_pre, acted_low, keep, send = call(
        forward_kernel,
        [
            row_shape,
            shape((count, 1)),
            row_shape,
            low_shape,
            shape((count, hidden)),
            shape((count, hidden), bf16),
            *half_shapes,
        ],
        [],
        [*sum_halves(keep, send, mp), x_mine[1], x_other[1], affine_one, bias_up, upward_w, downward_w],
        "forward",
        spare=8 << 20,
    )

    second_normed, second_inv, picked_low, top_feature, logits, stats = call(
        logits_kernel,
        [
            row_shape,
            shape((count, 1)),
            low_shape,
            shape((1, 128)),
            shape((vocab, count)),
            shape((8, count)),
        ],
        [],
        [*sum_halves(keep, send, mp), first_out, affine_two, target_codes, *table_parts],
        "logits",
        spare=8 << 20,
    )
    everyone = [stats] + [swap(stats, "mp", mp, bit) for bit in range(1, mp)]
    grad_logits, loss_part, keep, send = call(
        head_kernel,
        [shape((vocab, count), bf16), shape((1, 128)), *half_shapes],
        [],
        [*everyone, target_codes, logits, *table_parts],
        "head",
        spare=8 << 20,
    )

    grad_pre2, branch_grad, upper_grad, sums_two, upper_sums, keep, send = call(
        backward_kernel,
        [
            row_shape,
            low_shape,
            shape((count, hidden), bf16),
            shape((3, D)),
            shape((1, hidden)),
            *half_shapes,
        ],
        [],
        [
            *sum_halves(keep, send, mp),
            second_normed,
            second_inv,
            gain_two,
            upper_pre,
            upward_w,
            downward_w,
        ],
        "backward",
        spare=8 << 20,
    )
    keep, send, sums_one, query_sums, keyval_sums, attended_grad, query_grad, keyval_grad = call(
        back_attention_kernel,
        [
            shape((tokens // 2, D)),
            shape((tokens // 2, D)),
            shape((3, D)),
            shape((1, inner)),
            shape((1, 2 * inner)),
            low_shape,
            shape((count, inner), bf16),
            shape((tokens, 2 * inner), bf16),
        ],
        [all_positions, rank_one],
        [
            *sum_halves(keep, send, mp),
            grad_pre2,
            first_normed,
            first_inv,
            gain_one,
            joined_w,
            output_w,
            keyval,
            queries,
            probs,
        ],
        "back_attention",
        [pltpu.VMEM((count, D), f32)],
        10 << 20,
    )
    groups = dp if fast else 1
    layer_grad = call(
        back_weights_kernel,
        [shape((blocks // groups, KB, KB), bf16)] * groups,
        corners,
        [
            x_mine[0],
            x_other[0],
            keyval_grad,
            x_mine[2],
            x_other[2],
            query_grad,
            mixed_low,
            attended_grad,
            acted_low,
            branch_grad,
            first_low,
            upper_grad,
        ],
        "back_weights",
        [pltpu.VMEM((D + inner, 3 * inner + 2 * hidden), bf16)],
        VMEM_MOST,
    )

    def quarters_of(value):
        return (
            lax.dynamic_slice_in_dim(value, high_bit * share, share, 0),
            lax.dynamic_slice_in_dim(value, (1 - high_bit) * share, share, 0),
        )

    def embedding(keep, came):
        return call(
            embedding_kernel,
            [shape((share, D)), shape((2, D)), shape((1, 128))],
            [],
            [keep, came, own_words, own_places, gain_zero],
            "embedding",
            spare=8 << 20,
        )

    def embedding_far(keep, send):
        keep, send = quarters_of(keep + swap(send, "mp", mp, 1))
        return keep, swap(half_float(send), "mp", mp, 2)

    def own_embedding(keep, far):
        grad, sums, limit = embedding(keep, float_half(far))
        return half_float(grad, limit[0, 0]), sums, limit

    def all_embedding(sent, far, near):
        return [float_half(pair) for pair in (sent, far, *near)]

    def vector_of(sums_zero, limit):
        def spread(part, width, start):
            return lax.dynamic_update_slice_in_dim(jnp.zeros((1, width), f32), part, start, 1)

        bound = share * limit[:, :1] + rank_first * count * top_feature[:, :1]
        return jnp.concatenate(
            [
                sums_zero,
                spread(query_sums, D, model_rank * inner),
                spread(keyval_sums[:, inner:], D, model_rank * inner),
                sums_one[2:3] * rank_first,
                sums_one[0:2] * rank_first,
                spread(upper_sums, FF, model_rank * hidden).reshape(ff_rows, D),
                sums_two[2:3] * rank_first,
                sums_two[0:2] * rank_first,
                jnp.concatenate(
                    [
                        jnp.broadcast_to(loss_part[:, :1] * rank_first, (1, D // 2)),
                        jnp.broadcast_to(bound, (1, D // 2)),
                    ],
                    axis=1,
                ),
            ],
            axis=0,
        )

    def shampoo_products(total):
        scale = power_scale(jnp.max(jnp.abs(total)))
        gradient = total[None] / scale
        return (
            scale,
            jnp.einsum("...ij,...kj->...ik", gradient, gradient, precision=HIGH),
            jnp.einsum("...ji,...jk->...ik", gradient, gradient, precision=HIGH),
            jnp.einsum(
                "...ij,...jk->...ik",
                jnp.einsum("...ij,...jk->...ik", root_left, gradient, precision=HIGH),
                root_right,
                precision=HIGH,
            ),
        )

    def reduce_step(parts, k, moving, kind, beside):
        met = along_x(parts[2 * k + 1].astype(kind))
        if moving is None:
            met, beside = fence(met, beside)
            return parts[2 * k].astype(f32) + met.astype(f32), beside
        came = ring_step(moving.astype(kind))
        met, came, beside = fence(met, came, beside)
        return parts[2 * k].astype(f32) + came.astype(f32) + met.astype(f32), beside

    if fast:
        total, far = reduce_step(layer_grad, 1, None, bf16, embedding_far(keep, send))
        keep, far = far
        sent, sums_zero, limit_here = own_embedding(keep, far)
        far = swap(sent, "mp", mp, 2)
        total, beside = reduce_step(
            layer_grad, 2, total, bf16, (sent, far, sums_zero, limit_here)
        )
        sent, far, sums_zero, limit_here = beside
        near = swap((sent, far), "mp", mp, 1)
        vector_part = mp_sum(vector_of(sums_zero, limit_here), mp)
        total, beside = reduce_step(
            layer_grad, 3, total, bf16, (sent, far, near, vector_part)
        )
        *embed_parts, vector_part = beside
        vector_part = z_sum(x_sum(vector_part, dp), dp)
        parts = parts_gradient(
            dp,
            code_row,
            place_codes,
            place_rows,
            all_embedding(*embed_parts),
            grad_logits,
            picked_low,
        )
        layer_total, beside = reduce_step(layer_grad, 0, total, bf16, (parts, vector_part))
        parts, vector_part = beside
        scale_all = power_scale(vector_part[-1, D // 2])
        inverse = 1.0 / scale_all

        def leaving(k):
            return (parts[2 * k + 1] * inverse).astype(f16)

        met, ready, parts, layer_total = fence(
            along_x(leaving(1)), leaving(2), parts, layer_total
        )
        total = parts[2] * inverse + met.astype(f32)
        layer_scale, gram_left, gram_right, shaped = shampoo_products(layer_total)
        squares = jnp.sum(layer_total * layer_total)
        met, came, ready, parts, squares, layer_scale, gram_left = fence(
            along_x(ready),
            ring_step(total.astype(f16)),
            leaving(3),
            parts,
            squares,
            layer_scale,
            gram_left,
        )
        total = parts[4] * inverse + came.astype(f32) + met.astype(f32)
        met, came, ready, parts, gram_right = fence(
            along_x(ready), ring_step(total.astype(f16)), leaving(0), parts, gram_right
        )
        total = parts[6] * inverse + came.astype(f32) + met.astype(f32)
        met, came, parts, shaped = fence(
            along_x(ready), ring_step(total.astype(f16)), parts, shaped
        )
        total = parts[0] * inverse + came.astype(f32) + met.astype(f32)
        table_total = total[:VOC_DEV] * scale_all
        place_total = total[VOC_PAD:] * scale_all
        squares = squares + jnp.sum(table_total * table_total)
        squares = jnp.broadcast_to(squares + jnp.sum(place_total * place_total), (1, 128))

        def sided(one, two, bit):
            return jnp.where(bit == 0, jnp.stack([one, two]), jnp.stack([two, one]))

        squares = z_sum(squares, dp)
        steps = [total[VOC_PAD:].astype(f16)]
        for shift in range(1, RING):
            pairs = [(i, (i + 2 * shift) % dp) for i in range(dp)]
            steps.append(lax.ppermute(steps[0], "dp", pairs))
        squares, steps = fence(squares, steps)
        squares = x_sum(squares, dp)
        steps = jnp.stack(steps[::-1] * 2)
        steps = lax.dynamic_slice_in_dim(steps, (RING - 1 - z_here) % RING, RING, 0)
        squares, steps, near = fence(squares, steps, along_x(steps))
        squares = mp_sum(squares, mp)
        place_all = sided(steps, near, x_here).transpose(1, 0, 2, 3)
        place_all = place_all.reshape(place_rows, D)
        place_all = sided(place_all, swap(place_all, "mp", mp, 2), high_bit)
        place_all = sided(place_all, swap(place_all, "mp", mp, 1), low_bit)
        place_sum = place_all.transpose(1, 0, 2, 3).reshape(LEN, D).astype(f32) * scale_all
        squares = squares[0, 0]
    else:
        layer_total = lax.psum_scatter(
            layer_grad[0].astype(f32), "dp", scatter_dimension=0, tiled=True
        )
        layer_scale, gram_left, gram_right, shaped = shampoo_products(layer_total)
        sent, sums_zero, limit_here = own_embedding(*embedding_far(keep, send))
        far = swap(sent, "mp", mp, 2)
        embed_parts = all_embedding(sent, far, swap((sent, far), "mp", mp, 1))
        upper, lower = split(jnp.concatenate(embed_parts, axis=0), 2)
        vector_part = butterfly(vector_of(sums_zero, limit_here), jnp.add, dp, mp)
        table_grad, place_grad = table_gradient(
            code_row, place_codes, place_rows, upper, lower, grad_logits, picked_low
        )
        table_total = lax.psum_scatter(table_grad, "dp", scatter_dimension=0, tiled=True)[:VOC_DEV]
        place_total = lax.psum_scatter(place_grad, "dp", scatter_dimension=0, tiled=True)
        place_sum = lax.all_gather(
            lax.all_gather(place_total, "dp", axis=0, tiled=True), "mp", axis=0, tiled=True
        )
        squares = jnp.sum(layer_total * layer_total) + jnp.sum(table_total * table_total)
        squares = jnp.broadcast_to(squares + jnp.sum(place_total * place_total), (1, 128))
        squares = butterfly(squares, jnp.add, dp, mp)[0, 0]
    tail_sum, loss_sum = vector_part[:-1], vector_part[-1, 0]

    squares = squares + jnp.sum(tail_sum * tail_sum)
    grad_norm = jnp.sqrt(squares)
    count_all = rows * dp * POS
    limit = CLIP_FACTOR * math.sqrt(count_all)
    factor = jnp.minimum(1.0, limit / grad_norm)
    shrink = factor * layer_scale

    left_new = STAT_DECAY * stats_left + (1.0 - STAT_DECAY) * (shrink * shrink) * gram_left
    right_new = STAT_DECAY * stats_right + (1.0 - STAT_DECAY) * (shrink * shrink) * gram_right
    layer_new = layer_master - RATE_SHAMPOO * (shaped * shrink + DECAY_LAYER * layer_master)

    table_new, table_one, table_two = adam_step(
        table_master, table_first, table_second, table_total * factor, DECAY_TABLE
    )
    vector_sum = jnp.concatenate([place_sum, tail_sum], axis=0)
    vector_new, vector_one, vector_two = adam_step(
        vector_master, vector_first, vector_second, vector_sum * factor, 0.0
    )
    loss = loss_sum / f32(count_all)
    return (
        loss,
        grad_norm,
        layer_new,
        left_new,
        right_new,
        table_new,
        table_one,
        table_two,
        vector_new,
        vector_one,
        vector_two,
    )


def solution(mesh):
    blocks = P("mp", "dp", None, None)
    vocab = P(("dp", "mp"), None)
    rows = P("dp", None)
    return jax.shard_map(
        local,
        mesh=mesh,
        in_specs=(rows,) * 4 + (P(),) + (blocks,) * 5 + (vocab,) * 3 + (P(),) * 3,
        out_specs=(P(), P()) + (blocks,) * 3 + (vocab,) * 3 + (P(),) * 3,
        check_vma=False,
    )
```
